32 devices in a mesh: half: 2 (over x), gx: 4 (over z), gy: 4 (over y, core).
Axes of the slice: x: 2, y: 2, z: 4, core: 2. Of those that a mesh axis runs over, the one named last changes fastest.
Arguments:
- state: float32 [2, 20, 8, 64, 128], P('half', None, 'gx', 'gy'), may hold values from -4 to 4
- levels: int32 [4, 8, 64], P(None, 'gx', 'gy'), may hold values from 0 to 128
- old_flux: float32 [2, 8, 64, 128], P(None, 'gx', 'gy'), may hold values from -4 to 4
- eco_prey: int32 [19], replicated, may hold values from 0 to 18
- eco_rate: float32 [19], replicated, may hold values from 0.3 to 3
Outputs:
- state_next: float32 [2, 20, 8, 64, 128], P('half', None, 'gx', 'gy')
The draws below stay inside these ranges and needn't reach their ends.
All inputs are finite; a program needn't handle non-finite values.
Results may differ from the reference program's by a relative error of at most 0.00013.
Values sent between devices are 32-bit elements; how exact they have to be, the bound alone decides.
A program may use at most 64 MiB of HBM per device.

```python
import math
import jax
import jax.numpy as jnp
from jax import lax

K = 128
NT = 19
NSUB = 4
CHANNELS = 20
NXC = 8
NYC = 64


def with_ends(result, stream_key, low, high):
    longest = result.shape.index(max(result.shape))
    spots = []
    for shift in (0, 1):
        where = [jax.random.randint(jax.random.fold_in(stream_key, axis), (), 0, length) for axis, length in enumerate(result.shape)]
        where[longest] = (where[longest] + shift) % result.shape[longest]
        spots.append(tuple(where))
    return result.at[spots[0]].set(low).at[spots[1]].set(high)


def shard_levels(own_key, shape, cuts, smallest, top_value):
    level = 1.0
    for dim, shards_of in cuts:
        draws = jax.random.uniform(jax.random.fold_in(jax.random.fold_in(own_key, 6), dim), (shards_of,), jnp.float32, smallest / len(cuts), top_value / len(cuts))
        level = level * jnp.repeat(jnp.exp(draws), shape[dim] // shards_of).reshape((-1,) + (1,) * (len(shape) - 1 - dim))
    return level


def noise(rng, dims, width, reach, cuts=(), kind=jnp.bfloat16):
    values = width * jax.random.normal(rng, dims, jnp.float32)
    if cuts:
        values = values * shard_levels(rng, dims, cuts, -0.22, 0.18)
    return jnp.clip(values, -reach, reach).astype(kind)


def setup_inputs(seed: int = 0) -> dict:
    key_list = jax.random.split(jax.random.key(seed), 6)
    state = noise(key_list[0], (2, CHANNELS, NXC, NYC, K), 1.0, 4.0, ((0, 2), (2, 4), (3, 4)), jnp.float32)
    levels = with_ends(jax.random.randint(key_list[1], (4, NXC, NYC), 0, K + 1), jax.random.fold_in(key_list[1], 1), 0, K).astype(jnp.int32)
    old_flux = noise(key_list[2], (2, NXC, NYC, K), 1.0, 4.0, ((1, 4), (2, 4)), jnp.float32)
    eco_prey = with_ends(jax.random.randint(key_list[3], (NT,), 0, NT), jax.random.fold_in(key_list[3], 1), 0, NT - 1).astype(jnp.int32)
    eco_rate = jnp.clip(jnp.exp(jax.random.uniform(key_list[4], (NT,), jnp.float32, math.log(0.3), math.log(3.0))), 0.3, 3.0)
    return {"state": state, "levels": levels, "old_flux": old_flux, "eco_prey": eco_prey, "eco_rate": eco_rate}


DT = 0.1
NU = 1.0
CORIOLIS = 0.5
DRAG = 0.1
MORTALITY = 0.1
HEATING = 2.0
SURFACE = 8.0


def to_fine(coarse):
    fields = coarse.shape[0] // 4
    size_x, size_y, depth = coarse.shape[1], coarse.shape[2], coarse.shape[3]
    split = coarse.reshape(fields, 2, 2, size_x, size_y, depth).transpose(0, 3, 1, 4, 2, 5)
    return split.reshape(fields, 2 * size_x, 2 * size_y, depth)


def to_coarse(fine_cells):
    fields, fine_x, fine_y, depth = fine_cells.shape
    split = fine_cells.reshape(fields, fine_x // 2, 2, fine_y // 2, 2, depth).transpose(0, 2, 4, 1, 3, 5)
    return split.reshape(fields * 4, fine_x // 2, fine_y // 2, depth)


def fine_levels(levels):
    size_x, size_y = levels.shape[1], levels.shape[2]
    return levels.reshape(2, 2, size_x, size_y).transpose(2, 0, 3, 1).reshape(2 * size_x, 2 * size_y)


def wet_of(levels, depth):
    shape = levels.shape + (depth,)
    return (lax.broadcasted_iota(jnp.int32, shape, len(shape) - 1) < levels[..., None]).astype(jnp.float32)


def padded(fields):
    return jnp.pad(fields, ((0, 0), (1, 1), (1, 1), (0, 0)))


def ocean_substep(fields, wet_mask, heating):
    centre = fields[:, 1:-1, 1:-1]
    to_east = fields[:, 2:, 1:-1]
    to_west = fields[:, :-2, 1:-1]
    to_north = fields[:, 1:-1, 2:]
    to_south = fields[:, 1:-1, :-2]
    speed_east = centre[0]
    speed_north = centre[1]
    advect = speed_east * (to_east - to_west) * 0.5 + speed_north * (to_north - to_south) * 0.5
    spread = to_east + to_west + to_north + to_south - 4.0 * centre
    zeroes = jnp.zeros_like(speed_east)
    forcing = jnp.stack([CORIOLIS * speed_north - DRAG * speed_east, -CORIOLIS * speed_east - DRAG * speed_north, zeroes + heating, zeroes, zeroes + 1.0])
    return wet_mask * (centre + DT * (NU * spread - advect + forcing))


def tracer_substep(fields, wet_mask, volume_flux, eco_prey, eco_rate):
    species = eco_rate.shape[0]
    centre = fields[:, 1:-1, 1:-1]
    to_east = fields[:, 2:, 1:-1]
    to_west = fields[:, :-2, 1:-1]
    to_north = fields[:, 1:-1, 2:]
    to_south = fields[:, 1:-1, :-2]
    advect = volume_flux[0] * (to_east - to_west) * 0.5 + volume_flux[1] * (to_north - to_south) * 0.5
    spread = to_east + to_west + to_north + to_south - 4.0 * centre
    living = centre[:species]
    prey_values = living[eco_prey.astype(jnp.int32)]
    growth = eco_rate[:, None, None, None] * living * jnp.tanh(prey_values) - MORTALITY * living
    reaction = jnp.concatenate([growth, jnp.zeros_like(centre[species:])], axis=0)
    return wet_mask * (centre + DT * (NU * spread - advect + reaction))


def absorption(tracer, wet_mask):
    depth = tracer.shape[-1]
    above_table = (lax.broadcasted_iota(jnp.int32, (depth, depth), 0) < lax.broadcasted_iota(jnp.int32, (depth, depth), 1)).astype(jnp.float32)
    attenuation = wet_mask * (0.03 + 0.05 * jax.nn.softplus(tracer[0]))
    overhead = jnp.einsum("xyk,kl->xyl", attenuation, above_table, precision=lax.Precision.HIGHEST)
    return SURFACE * jnp.exp(-overhead) * (1.0 - jnp.exp(-attenuation))


def coarse_mean(fine_cells):
    fields, fine_x, fine_y, depth = fine_cells.shape
    return fine_cells.reshape(fields, fine_x // 2, 2, fine_y // 2, 2, depth).sum(axis=(2, 4)) * 0.25


def reference(state, levels, old_flux, eco_prey, eco_rate):
    depth = state.shape[-1]
    wet_fine = wet_of(fine_levels(levels), depth)
    wet_coarse = wet_of(jnp.max(levels, axis=0), depth)
    ocean_cells = to_fine(state[0]) * wet_fine
    tracer = state[1] * wet_coarse
    running = jnp.zeros((2,) + wet_coarse.shape, jnp.float32)
    for substep in range(NSUB):
        ocean_cells = ocean_substep(padded(ocean_cells), wet_fine, 0.0)
        running = running + coarse_mean(ocean_cells[0:2])
    for substep in range(NSUB):
        tracer = tracer_substep(padded(tracer), wet_coarse, old_flux, eco_prey, eco_rate)
    new_flux = running / NSUB
    absorbed = absorption(tracer, wet_coarse)
    heating = HEATING * jnp.repeat(jnp.repeat(absorbed, 2, axis=0), 2, axis=1)
    ocean_cells = ocean_substep(padded(ocean_cells), wet_fine, heating)
    tracer = tracer_substep(padded(tracer), wet_coarse, new_flux, eco_prey, eco_rate)
    return jnp.stack([to_coarse(ocean_cells), tracer])
```

```python
import jax
import jax.numpy as jnp
from jax import lax
from jax.experimental import pallas as pl
from jax.experimental.pallas import tpu as pltpu
from jax.sharding import PartitionSpec as P

NSUB = 4
STEPS = NSUB + 1
DT = 0.1
NU = 1.0
CORIOLIS = 0.5
DRAG = 0.1
MORTALITY = 0.1
HEATING = 2.0
SURFACE = 8.0
MESH = pl.DeviceIdType.MESH
WEST, EAST, SOUTH, NORTH = 0, 1, 2, 3


def kernel(
    state_hbm, levels_ref, flux_hbm, prey_ref, rate_ref, out_hbm,
    raw, cur, tanhs, hx, ys, yr, wet, flux, run, light, heat,
    load_sem, flux_sem, store_sem, send_sem, recv_sem, pair_send, pair_recv,
):
    groups = cur.shape[1]
    size_x, size_y, depth = cur.shape[3:]
    last_x, last_y = size_x - 1, size_y - 1
    species = prey_ref.shape[0]
    half = lax.axis_index("half")
    gx, gy = lax.axis_index("gx"), lax.axis_index("gy")
    nx, ny = lax.axis_size("gx"), lax.axis_size("gy")
    is_ocean = half == 0
    has = (gx > 0, gx < nx - 1, gy > 0, gy < ny - 1)
    peer = ({"gx": gx - 1}, {"gx": gx + 1}, {"gy": gy - 1}, {"gy": gy + 1})
    partner = {"half": 1 - half}

    def load(g):
        return pltpu.make_async_copy(state_hbm.at[0, pl.ds(4 * g, 4)], raw.at[g], load_sem.at[g])

    def store(g):
        return pltpu.make_async_copy(
            cur.at[STEPS, g], out_hbm.at[0, pl.ds(4 * g, 4)], store_sem.at[g]
        )

    flux_load = pltpu.make_async_copy(flux_hbm, flux.at[0], flux_sem)
    for g in range(groups):
        load(g).start()
    flux_load.start()

    barrier = pltpu.get_barrier_semaphore()
    for side in range(4):
        @pl.when(has[side])
        def _():
            pl.semaphore_signal(barrier, inc=1, device_id=peer[side], device_id_type=MESH)
    pl.semaphore_signal(barrier, inc=1, device_id=partner, device_id_type=MESH)

    for side in (WEST, EAST):
        @pl.when(jnp.logical_not(has[side]))
        def _():
            for s in range(STEPS):
                hx[s, side] = jnp.zeros(hx.shape[2:], jnp.float32)
    for side in (SOUTH, NORTH):
        @pl.when(jnp.logical_not(has[side]))
        def _():
            for s in range(STEPS):
                yr[s, side - 2] = jnp.zeros(yr.shape[2:], jnp.float32)

    rows = lax.broadcasted_iota(jnp.int32, (size_y, depth), 0)
    level_k = lax.broadcasted_iota(jnp.int32, (size_y, depth), 1).astype(jnp.float32)
    diagonal = lax.broadcasted_iota(jnp.int32, (size_y, size_y), 0) == lax.broadcasted_iota(
        jnp.int32, (size_y, size_y), 1
    )
    for i in range(size_x):
        active = []
        for c in range(4):
            line = levels_ref[c, pl.ds(i, 1), :].astype(jnp.float32)
            spread = jnp.where(diagonal, jnp.broadcast_to(line, (size_y, size_y)), 0.0)
            active.append(jnp.sum(spread, axis=1, keepdims=True))
        most = jnp.maximum(jnp.maximum(active[0], active[1]), jnp.maximum(active[2], active[3]))
        for c in range(4):
            mine = jnp.where(is_ocean, active[c], most)
            wet[c, i] = jnp.where(level_k < mine, 1.0, 0.0)

    run[...] = jnp.zeros(run.shape, jnp.float32)
    heat[...] = jnp.zeros(heat.shape, jnp.float32)

    def x_copy(s, g, side, ocean):
        row = 0 if side == WEST else last_x
        if ocean:
            channels = pl.ds(0, 2) if side == WEST else pl.ds(2, 2)
            src = cur.at[s, g, channels, row]
            dst = hx.at[s, 1 - side, g, pl.ds(0, 2)]
        else:
            src = cur.at[s, g, :, row]
            dst = hx.at[s, 1 - side, g]
        return pltpu.make_async_remote_copy(
            src, dst, send_sem.at[s, g, side], recv_sem.at[s, g, 1 - side],
            device_id=peer[side], device_id_type=MESH,
        )

    def y_copy(s, g, side):
        return pltpu.make_async_remote_copy(
            ys.at[s, side - 2, g], yr.at[s, 3 - side, g],
            send_sem.at[s, g, side], recv_sem.at[s, g, 5 - side],
            device_id=peer[side], device_id_type=MESH,
        )

    def copy_of(s, g, side, ocean):
        return x_copy(s, g, side, ocean) if side < 2 else y_copy(s, g, side)

    def start_copies(s, g, ocean):
        for side in range(4):
            @pl.when(has[side])
            def _():
                copy_of(s, g, side, ocean).start()

    def wait_arrivals(s, g, ocean):
        for side in range(4):
            @pl.when(has[side])
            def _():
                if side < 2:
                    lands = hx.at[s, side, g, pl.ds(0, 2)] if ocean else hx.at[s, side, g]
                else:
                    lands = yr.at[s, side - 2, g]
                pltpu.make_async_remote_copy(
                    lands, lands, send_sem.at[s, g, side], recv_sem.at[s, g, side],
                    device_id=peer[side], device_id_type=MESH,
                ).wait_recv()

    def wait_sends(ocean):
        def step(s, carry):
            def group(g, inner):
                for side in range(4):
                    @pl.when(has[side])
                    def _():
                        copy_of(s, g, side, ocean).wait_send()
                return inner
            return lax.fori_loop(0, groups, group, carry)
        lax.fori_loop(0, STEPS, step, 0)

    def put(s, g, c, i, value):
        cur[s, g, c, i] = value
        ys[s, 0, g, pl.ds(c * size_x + i, 1), :] = value[0:1]
        ys[s, 1, g, pl.ds(c * size_x + i, 1), :] = value[last_y:]

    def north_of(value, s, g, c, i):
        arrived = yr[s, 1, g, pl.ds(c * size_x + i, 1), :]
        return jnp.where(rows == last_y, arrived, pltpu.roll(value, size_y - 1, 0))

    def south_of(value, s, g, c, i):
        arrived = yr[s, 0, g, pl.ds(c * size_x + i, 1), :]
        return jnp.where(rows == 0, arrived, pltpu.roll(value, 1, 0))

    def ocean_part():
        def first(g, carry):
            load(g).wait()
            for c in range(4):
                for i in range(size_x):
                    put(0, g, c, i, raw[g, c, i] * wet[c, i])
            start_copies(0, g, True)
            return carry

        lax.fori_loop(0, groups, first, 0)
        flux_load.wait()

        def pair_copy():
            return pltpu.make_async_remote_copy(
                run, flux.at[1], pair_send, pair_recv, device_id=partner, device_id_type=MESH
            )

        def step(s, carry):
            def field(f, inner):
                wait_arrivals(s, f, True)

                @pl.when(jnp.logical_and(s == NSUB, f == 2))
                def _():
                    pltpu.make_async_remote_copy(
                        light, light, pair_send, pair_recv,
                        device_id=partner, device_id_type=MESH,
                    ).wait_recv()
                    heat[...] = light[...] * HEATING

                of_u = jnp.where(f == 0, -DRAG, jnp.where(f == 1, -CORIOLIS, 0.0))
                of_v = jnp.where(f == 0, CORIOLIS, jnp.where(f == 1, -DRAG, 0.0))
                of_heat = jnp.where(f == 2, 1.0, 0.0)
                ageing = jnp.where(f == 4, 1.0, 0.0)
                for i in range(size_x):
                    total = None
                    for c in range(4):
                        a, b = c // 2, c % 2
                        centre = cur[s, f, c, i]
                        if a == 0:
                            to_east = cur[s, f, 2 + b, i]
                            to_west = cur[s, f, 2 + b, i - 1] if i > 0 else hx[s, WEST, f, b]
                        else:
                            to_west = cur[s, f, b, i]
                            to_east = cur[s, f, b, i + 1] if i < last_x else hx[s, EAST, f, b]
                        other = cur[s, f, 2 * a + 1 - b, i]
                        if b == 0:
                            to_north = other
                            to_south = south_of(other, s, f, c + 1, i)
                        else:
                            to_south = other
                            to_north = north_of(other, s, f, c - 1, i)
                        u, v = cur[s, 0, c, i], cur[s, 1, c, i]
                        spread = to_east + to_west + to_north + to_south - 4.0 * centre
                        advect = u * (to_east - to_west) * 0.5 + v * (to_north - to_south) * 0.5
                        forcing = of_u * u + of_v * v + of_heat * heat[i] + ageing
                        new = wet[c, i] * (centre + DT * (NU * spread - advect + forcing))
                        put(s + 1, f, c, i, new)
                        total = new if total is None else total + new

                    @pl.when(jnp.logical_and(f < 2, s < NSUB))
                    def _():
                        run[f, i] = run[f, i] + total * (0.25 / NSUB)

                @pl.when(s < NSUB)
                def _():
                    start_copies(s + 1, f, True)

                @pl.when(jnp.logical_and(s == NSUB - 1, f == 1))
                def _():
                    pair_copy().start()

                @pl.when(s == NSUB)
                def _():
                    store(f).start()
                return inner
            return lax.fori_loop(0, groups, field, carry)

        lax.fori_loop(0, STEPS, step, 0)
        wait_sends(True)
        pair_copy().wait_send()

    def tracer_part():
        def first(g, carry):
            load(g).wait()
            for c in range(4):
                for i in range(size_x):
                    value = raw[g, c, i] * wet[c, i]
                    put(0, g, c, i, value)
                    tanhs[0, 4 * g + c, i] = jnp.tanh(value)
            start_copies(0, g, False)
            return carry

        lax.fori_loop(0, groups, first, 0)
        flux_load.wait()

        def pair_copy():
            return pltpu.make_async_remote_copy(
                heat, light, pair_send, pair_recv, device_id=partner, device_id_type=MESH
            )

        def step(s, carry):
            now, later = lax.rem(s, 2), lax.rem(s + 1, 2)
            which = s // NSUB

            @pl.when(s == NSUB)
            def _():
                pltpu.make_async_remote_copy(
                    flux.at[1], flux.at[1], pair_send, pair_recv,
                    device_id=partner, device_id_type=MESH,
                ).wait_recv()

            def group(g, inner):
                wait_arrivals(s, g, False)
                for c in range(4):
                    t = 4 * g + c
                    living = jnp.where(t < species, 1.0, 0.0)
                    slot = jnp.minimum(t, species - 1)
                    rate = rate_ref[slot] * living
                    mortality = MORTALITY * living
                    prey = prey_ref[slot]
                    for i in range(size_x):
                        centre = cur[s, g, c, i]
                        to_west = cur[s, g, c, i - 1] if i > 0 else hx[s, WEST, g, c]
                        to_east = cur[s, g, c, i + 1] if i < last_x else hx[s, EAST, g, c]
                        to_north = north_of(centre, s, g, c, i)
                        to_south = south_of(centre, s, g, c, i)
                        spread = to_east + to_west + to_north + to_south - 4.0 * centre
                        advect = (
                            flux[which, 0, i] * (to_east - to_west) * 0.5
                            + flux[which, 1, i] * (to_north - to_south) * 0.5
                        )
                        reaction = rate * centre * tanhs[now, prey, i] - mortality * centre
                        new = wet[c, i] * (centre + DT * (NU * spread - advect + reaction))
                        put(s + 1, g, c, i, new)
                        tanhs[later, t, i] = jnp.tanh(new)

                @pl.when(s < NSUB)
                def _():
                    start_copies(s + 1, g, False)

                @pl.when(jnp.logical_and(s == NSUB - 1, g == 0))
                def _():
                    above = (
                        lax.broadcasted_iota(jnp.int32, (depth, depth), 0)
                        < lax.broadcasted_iota(jnp.int32, (depth, depth), 1)
                    ).astype(jnp.float32)
                    for i in range(size_x):
                        green = cur[s + 1, 0, 0, i]
                        soft = jnp.maximum(green, 0.0) + jnp.log(1.0 + jnp.exp(-jnp.abs(green)))
                        attenuation = wet[0, i] * (0.03 + 0.05 * soft)
                        overhead = jnp.dot(
                            attenuation, above, precision=lax.Precision.HIGHEST,
                            preferred_element_type=jnp.float32,
                        )
                        heat[i] = SURFACE * jnp.exp(-overhead) * (1.0 - jnp.exp(-attenuation))
                    pair_copy().start()

                @pl.when(s == NSUB)
                def _():
                    store(g).start()
                return inner
            return lax.fori_loop(0, groups, group, carry)

        lax.fori_loop(0, STEPS, step, 0)
        wait_sends(False)
        pair_copy().wait_send()

    greeted = 1
    for side in range(4):
        greeted = greeted + has[side].astype(jnp.int32)
    pl.semaphore_wait(barrier, greeted)

    pl.when(is_ocean)(ocean_part)
    pl.when(jnp.logical_not(is_ocean))(tracer_part)
    for g in range(groups):
        store(g).wait()


def body(state, levels, old_flux, eco_prey, eco_rate):
    channels, size_x, size_y, depth = state.shape[1:]
    groups = channels // 4
    f32 = jnp.float32
    tile = (size_x, size_y, depth)
    return pl.pallas_call(
        kernel,
        out_shape=jax.ShapeDtypeStruct(state.shape, f32),
        in_specs=[
            pl.BlockSpec(memory_space=pl.ANY),
            pl.BlockSpec(memory_space=pltpu.VMEM),
            pl.BlockSpec(memory_space=pl.ANY),
            pl.BlockSpec(memory_space=pltpu.SMEM),
            pl.BlockSpec(memory_space=pltpu.SMEM),
        ],
        out_specs=pl.BlockSpec(memory_space=pl.ANY),
        scratch_shapes=[
            pltpu.VMEM((groups, 4) + tile, f32),
            pltpu.VMEM((STEPS + 1, groups, 4) + tile, f32),
            pltpu.VMEM((2, channels) + tile, f32),
            pltpu.VMEM((STEPS, 2, groups, 4, size_y, depth), f32),
            pltpu.VMEM((STEPS + 1, 2, groups, 4 * size_x, depth), f32),
            pltpu.VMEM((STEPS, 2, groups, 4 * size_x, depth), f32),
            pltpu.VMEM((4,) + tile, f32),
            pltpu.VMEM((2, 2) + tile, f32),
            pltpu.VMEM((2,) + tile, f32),
            pltpu.VMEM(tile, f32),
            pltpu.VMEM(tile, f32),
            pltpu.SemaphoreType.DMA((groups,)),
            pltpu.SemaphoreType.DMA,
            pltpu.SemaphoreType.DMA((groups,)),
            pltpu.SemaphoreType.DMA((STEPS, groups, 4)),
            pltpu.SemaphoreType.DMA((STEPS, groups, 4)),
            pltpu.SemaphoreType.DMA,
            pltpu.SemaphoreType.DMA,
        ],
        compiler_params=pltpu.CompilerParams(
            collective_id=0, has_side_effects=True, vmem_limit_bytes=24 * 1024 * 1024
        ),
    )(state, levels, old_flux, eco_prey, eco_rate)


def solution(mesh):
    placed = (
        P("half", None, "gx", "gy", None),
        P(None, "gx", "gy"),
        P(None, "gx", "gy", None),
        P(),
        P(),
    )
    return jax.shard_map(
        body,
        mesh=mesh,
        in_specs=placed,
        out_specs=P("half", None, "gx", "gy", None),
        check_vma=False,
    )
```

```python
import jax
import jax.numpy as jnp
from jax import lax
from jax.experimental import pallas as pl
from jax.experimental.pallas import tpu as pltpu
from jax.sharding import PartitionSpec as P

NSUB = 4
STEPS = NSUB + 1
DT = 0.1
NU = 1.0
CORIOLIS = 0.5
DRAG = 0.1
MORTALITY = 0.1
HEATING = 2.0
SURFACE = 8.0
MESH = pl.DeviceIdType.MESH
WEST, EAST, SOUTH, NORTH = 0, 1, 2, 3


def kernel(
    state_hbm, levels_hbm, flux_hbm, prey_hbm, rate_hbm, out_hbm,
    levels_ref, prey_ref, rate_ref, raw, cur, tanhs, hx, ys, yr, wet, flux, run, light, heat,
    load_sem, small_sem, store_sem, send_sem, recv_sem, pair_send, pair_recv,
):
    groups = cur.shape[1]
    size_x, size_y, depth = cur.shape[3:]
    last_x, last_y = size_x - 1, size_y - 1
    species = prey_ref.shape[0]
    half = lax.axis_index("half")
    gx, gy = lax.axis_index("gx"), lax.axis_index("gy")
    nx, ny = lax.axis_size("gx"), lax.axis_size("gy")
    is_ocean = half == 0
    has = (gx > 0, gx < nx - 1, gy > 0, gy < ny - 1)
    peer = ({"gx": gx - 1}, {"gx": gx + 1}, {"gy": gy - 1}, {"gy": gy + 1})
    partner = {"half": 1 - half}

    def load(g):
        return pltpu.make_async_copy(state_hbm.at[0, pl.ds(4 * g, 4)], raw.at[g], load_sem.at[g])

    def store(g):
        return pltpu.make_async_copy(
            cur.at[STEPS, g], out_hbm.at[0, pl.ds(4 * g, 4)], store_sem.at[g]
        )

    levels_load = pltpu.make_async_copy(levels_hbm, levels_ref, small_sem.at[0])
    flux_load = pltpu.make_async_copy(flux_hbm, flux.at[0], small_sem.at[1])
    prey_load = pltpu.make_async_copy(prey_hbm, prey_ref, small_sem.at[2])
    rate_load = pltpu.make_async_copy(rate_hbm, rate_ref, small_sem.at[3])
    levels_load.start()
    for g in range(groups):
        load(g).start()
    flux_load.start()
    prey_load.start()
    rate_load.start()

    barrier = pltpu.get_barrier_semaphore()
    for side in range(4):
        @pl.when(has[side])
        def _():
            pl.semaphore_signal(barrier, inc=1, device_id=peer[side], device_id_type=MESH)
    pl.semaphore_signal(barrier, inc=1, device_id=partner, device_id_type=MESH)

    for side in (WEST, EAST):
        @pl.when(jnp.logical_not(has[side]))
        def _():
            for s in range(STEPS):
                hx[s, side] = jnp.zeros(hx.shape[2:], jnp.float32)
    for side in (SOUTH, NORTH):
        @pl.when(jnp.logical_not(has[side]))
        def _():
            for s in range(STEPS):
                yr[s, side - 2] = jnp.zeros(yr.shape[2:], jnp.float32)

    rows = lax.broadcasted_iota(jnp.int32, (size_y, depth), 0)
    level_k = lax.broadcasted_iota(jnp.int32, (size_y, depth), 1).astype(jnp.float32)
    diagonal = lax.broadcasted_iota(jnp.int32, (size_y, size_y), 0) == lax.broadcasted_iota(
        jnp.int32, (size_y, size_y), 1
    )
    levels_load.wait()
    for i in range(size_x):
        active = []
        for c in range(4):
            line = levels_ref[c, pl.ds(i, 1), :].astype(jnp.float32)
            spread = jnp.where(diagonal, jnp.broadcast_to(line, (size_y, size_y)), 0.0)
            active.append(jnp.sum(spread, axis=1, keepdims=True))
        most = jnp.maximum(jnp.maximum(active[0], active[1]), jnp.maximum(active[2], active[3]))
        for c in range(4):
            mine = jnp.where(is_ocean, active[c], most)
            wet[c, i] = jnp.where(level_k < mine, 1.0, 0.0)

    run[...] = jnp.zeros(run.shape, jnp.float32)
    heat[...] = jnp.zeros(heat.shape, jnp.float32)

    def x_copy(s, g, side, ocean):
        row = 0 if side == WEST else last_x
        if ocean:
            channels = pl.ds(0, 2) if side == WEST else pl.ds(2, 2)
            src = cur.at[s, g, channels, row]
            dst = hx.at[s, 1 - side, g, pl.ds(0, 2)]
        else:
            src = cur.at[s, g, :, row]
            dst = hx.at[s, 1 - side, g]
        return pltpu.make_async_remote_copy(
            src, dst, send_sem.at[s, g, side], recv_sem.at[s, g, 1 - side],
            device_id=peer[side], device_id_type=MESH,
        )

    def y_copy(s, g, side):
        return pltpu.make_async_remote_copy(
            ys.at[s, side - 2, g], yr.at[s, 3 - side, g],
            send_sem.at[s, g, side], recv_sem.at[s, g, 5 - side],
            device_id=peer[side], device_id_type=MESH,
        )

    def copy_of(s, g, side, ocean):
        return x_copy(s, g, side, ocean) if side < 2 else y_copy(s, g, side)

    def start_copies(s, g, ocean):
        for side in range(4):
            @pl.when(has[side])
            def _():
                copy_of(s, g, side, ocean).start()

    def wait_arrivals(s, g, ocean):
        for side in range(4):
            @pl.when(has[side])
            def _():
                if side < 2:
                    lands = hx.at[s, side, g, pl.ds(0, 2)] if ocean else hx.at[s, side, g]
                else:
                    lands = yr.at[s, side - 2, g]
                pltpu.make_async_remote_copy(
                    lands, lands, send_sem.at[s, g, side], recv_sem.at[s, g, side],
                    device_id=peer[side], device_id_type=MESH,
                ).wait_recv()

    def wait_sends(ocean):
        def step(s, carry):
            def group(g, inner):
                for side in range(4):
                    @pl.when(has[side])
                    def _():
                        copy_of(s, g, side, ocean).wait_send()
                return inner
            return lax.fori_loop(0, groups, group, carry)
        lax.fori_loop(0, STEPS, step, 0)

    def put(s, g, c, i, value):
        cur[s, g, c, i] = value
        ys[s, 0, g, pl.ds(c * size_x + i, 1), :] = value[0:1]
        ys[s, 1, g, pl.ds(c * size_x + i, 1), :] = value[last_y:]

    def north_of(value, s, g, c, i):
        arrived = yr[s, 1, g, pl.ds(c * size_x + i, 1), :]
        return jnp.where(rows == last_y, arrived, pltpu.roll(value, size_y - 1, 0))

    def south_of(value, s, g, c, i):
        arrived = yr[s, 0, g, pl.ds(c * size_x + i, 1), :]
        return jnp.where(rows == 0, arrived, pltpu.roll(value, 1, 0))

    def ocean_part():
        def first(g, carry):
            load(g).wait()
            for c in range(4):
                for i in range(size_x):
                    put(0, g, c, i, raw[g, c, i] * wet[c, i])
            start_copies(0, g, True)
            return carry

        lax.fori_loop(0, groups, first, 0)
        flux_load.wait()
        prey_load.wait()
        rate_load.wait()

        def pair_copy():
            return pltpu.make_async_remote_copy(
                run, flux.at[1], pair_send, pair_recv, device_id=partner, device_id_type=MESH
            )

        def step(s, carry):
            def field(f, inner):
                wait_arrivals(s, f, True)

                @pl.when(jnp.logical_and(s == NSUB, f == 2))
                def _():
                    pltpu.make_async_remote_copy(
                        light, light, pair_send, pair_recv,
                        device_id=partner, device_id_type=MESH,
                    ).wait_recv()
                    heat[...] = light[...] * HEATING

                of_u = jnp.where(f == 0, -DRAG, jnp.where(f == 1, -CORIOLIS, 0.0))
                of_v = jnp.where(f == 0, CORIOLIS, jnp.where(f == 1, -DRAG, 0.0))
                of_heat = jnp.where(f == 2, 1.0, 0.0)
                ageing = jnp.where(f == 4, 1.0, 0.0)
                for i in range(size_x):
                    total = None
                    for c in range(4):
                        a, b = c // 2, c % 2
                        centre = cur[s, f, c, i]
                        if a == 0:
                            to_east = cur[s, f, 2 + b, i]
                            to_west = cur[s, f, 2 + b, i - 1] if i > 0 else hx[s, WEST, f, b]
                        else:
                            to_west = cur[s, f, b, i]
                            to_east = cur[s, f, b, i + 1] if i < last_x else hx[s, EAST, f, b]
                        other = cur[s, f, 2 * a + 1 - b, i]
                        if b == 0:
                            to_north = other
                            to_south = south_of(other, s, f, c + 1, i)
                        else:
                            to_south = other
                            to_north = north_of(other, s, f, c - 1, i)
                        u, v = cur[s, 0, c, i], cur[s, 1, c, i]
                        spread = to_east + to_west + to_north + to_south - 4.0 * centre
                        advect = u * (to_east - to_west) * 0.5 + v * (to_north - to_south) * 0.5
                        forcing = of_u * u + of_v * v + of_heat * heat[i] + ageing
                        new = wet[c, i] * (centre + DT * (NU * spread - advect + forcing))
                        put(s + 1, f, c, i, new)
                        total = new if total is None else total + new

                    @pl.when(jnp.logical_and(f < 2, s < NSUB))
                    def _():
                        run[f, i] = run[f, i] + total * (0.25 / NSUB)

                @pl.when(s < NSUB)
                def _():
                    start_copies(s + 1, f, True)

                @pl.when(jnp.logical_and(s == NSUB - 1, f == 1))
                def _():
                    pair_copy().start()

                @pl.when(s == NSUB)
                def _():
                    store(f).start()
                return inner
            return lax.fori_loop(0, groups, field, carry)

        lax.fori_loop(0, STEPS, step, 0)
        wait_sends(True)
        pair_copy().wait_send()

    def tracer_part():
        def first(g, carry):
            load(g).wait()
            for c in range(4):
                for i in range(size_x):
                    value = raw[g, c, i] * wet[c, i]
                    put(0, g, c, i, value)
                    tanhs[0, 4 * g + c, i] = jnp.tanh(value)
            start_copies(0, g, False)
            return carry

        lax.fori_loop(0, groups, first, 0)
        flux_load.wait()
        prey_load.wait()
        rate_load.wait()

        def pair_copy():
            return pltpu.make_async_remote_copy(
                heat, light, pair_send, pair_recv, device_id=partner, device_id_type=MESH
            )

        def step(s, carry):
            now, later = lax.rem(s, 2), lax.rem(s + 1, 2)
            which = s // NSUB

            @pl.when(s == NSUB)
            def _():
                pltpu.make_async_remote_copy(
                    flux.at[1], flux.at[1], pair_send, pair_recv,
                    device_id=partner, device_id_type=MESH,
                ).wait_recv()

            def group(g, inner):
                wait_arrivals(s, g, False)
                for c in range(4):
                    t = 4 * g + c
                    living = jnp.where(t < species, 1.0, 0.0)
                    slot = jnp.minimum(t, species - 1)
                    rate = rate_ref[slot] * living
                    mortality = MORTALITY * living
                    prey = prey_ref[slot]
                    for i in range(size_x):
                        centre = cur[s, g, c, i]
                        to_west = cur[s, g, c, i - 1] if i > 0 else hx[s, WEST, g, c]
                        to_east = cur[s, g, c, i + 1] if i < last_x else hx[s, EAST, g, c]
                        to_north = north_of(centre, s, g, c, i)
                        to_south = south_of(centre, s, g, c, i)
                        spread = to_east + to_west + to_north + to_south - 4.0 * centre
                        advect = (
                            flux[which, 0, i] * (to_east - to_west) * 0.5
                            + flux[which, 1, i] * (to_north - to_south) * 0.5
                        )
                        reaction = rate * centre * tanhs[now, prey, i] - mortality * centre
                        new = wet[c, i] * (centre + DT * (NU * spread - advect + reaction))
                        put(s + 1, g, c, i, new)
                        tanhs[later, t, i] = jnp.tanh(new)

                @pl.when(s < NSUB)
                def _():
                    start_copies(s + 1, g, False)

                @pl.when(jnp.logical_and(s == NSUB - 1, g == 0))
                def _():
                    above = (
                        lax.broadcasted_iota(jnp.int32, (depth, depth), 0)
                        < lax.broadcasted_iota(jnp.int32, (depth, depth), 1)
                    ).astype(jnp.float32)
                    for i in range(size_x):
                        green = cur[s + 1, 0, 0, i]
                        soft = jnp.maximum(green, 0.0) + jnp.log(1.0 + jnp.exp(-jnp.abs(green)))
                        attenuation = wet[0, i] * (0.03 + 0.05 * soft)
                        overhead = jnp.dot(
                            attenuation, above, precision=lax.Precision.HIGHEST,
                            preferred_element_type=jnp.float32,
                        )
                        heat[i] = SURFACE * jnp.exp(-overhead) * (1.0 - jnp.exp(-attenuation))
                    pair_copy().start()

                @pl.when(s == NSUB)
                def _():
                    store(g).start()
                return inner
            return lax.fori_loop(0, groups, group, carry)

        lax.fori_loop(0, STEPS, step, 0)
        wait_sends(False)
        pair_copy().wait_send()

    greeted = 1
    for side in range(4):
        greeted = greeted + has[side].astype(jnp.int32)
    pl.semaphore_wait(barrier, greeted)

    pl.when(is_ocean)(ocean_part)
    pl.when(jnp.logical_not(is_ocean))(tracer_part)
    for g in range(groups):
        store(g).wait()


def body(state, levels, old_flux, eco_prey, eco_rate):
    channels, size_x, size_y, depth = state.shape[1:]
    groups = channels // 4
    f32 = jnp.float32
    tile = (size_x, size_y, depth)
    return pl.pallas_call(
        kernel,
        out_shape=jax.ShapeDtypeStruct(state.shape, f32),
        in_specs=[pl.BlockSpec(memory_space=pl.ANY)] * 5,
        out_specs=pl.BlockSpec(memory_space=pl.ANY),
        scratch_shapes=[
            pltpu.VMEM(levels.shape, levels.dtype),
            pltpu.SMEM(eco_prey.shape, eco_prey.dtype),
            pltpu.SMEM(eco_rate.shape, eco_rate.dtype),
            pltpu.VMEM((groups, 4) + tile, f32),
            pltpu.VMEM((STEPS + 1, groups, 4) + tile, f32),
            pltpu.VMEM((2, channels) + tile, f32),
            pltpu.VMEM((STEPS, 2, groups, 4, size_y, depth), f32),
            pltpu.VMEM((STEPS + 1, 2, groups, 4 * size_x, depth), f32),
            pltpu.VMEM((STEPS, 2, groups, 4 * size_x, depth), f32),
            pltpu.VMEM((4,) + tile, f32),
            pltpu.VMEM((2, 2) + tile, f32),
            pltpu.VMEM((2,) + tile, f32),
            pltpu.VMEM(tile, f32),
            pltpu.VMEM(tile, f32),
            pltpu.SemaphoreType.DMA((groups,)),
            pltpu.SemaphoreType.DMA((4,)),
            pltpu.SemaphoreType.DMA((groups,)),
            pltpu.SemaphoreType.DMA((STEPS, groups, 4)),
            pltpu.SemaphoreType.DMA((STEPS, groups, 4)),
            pltpu.SemaphoreType.DMA,
            pltpu.SemaphoreType.DMA,
        ],
        compiler_params=pltpu.CompilerParams(
            collective_id=0, has_side_effects=True, vmem_limit_bytes=60 * 1024 * 1024
        ),
    )(state, levels, old_flux, eco_prey, eco_rate)


def solution(mesh):
    placed = (
        P("half", None, "gx", "gy", None),
        P(None, "gx", "gy"),
        P(None, "gx", "gy", None),
        P(),
        P(),
    )
    return jax.shard_map(
        body,
        mesh=mesh,
        in_specs=placed,
        out_specs=P("half", None, "gx", "gy", None),
        check_vma=False,
    )
```

```python
import jax
import jax.numpy as jnp
from jax import lax
from jax.experimental import pallas as pl
from jax.experimental.pallas import tpu as pltpu
from jax.sharding import PartitionSpec as P

NSUB = 4
STEPS = NSUB + 1
DT = 0.1
NU = 1.0
CORIOLIS = 0.5
DRAG = 0.1
MORTALITY = 0.1
HEATING = 2.0
SURFACE = 8.0
MESH = pl.DeviceIdType.MESH
WEST, EAST, SOUTH, NORTH = 0, 1, 2, 3


def kernel(
    state_hbm, levels_hbm, flux_hbm, prey_hbm, rate_hbm, out_ref,
    levels_ref, prey_ref, rate_ref, raw, cur, tanhs, hx, ys, yr, wet, flux, run, light, heat,
    load_sem, small_sem, send_sem, recv_sem, pair_send, pair_recv, ready_sem,
):
    groups = cur.shape[1]
    size_x, size_y, depth = cur.shape[3:]
    last_x, last_y = size_x - 1, size_y - 1
    species = prey_ref.shape[0]
    half = lax.axis_index("half")
    gx, gy = lax.axis_index("gx"), lax.axis_index("gy")
    nx, ny = lax.axis_size("gx"), lax.axis_size("gy")
    is_ocean = half == 0
    has = (gx > 0, gx < nx - 1, gy > 0, gy < ny - 1)
    peer = ({"gx": gx - 1}, {"gx": gx + 1}, {"gy": gy - 1}, {"gy": gy + 1})
    partner = {"half": 1 - half}

    def load(g):
        return pltpu.make_async_copy(state_hbm.at[0, pl.ds(4 * g, 4)], raw.at[g], load_sem.at[g])

    levels_load = pltpu.make_async_copy(levels_hbm, levels_ref, small_sem.at[0])
    flux_load = pltpu.make_async_copy(flux_hbm, flux.at[0], small_sem.at[1])
    prey_load = pltpu.make_async_copy(prey_hbm, prey_ref, small_sem.at[2])
    rate_load = pltpu.make_async_copy(rate_hbm, rate_ref, small_sem.at[3])
    levels_load.start()
    for g in range(groups):
        load(g).start()
    flux_load.start()
    prey_load.start()
    rate_load.start()

    barrier = pltpu.get_barrier_semaphore()
    for side in range(4):
        @pl.when(has[side])
        def _():
            pl.semaphore_signal(barrier, inc=1, device_id=peer[side], device_id_type=MESH)

    @pl.when(jnp.logical_not(is_ocean))
    def _():
        pl.semaphore_signal(barrier, inc=1, device_id=partner, device_id_type=MESH)

    for side in (WEST, EAST):
        @pl.when(jnp.logical_not(has[side]))
        def _():
            for s in range(STEPS):
                hx[s, side] = jnp.zeros(hx.shape[2:], jnp.float32)
    for side in (SOUTH, NORTH):
        @pl.when(jnp.logical_not(has[side]))
        def _():
            for s in range(STEPS):
                yr[s, side - 2] = jnp.zeros(yr.shape[2:], jnp.float32)

    rows = lax.broadcasted_iota(jnp.int32, (size_y, depth), 0)
    level_k = lax.broadcasted_iota(jnp.int32, (size_y, depth), 1).astype(jnp.float32)
    diagonal = lax.broadcasted_iota(jnp.int32, (size_y, size_y), 0) == lax.broadcasted_iota(
        jnp.int32, (size_y, size_y), 1
    )
    levels_load.wait()
    for i in range(size_x):
        active = []
        for c in range(4):
            line = levels_ref[c, pl.ds(i, 1), :].astype(jnp.float32)
            spread = jnp.where(diagonal, jnp.broadcast_to(line, (size_y, size_y)), 0.0)
            active.append(jnp.sum(spread, axis=1, keepdims=True))
        most = jnp.maximum(jnp.maximum(active[0], active[1]), jnp.maximum(active[2], active[3]))
        for c in range(4):
            mine = jnp.where(is_ocean, active[c], most)
            wet[c, i] = jnp.where(level_k < mine, 1.0, 0.0)

    run[...] = jnp.zeros(run.shape, jnp.float32)
    heat[...] = jnp.zeros(heat.shape, jnp.float32)

    def x_copy(s, g, side, ocean):
        row = 0 if side == WEST else last_x
        if ocean:
            channels = pl.ds(0, 2) if side == WEST else pl.ds(2, 2)
            src = cur.at[s, g, channels, row]
            dst = hx.at[s, 1 - side, g, pl.ds(0, 2)]
        else:
            src = cur.at[s, g, :, row]
            dst = hx.at[s, 1 - side, g]
        return pltpu.make_async_remote_copy(
            src, dst, send_sem.at[s, g, side], recv_sem.at[s, g, 1 - side],
            device_id=peer[side], device_id_type=MESH,
        )

    def y_copy(s, g, side):
        return pltpu.make_async_remote_copy(
            ys.at[s, side - 2, g], yr.at[s, 3 - side, g],
            send_sem.at[s, g, side], recv_sem.at[s, g, 5 - side],
            device_id=peer[side], device_id_type=MESH,
        )

    def copy_of(s, g, side, ocean):
        return x_copy(s, g, side, ocean) if side < 2 else y_copy(s, g, side)

    def start_copies(s, g, ocean):
        for side in range(4):
            @pl.when(has[side])
            def _():
                copy_of(s, g, side, ocean).start()

    def wait_arrivals(s, g, ocean):
        for side in range(4):
            @pl.when(has[side])
            def _():
                if side < 2:
                    lands = hx.at[s, side, g, pl.ds(0, 2)] if ocean else hx.at[s, side, g]
                else:
                    lands = yr.at[s, side - 2, g]
                pltpu.make_async_remote_copy(
                    lands, lands, send_sem.at[s, g, side], recv_sem.at[s, g, side],
                    device_id=peer[side], device_id_type=MESH,
                ).wait_recv()

    def wait_sends(ocean):
        def step(s, carry):
            def group(g, inner):
                for side in range(4):
                    @pl.when(has[side])
                    def _():
                        copy_of(s, g, side, ocean).wait_send()
                return inner
            return lax.fori_loop(0, groups, group, carry)
        lax.fori_loop(0, STEPS, step, 0)

    def put(s, g, c, i, value):
        cur[s, g, c, i] = value
        ys[s, 0, g, pl.ds(c * size_x + i, 1), :] = value[0:1]
        ys[s, 1, g, pl.ds(c * size_x + i, 1), :] = value[last_y:]

    def north_of(value, s, g, c, i):
        arrived = yr[s, 1, g, pl.ds(c * size_x + i, 1), :]
        return jnp.where(rows == last_y, arrived, pltpu.roll(value, size_y - 1, 0))

    def south_of(value, s, g, c, i):
        arrived = yr[s, 0, g, pl.ds(c * size_x + i, 1), :]
        return jnp.where(rows == 0, arrived, pltpu.roll(value, 1, 0))

    def ocean_part():
        def first(g, carry):
            load(g).wait()
            for c in range(4):
                for i in range(size_x):
                    put(0, g, c, i, raw[g, c, i] * wet[c, i])
            start_copies(0, g, True)
            return carry

        lax.fori_loop(0, groups, first, 0)
        flux_load.wait()
        prey_load.wait()
        rate_load.wait()

        def pair_copy():
            return pltpu.make_async_remote_copy(
                run, flux.at[1], pair_send, pair_recv, device_id=partner, device_id_type=MESH
            )

        def step(s, carry):
            def field(f, inner):
                wait_arrivals(s, f, True)

                @pl.when(jnp.logical_and(s == NSUB, f == 2))
                def _():
                    pltpu.make_async_remote_copy(
                        light, light, pair_send, pair_recv,
                        device_id=partner, device_id_type=MESH,
                    ).wait_recv()
                    heat[...] = light[...] * HEATING

                of_u = jnp.where(f == 0, -DRAG, jnp.where(f == 1, -CORIOLIS, 0.0))
                of_v = jnp.where(f == 0, CORIOLIS, jnp.where(f == 1, -DRAG, 0.0))
                of_heat = jnp.where(f == 2, 1.0, 0.0)
                ageing = jnp.where(f == 4, 1.0, 0.0)
                for i in range(size_x):
                    total = None
                    for c in range(4):
                        a, b = c // 2, c % 2
                        centre = cur[s, f, c, i]
                        if a == 0:
                            to_east = cur[s, f, 2 + b, i]
                            to_west = cur[s, f, 2 + b, i - 1] if i > 0 else hx[s, WEST, f, b]
                        else:
                            to_west = cur[s, f, b, i]
                            to_east = cur[s, f, b, i + 1] if i < last_x else hx[s, EAST, f, b]
                        other = cur[s, f, 2 * a + 1 - b, i]
                        if b == 0:
                            to_north = other
                            to_south = south_of(other, s, f, c + 1, i)
                        else:
                            to_south = other
                            to_north = north_of(other, s, f, c - 1, i)
                        u, v = cur[s, 0, c, i], cur[s, 1, c, i]
                        spread = to_east + to_west + to_north + to_south - 4.0 * centre
                        advect = u * (to_east - to_west) * 0.5 + v * (to_north - to_south) * 0.5
                        forcing = of_u * u + of_v * v + of_heat * heat[i] + ageing
                        new = wet[c, i] * (centre + DT * (NU * spread - advect + forcing))
                        put(s + 1, f, c, i, new)
                        out_ref[0, 4 * f + c, i] = new
                        total = new if total is None else total + new

                    @pl.when(jnp.logical_and(f < 2, s < NSUB))
                    def _():
                        run[f, i] = run[f, i] + total * (0.25 / NSUB)

                @pl.when(s < NSUB)
                def _():
                    start_copies(s + 1, f, True)

                @pl.when(jnp.logical_and(s == NSUB - 1, f == 1))
                def _():
                    pair_copy().start()
                return inner
            return lax.fori_loop(0, groups, field, carry)

        lax.fori_loop(0, STEPS, step, 0)
        wait_sends(True)
        pair_copy().wait_send()

    def tracer_part():
        def first(g, carry):
            load(g).wait()
            for c in range(4):
                for i in range(size_x):
                    value = raw[g, c, i] * wet[c, i]
                    put(0, g, c, i, value)
                    tanhs[0, 4 * g + c, i] = jnp.tanh(value)
            start_copies(0, g, False)
            return carry

        lax.fori_loop(0, groups, first, 0)
        flux_load.wait()
        prey_load.wait()
        rate_load.wait()

        def pair_copy():
            return pltpu.make_async_remote_copy(
                heat, light, pair_send, pair_recv, device_id=partner, device_id_type=MESH
            )

        def step(s, carry):
            now, later = lax.rem(s, 2), lax.rem(s + 1, 2)
            which = s // NSUB

            @pl.when(s == NSUB)
            def _():
                pltpu.make_async_remote_copy(
                    flux.at[1], flux.at[1], pair_send, pair_recv,
                    device_id=partner, device_id_type=MESH,
                ).wait_recv()

            def group(g, inner):
                wait_arrivals(s, g, False)
                for c in range(4):
                    t = 4 * g + c
                    living = jnp.where(t < species, 1.0, 0.0)
                    slot = jnp.minimum(t, species - 1)
                    rate = rate_ref[slot] * living
                    mortality = MORTALITY * living
                    prey = prey_ref[slot]
                    for i in range(size_x):
                        centre = cur[s, g, c, i]
                        to_west = cur[s, g, c, i - 1] if i > 0 else hx[s, WEST, g, c]
                        to_east = cur[s, g, c, i + 1] if i < last_x else hx[s, EAST, g, c]
                        to_north = north_of(centre, s, g, c, i)
                        to_south = south_of(centre, s, g, c, i)
                        spread = to_east + to_west + to_north + to_south - 4.0 * centre
                        advect = (
                            flux[which, 0, i] * (to_east - to_west) * 0.5
                            + flux[which, 1, i] * (to_north - to_south) * 0.5
                        )
                        reaction = rate * centre * tanhs[now, prey, i] - mortality * centre
                        new = wet[c, i] * (centre + DT * (NU * spread - advect + reaction))
                        put(s + 1, g, c, i, new)
                        out_ref[0, t, i] = new
                        tanhs[later, t, i] = jnp.tanh(new)

                @pl.when(s < NSUB)
                def _():
                    start_copies(s + 1, g, False)

                @pl.when(jnp.logical_and(s == NSUB - 1, g == 0))
                def _():
                    above = (
                        lax.broadcasted_iota(jnp.int32, (depth, depth), 0)
                        < lax.broadcasted_iota(jnp.int32, (depth, depth), 1)
                    ).astype(jnp.float32)
                    for i in range(size_x):
                        green = cur[s + 1, 0, 0, i]
                        soft = jnp.maximum(green, 0.0) + jnp.log(1.0 + jnp.exp(-jnp.abs(green)))
                        attenuation = wet[0, i] * (0.03 + 0.05 * soft)
                        overhead = jnp.dot(
                            attenuation, above, precision=lax.Precision.HIGHEST,
                            preferred_element_type=jnp.float32,
                        )
                        heat[i] = SURFACE * jnp.exp(-overhead) * (1.0 - jnp.exp(-attenuation))
                    pl.semaphore_wait(ready_sem, 1)
                    pair_copy().start()
                return inner
            return lax.fori_loop(0, groups, group, carry)

        lax.fori_loop(0, STEPS, step, 0)
        wait_sends(False)
        pair_copy().wait_send()

    greeted = is_ocean.astype(jnp.int32)
    for side in range(4):
        greeted = greeted + has[side].astype(jnp.int32)
    pl.semaphore_wait(barrier, greeted)

    @pl.when(is_ocean)
    def _():
        pl.semaphore_signal(ready_sem, inc=1, device_id=partner, device_id_type=MESH)

    pl.when(is_ocean)(ocean_part)
    pl.when(jnp.logical_not(is_ocean))(tracer_part)


def body(state, levels, old_flux, eco_prey, eco_rate):
    channels, size_x, size_y, depth = state.shape[1:]
    groups = channels // 4
    f32 = jnp.float32
    tile = (size_x, size_y, depth)
    return pl.pallas_call(
        kernel,
        out_shape=pltpu.VMEM(state.shape, f32),
        in_specs=[pl.BlockSpec(memory_space=pltpu.HBM)] * 5,
        out_specs=pl.BlockSpec(memory_space=pltpu.VMEM),
        scratch_shapes=[
            pltpu.VMEM(levels.shape, levels.dtype),
            pltpu.SMEM(eco_prey.shape, eco_prey.dtype),
            pltpu.SMEM(eco_rate.shape, eco_rate.dtype),
            pltpu.VMEM((groups, 4) + tile, f32),
            pltpu.VMEM((STEPS + 1, groups, 4) + tile, f32),
            pltpu.VMEM((2, channels) + tile, f32),
            pltpu.VMEM((STEPS, 2, groups, 4, size_y, depth), f32),
            pltpu.VMEM((STEPS + 1, 2, groups, 4 * size_x, depth), f32),
            pltpu.VMEM((STEPS, 2, groups, 4 * size_x, depth), f32),
            pltpu.VMEM((4,) + tile, f32),
            pltpu.VMEM((2, 2) + tile, f32),
            pltpu.VMEM((2,) + tile, f32),
            pltpu.VMEM(tile, f32),
            pltpu.VMEM(tile, f32),
            pltpu.SemaphoreType.DMA((groups,)),
            pltpu.SemaphoreType.DMA((4,)),
            pltpu.SemaphoreType.DMA((STEPS, groups, 4)),
            pltpu.SemaphoreType.DMA((STEPS, groups, 4)),
            pltpu.SemaphoreType.DMA,
            pltpu.SemaphoreType.DMA,
            pltpu.SemaphoreType.REGULAR,
        ],
        compiler_params=pltpu.CompilerParams(
            collective_id=0, has_side_effects=True, vmem_limit_bytes=60 * 1024 * 1024
        ),
    )(state, levels, old_flux, eco_prey, eco_rate)


def solution(mesh):
    placed = (
        P("half", None, "gx", "gy", None),
        P(None, "gx", "gy"),
        P(None, "gx", "gy", None),
        P(),
        P(),
    )
    return jax.shard_map(
        body,
        mesh=mesh,
        in_specs=placed,
        out_specs=P("half", None, "gx", "gy", None),
        check_vma=False,
    )
```

```python
import jax
import jax.numpy as jnp
from jax import lax
from jax.experimental import pallas as pl
from jax.experimental.pallas import tpu as pltpu
from jax.sharding import PartitionSpec as P

NSUB = 4
STEPS = NSUB + 1
DT = 0.1
NU = 1.0
CORIOLIS = 0.5
DRAG = 0.1
MORTALITY = 0.1
HEATING = 2.0
SURFACE = 8.0
MESH = pl.DeviceIdType.MESH
WEST, EAST, SOUTH, NORTH = 0, 1, 2, 3


def kernel(
    state_hbm, levels_hbm, flux_hbm, prey_hbm, rate_hbm, out_ref,
    levels_ref, prey_ref, rate_ref, raw, cur, tanhs, hx, ys, yr, wet, flux, run, light, heat,
    load_sem, small_sem, send_sem, recv_sem, pair_send, pair_recv, ready_sem,
):
    groups = cur.shape[1]
    size_x, size_y, depth = cur.shape[3:]
    last_x, last_y = size_x - 1, size_y - 1
    species = prey_ref.shape[0]
    half = lax.axis_index("half")
    gx, gy = lax.axis_index("gx"), lax.axis_index("gy")
    nx, ny = lax.axis_size("gx"), lax.axis_size("gy")
    is_ocean = half == 0
    has = (gx > 0, gx < nx - 1, gy > 0, gy < ny - 1)
    peer = ({"gx": gx - 1}, {"gx": gx + 1}, {"gy": gy - 1}, {"gy": gy + 1})
    partner = {"half": 1 - half}

    def load(g):
        return pltpu.make_async_copy(state_hbm.at[0, pl.ds(4 * g, 4)], raw.at[g], load_sem.at[g])

    levels_load = pltpu.make_async_copy(levels_hbm, levels_ref, small_sem.at[0])
    flux_load = pltpu.make_async_copy(flux_hbm, flux.at[0], small_sem.at[1])
    prey_load = pltpu.make_async_copy(prey_hbm, prey_ref, small_sem.at[2])
    rate_load = pltpu.make_async_copy(rate_hbm, rate_ref, small_sem.at[3])
    levels_load.start()
    for g in range(groups):
        load(g).start()
    flux_load.start()
    prey_load.start()
    rate_load.start()

    barrier = pltpu.get_barrier_semaphore()
    for side in range(4):
        @pl.when(has[side])
        def _():
            pl.semaphore_signal(barrier, inc=1, device_id=peer[side], device_id_type=MESH)

    @pl.when(jnp.logical_not(is_ocean))
    def _():
        pl.semaphore_signal(barrier, inc=1, device_id=partner, device_id_type=MESH)

    for side in (WEST, EAST):
        @pl.when(jnp.logical_not(has[side]))
        def _():
            for s in range(STEPS):
                hx[s, side] = jnp.zeros(hx.shape[2:], jnp.float32)
    for side in (SOUTH, NORTH):
        @pl.when(jnp.logical_not(has[side]))
        def _():
            for s in range(STEPS):
                yr[s, side - 2] = jnp.zeros(yr.shape[2:], jnp.float32)

    rows = lax.broadcasted_iota(jnp.int32, (size_y, depth), 0)
    level_k = lax.broadcasted_iota(jnp.int32, (size_y, depth), 1).astype(jnp.float32)
    diagonal = lax.broadcasted_iota(jnp.int32, (size_y, size_y), 0) == lax.broadcasted_iota(
        jnp.int32, (size_y, size_y), 1
    )
    levels_load.wait()
    for i in range(size_x):
        active = []
        for c in range(4):
            line = levels_ref[c, pl.ds(i, 1), :].astype(jnp.float32)
            spread = jnp.where(diagonal, jnp.broadcast_to(line, (size_y, size_y)), 0.0)
            active.append(jnp.sum(spread, axis=1, keepdims=True))
        most = jnp.maximum(jnp.maximum(active[0], active[1]), jnp.maximum(active[2], active[3]))
        for c in range(4):
            mine = jnp.where(is_ocean, active[c], most)
            wet[c, i] = jnp.where(level_k < mine, 1.0, 0.0)

    run[...] = jnp.zeros(run.shape, jnp.float32)
    heat[...] = jnp.zeros(heat.shape, jnp.float32)

    def x_copy(s, g, side, ocean):
        row = 0 if side == WEST else last_x
        if ocean:
            channels = pl.ds(0, 2) if side == WEST else pl.ds(2, 2)
            src = cur.at[s, g, channels, row]
            dst = hx.at[s, 1 - side, g, pl.ds(0, 2)]
        else:
            src = cur.at[s, g, :, row]
            dst = hx.at[s, 1 - side, g]
        return pltpu.make_async_remote_copy(
            src, dst, send_sem.at[s, g, side], recv_sem.at[s, g, 1 - side],
            device_id=peer[side], device_id_type=MESH,
        )

    def y_copy(s, g, side):
        return pltpu.make_async_remote_copy(
            ys.at[s, side - 2, g], yr.at[s, 3 - side, g],
            send_sem.at[s, g, side], recv_sem.at[s, g, 5 - side],
            device_id=peer[side], device_id_type=MESH,
        )

    def copy_of(s, g, side, ocean):
        return x_copy(s, g, side, ocean) if side < 2 else y_copy(s, g, side)

    def start_copies(s, g, ocean):
        for side in range(4):
            @pl.when(has[side])
            def _():
                copy_of(s, g, side, ocean).start()

    def wait_arrivals(s, g, ocean):
        for side in range(4):
            @pl.when(has[side])
            def _():
                if side < 2:
                    lands = hx.at[s, side, g, pl.ds(0, 2)] if ocean else hx.at[s, side, g]
                else:
                    lands = yr.at[s, side - 2, g]
                pltpu.make_async_remote_copy(
                    lands, lands, send_sem.at[s, g, side], recv_sem.at[s, g, side],
                    device_id=peer[side], device_id_type=MESH,
                ).wait_recv()

    def wait_sends(ocean):
        def step(s, carry):
            def group(g, inner):
                for side in range(4):
                    @pl.when(has[side])
                    def _():
                        copy_of(s, g, side, ocean).wait_send()
                return inner
            return lax.fori_loop(0, groups, group, carry)
        lax.fori_loop(0, STEPS, step, 0)

    tiles = [(c, i) for c in range(4) for i in range(size_x)]

    def put(s, g, values):
        for (c, i), value in zip(tiles, values):
            cur[s, g, c, i] = value
            ys[s, 0, g, pl.ds(c * size_x + i, 1), :] = value[0:1]
            ys[s, 1, g, pl.ds(c * size_x + i, 1), :] = value[last_y:]

    def north_of(value, s, g, c, i):
        arrived = yr[s, 1, g, pl.ds(c * size_x + i, 1), :]
        return jnp.where(rows == last_y, arrived, pltpu.roll(value, size_y - 1, 0))

    def south_of(value, s, g, c, i):
        arrived = yr[s, 0, g, pl.ds(c * size_x + i, 1), :]
        return jnp.where(rows == 0, arrived, pltpu.roll(value, 1, 0))

    def ocean_part():
        def first(g, carry):
            load(g).wait()
            put(0, g, [raw[g, c, i] * wet[c, i] for c, i in tiles])
            start_copies(0, g, True)
            return carry

        lax.fori_loop(0, groups, first, 0)
        flux_load.wait()
        prey_load.wait()
        rate_load.wait()

        def pair_copy():
            return pltpu.make_async_remote_copy(
                run, flux.at[1], pair_send, pair_recv, device_id=partner, device_id_type=MESH
            )

        def step(s, carry):
            def field(f, inner):
                wait_arrivals(s, f, True)

                @pl.when(jnp.logical_and(s == NSUB, f == 2))
                def _():
                    pltpu.make_async_remote_copy(
                        light, light, pair_send, pair_recv,
                        device_id=partner, device_id_type=MESH,
                    ).wait_recv()
                    heat[...] = light[...] * HEATING

                of_u = jnp.where(f == 0, -DRAG, jnp.where(f == 1, -CORIOLIS, 0.0))
                of_v = jnp.where(f == 0, CORIOLIS, jnp.where(f == 1, -DRAG, 0.0))
                of_heat = jnp.where(f == 2, 1.0, 0.0)
                ageing = jnp.where(f == 4, 1.0, 0.0)
                values = []
                for c, i in tiles:
                    a, b = c // 2, c % 2
                    centre = cur[s, f, c, i]
                    if a == 0:
                        to_east = cur[s, f, 2 + b, i]
                        to_west = cur[s, f, 2 + b, i - 1] if i > 0 else hx[s, WEST, f, b]
                    else:
                        to_west = cur[s, f, b, i]
                        to_east = cur[s, f, b, i + 1] if i < last_x else hx[s, EAST, f, b]
                    other = cur[s, f, 2 * a + 1 - b, i]
                    if b == 0:
                        to_north = other
                        to_south = south_of(other, s, f, c + 1, i)
                    else:
                        to_south = other
                        to_north = north_of(other, s, f, c - 1, i)
                    u, v = cur[s, 0, c, i], cur[s, 1, c, i]
                    spread = to_east + to_west + to_north + to_south - 4.0 * centre
                    advect = u * (to_east - to_west) * 0.5 + v * (to_north - to_south) * 0.5
                    forcing = of_u * u + of_v * v + of_heat * heat[i] + ageing
                    values.append(wet[c, i] * (centre + DT * (NU * spread - advect + forcing)))

                put(s + 1, f, values)

                @pl.when(s < NSUB)
                def _():
                    start_copies(s + 1, f, True)

                for (c, i), value in zip(tiles, values):
                    out_ref[0, 4 * f + c, i] = value

                @pl.when(jnp.logical_and(f < 2, s < NSUB))
                def _():
                    for i in range(size_x):
                        total = sum(value for (_, row), value in zip(tiles, values) if row == i)
                        run[f, i] = run[f, i] + total * (0.25 / NSUB)

                @pl.when(jnp.logical_and(s == NSUB - 1, f == 1))
                def _():
                    pair_copy().start()
                return inner
            return lax.fori_loop(0, groups, field, carry)

        lax.fori_loop(0, STEPS, step, 0)
        wait_sends(True)
        pair_copy().wait_send()

    def tracer_part():
        def first(g, carry):
            load(g).wait()
            values = [raw[g, c, i] * wet[c, i] for c, i in tiles]
            put(0, g, values)
            start_copies(0, g, False)
            for (c, i), value in zip(tiles, values):
                tanhs[0, 4 * g + c, i] = jnp.tanh(value)
            return carry

        lax.fori_loop(0, groups, first, 0)
        flux_load.wait()
        prey_load.wait()
        rate_load.wait()

        def pair_copy():
            return pltpu.make_async_remote_copy(
                heat, light, pair_send, pair_recv, device_id=partner, device_id_type=MESH
            )

        def step(s, carry):
            now, later = lax.rem(s, 2), lax.rem(s + 1, 2)
            which = s // NSUB

            @pl.when(s == NSUB)
            def _():
                pltpu.make_async_remote_copy(
                    flux.at[1], flux.at[1], pair_send, pair_recv,
                    device_id=partner, device_id_type=MESH,
                ).wait_recv()

            def group(g, inner):
                wait_arrivals(s, g, False)
                values = []
                for c in range(4):
                    t = 4 * g + c
                    living = jnp.where(t < species, 1.0, 0.0)
                    slot = jnp.minimum(t, species - 1)
                    rate = rate_ref[slot] * living
                    mortality = MORTALITY * living
                    prey = prey_ref[slot]
                    for i in range(size_x):
                        centre = cur[s, g, c, i]
                        to_west = cur[s, g, c, i - 1] if i > 0 else hx[s, WEST, g, c]
                        to_east = cur[s, g, c, i + 1] if i < last_x else hx[s, EAST, g, c]
                        to_north = north_of(centre, s, g, c, i)
                        to_south = south_of(centre, s, g, c, i)
                        spread = to_east + to_west + to_north + to_south - 4.0 * centre
                        advect = (
                            flux[which, 0, i] * (to_east - to_west) * 0.5
                            + flux[which, 1, i] * (to_north - to_south) * 0.5
                        )
                        reaction = rate * centre * tanhs[now, prey, i] - mortality * centre
                        values.append(
                            wet[c, i] * (centre + DT * (NU * spread - advect + reaction))
                        )
                put(s + 1, g, values)

                @pl.when(s < NSUB)
                def _():
                    start_copies(s + 1, g, False)

                for (c, i), value in zip(tiles, values):
                    out_ref[0, 4 * g + c, i] = value
                    tanhs[later, 4 * g + c, i] = jnp.tanh(value)

                @pl.when(jnp.logical_and(s == NSUB - 1, g == 0))
                def _():
                    above = (
                        lax.broadcasted_iota(jnp.int32, (depth, depth), 0)
                        < lax.broadcasted_iota(jnp.int32, (depth, depth), 1)
                    ).astype(jnp.float32)
                    for i in range(size_x):
                        green = cur[s + 1, 0, 0, i]
                        soft = jnp.maximum(green, 0.0) + jnp.log(1.0 + jnp.exp(-jnp.abs(green)))
                        attenuation = wet[0, i] * (0.03 + 0.05 * soft)
                        overhead = jnp.dot(
                            attenuation, above, precision=lax.Precision.HIGHEST,
                            preferred_element_type=jnp.float32,
                        )
                        heat[i] = SURFACE * jnp.exp(-overhead) * (1.0 - jnp.exp(-attenuation))
                    pl.semaphore_wait(ready_sem, 1)
                    pair_copy().start()
                return inner
            return lax.fori_loop(0, groups, group, carry)

        lax.fori_loop(0, STEPS, step, 0)
        wait_sends(False)
        pair_copy().wait_send()

    greeted = is_ocean.astype(jnp.int32)
    for side in range(4):
        greeted = greeted + has[side].astype(jnp.int32)
    pl.semaphore_wait(barrier, greeted)

    @pl.when(is_ocean)
    def _():
        pl.semaphore_signal(ready_sem, inc=1, device_id=partner, device_id_type=MESH)

    pl.when(is_ocean)(ocean_part)
    pl.when(jnp.logical_not(is_ocean))(tracer_part)


def body(state, levels, old_flux, eco_prey, eco_rate):
    channels, size_x, size_y, depth = state.shape[1:]
    groups = channels // 4
    f32 = jnp.float32
    tile = (size_x, size_y, depth)
    return pl.pallas_call(
        kernel,
        out_shape=pltpu.VMEM(state.shape, f32),
        in_specs=[pl.BlockSpec(memory_space=pltpu.HBM)] * 5,
        out_specs=pl.BlockSpec(memory_space=pltpu.VMEM),
        scratch_shapes=[
            pltpu.VMEM(levels.shape, levels.dtype),
            pltpu.SMEM(eco_prey.shape, eco_prey.dtype),
            pltpu.SMEM(eco_rate.shape, eco_rate.dtype),
            pltpu.VMEM((groups, 4) + tile, f32),
            pltpu.VMEM((STEPS + 1, groups, 4) + tile, f32),
            pltpu.VMEM((2, channels) + tile, f32),
            pltpu.VMEM((STEPS, 2, groups, 4, size_y, depth), f32),
            pltpu.VMEM((STEPS + 1, 2, groups, 4 * size_x, depth), f32),
            pltpu.VMEM((STEPS, 2, groups, 4 * size_x, depth), f32),
            pltpu.VMEM((4,) + tile, f32),
            pltpu.VMEM((2, 2) + tile, f32),
            pltpu.VMEM((2,) + tile, f32),
            pltpu.VMEM(tile, f32),
            pltpu.VMEM(tile, f32),
            pltpu.SemaphoreType.DMA((groups,)),
            pltpu.SemaphoreType.DMA((4,)),
            pltpu.SemaphoreType.DMA((STEPS, groups, 4)),
            pltpu.SemaphoreType.DMA((STEPS, groups, 4)),
            pltpu.SemaphoreType.DMA,
            pltpu.SemaphoreType.DMA,
            pltpu.SemaphoreType.REGULAR,
        ],
        compiler_params=pltpu.CompilerParams(
            collective_id=0, has_side_effects=True, vmem_limit_bytes=60 * 1024 * 1024
        ),
    )(state, levels, old_flux, eco_prey, eco_rate)


def solution(mesh):
    placed = (
        P("half", None, "gx", "gy", None),
        P(None, "gx", "gy"),
        P(None, "gx", "gy", None),
        P(),
        P(),
    )
    return jax.shard_map(
        body,
        mesh=mesh,
        in_specs=placed,
        out_specs=P("half", None, "gx", "gy", None),
        check_vma=False,
    )
```

```python
import jax
import jax.numpy as jnp
from jax import lax
from jax.experimental import pallas as pl
from jax.experimental.pallas import tpu as pltpu
from jax.sharding import PartitionSpec as P

NSUB = 4
STEPS = NSUB + 1
DT = 0.1
NU = 1.0
CORIOLIS = 0.5
DRAG = 0.1
MORTALITY = 0.1
HEATING = 2.0
SURFACE = 8.0
MESH = pl.DeviceIdType.MESH
WEST, EAST, SOUTH, NORTH = 0, 1, 2, 3


def kernel(
    state_hbm, levels_hbm, flux_hbm, prey_hbm, rate_hbm, out_ref,
    levels_ref, prey_ref, rate_ref, raw, cur, tanhs, preys, hosts, hx, ys, yr, wet, wetc, flux, run, light, heat,
    load_sem, small_sem, send_sem, recv_sem, pair_send, pair_recv, ready_sem,
):
    groups = raw.shape[0]
    guest = groups - 1
    own = guest
    size_x, size_y, depth = cur.shape[3:]
    last_x, last_y = size_x - 1, size_y - 1
    species = prey_ref.shape[0]
    half = lax.axis_index("half")
    gx, gy = lax.axis_index("gx"), lax.axis_index("gy")
    nx, ny = lax.axis_size("gx"), lax.axis_size("gy")
    is_ocean = half == 0
    has = (gx > 0, gx < nx - 1, gy > 0, gy < ny - 1)
    peer = ({"gx": gx - 1}, {"gx": gx + 1}, {"gy": gy - 1}, {"gy": gy + 1})
    partner = {"half": 1 - half}

    def load(g):
        return pltpu.make_async_copy(state_hbm.at[0, pl.ds(4 * g, 4)], raw.at[g], load_sem.at[g])

    levels_load = pltpu.make_async_copy(levels_hbm, levels_ref, small_sem.at[0])
    flux_load = pltpu.make_async_copy(flux_hbm, flux.at[0], small_sem.at[1])
    prey_load = pltpu.make_async_copy(prey_hbm, prey_ref, small_sem.at[2])
    rate_load = pltpu.make_async_copy(rate_hbm, rate_ref, small_sem.at[3])
    levels_load.start()
    for g in range(groups):
        load(g).start()
    flux_load.start()
    prey_load.start()
    rate_load.start()

    barrier = pltpu.get_barrier_semaphore()
    for side in range(4):
        @pl.when(has[side])
        def _():
            pl.semaphore_signal(barrier, inc=1, device_id=peer[side], device_id_type=MESH)

    @pl.when(jnp.logical_not(is_ocean))
    def _():
        pl.semaphore_signal(barrier, inc=1, device_id=partner, device_id_type=MESH)

    for side in (WEST, EAST):
        @pl.when(jnp.logical_not(has[side]))
        def _():
            for s in range(STEPS):
                hx[s, side] = jnp.zeros(hx.shape[2:], jnp.float32)
    for side in (SOUTH, NORTH):
        @pl.when(jnp.logical_not(has[side]))
        def _():
            for s in range(STEPS):
                yr[s, side - 2] = jnp.zeros(yr.shape[2:], jnp.float32)

    rows = lax.broadcasted_iota(jnp.int32, (size_y, depth), 0)
    level_k = lax.broadcasted_iota(jnp.int32, (size_y, depth), 1).astype(jnp.float32)
    diagonal = lax.broadcasted_iota(jnp.int32, (size_y, size_y), 0) == lax.broadcasted_iota(
        jnp.int32, (size_y, size_y), 1
    )
    levels_load.wait()
    for i in range(size_x):
        active = []
        for c in range(4):
            line = levels_ref[c, pl.ds(i, 1), :].astype(jnp.float32)
            spread = jnp.where(diagonal, jnp.broadcast_to(line, (size_y, size_y)), 0.0)
            active.append(jnp.sum(spread, axis=1, keepdims=True))
        most = jnp.maximum(jnp.maximum(active[0], active[1]), jnp.maximum(active[2], active[3]))
        for c in range(4):
            wet[c, i] = jnp.where(level_k < active[c], 1.0, 0.0)
        wetc[i] = jnp.where(level_k < most, 1.0, 0.0)

    run[...] = jnp.zeros(run.shape, jnp.float32)
    heat[...] = jnp.zeros(heat.shape, jnp.float32)

    def x_copy(s, g, side, ocean):
        row = 0 if side == WEST else last_x
        if ocean:
            channels = pl.ds(0, 2) if side == WEST else pl.ds(2, 2)
            src = cur.at[s, g, channels, row]
            dst = hx.at[s, 1 - side, g, pl.ds(0, 2)]
        else:
            src = cur.at[s, g, :, row]
            dst = hx.at[s, 1 - side, g]
        return pltpu.make_async_remote_copy(
            src, dst, send_sem.at[s, g, side], recv_sem.at[s, g, 1 - side],
            device_id=peer[side], device_id_type=MESH,
        )

    def y_copy(s, g, side):
        return pltpu.make_async_remote_copy(
            ys.at[s, side - 2, g], yr.at[s, 3 - side, g],
            send_sem.at[s, g, side], recv_sem.at[s, g, 5 - side],
            device_id=peer[side], device_id_type=MESH,
        )

    def copy_of(s, g, side, ocean):
        return x_copy(s, g, side, ocean) if side < 2 else y_copy(s, g, side)

    def start_copies(s, g, ocean):
        for side in range(4):
            @pl.when(has[side])
            def _():
                copy_of(s, g, side, ocean).start()

    def wait_arrivals(s, g, ocean):
        for side in range(4):
            @pl.when(has[side])
            def _():
                if side < 2:
                    lands = hx.at[s, side, g, pl.ds(0, 2)] if ocean else hx.at[s, side, g]
                else:
                    lands = yr.at[s, side - 2, g]
                pltpu.make_async_remote_copy(
                    lands, lands, send_sem.at[s, g, side], recv_sem.at[s, g, side],
                    device_id=peer[side], device_id_type=MESH,
                ).wait_recv()

    def pair_copy(src, dst, n):
        return pltpu.make_async_remote_copy(
            src, dst, pair_send.at[n], pair_recv.at[n], device_id=partner, device_id_type=MESH
        )

    def flux_copy():
        return pair_copy(run, flux.at[1], 0)

    def light_copy():
        return pair_copy(heat, light, 0)

    def guest_copy():
        return pair_copy(cur.at[0, guest], cur.at[0, groups], 1)

    def result_copy():
        return pair_copy(cur.at[STEPS, groups], out_ref.at[0, pl.ds(4 * guest, 4)], 1)

    def prey_copy(s):
        return pair_copy(preys.at[s], preys.at[s], 2 + s)

    def host_copy(s):
        return pair_copy(hosts.at[s], hosts.at[s], 2 + s)

    def wait_sends(first, end, ocean):
        def step(s, carry):
            def group(g, inner):
                for side in range(4):
                    @pl.when(has[side])
                    def _():
                        copy_of(s, g, side, ocean).wait_send()
                return inner
            return lax.fori_loop(first, end, group, carry)
        lax.fori_loop(0, STEPS, step, 0)

    tiles = [(c, i) for c in range(4) for i in range(size_x)]

    def put(s, g, values):
        for (c, i), value in zip(tiles, values):
            cur[s, g, c, i] = value
        put_rows(s, g, values)

    def put_rows(s, g, values):
        for (c, i), value in zip(tiles, values):
            ys[s, 0, g, pl.ds(c * size_x + i, 1), :] = value[0:1]
            ys[s, 1, g, pl.ds(c * size_x + i, 1), :] = value[last_y:]

    def north_of(value, s, g, c, i):
        arrived = yr[s, 1, g, pl.ds(c * size_x + i, 1), :]
        return jnp.where(rows == last_y, arrived, pltpu.roll(value, size_y - 1, 0))

    def south_of(value, s, g, c, i):
        arrived = yr[s, 0, g, pl.ds(c * size_x + i, 1), :]
        return jnp.where(rows == 0, arrived, pltpu.roll(value, 1, 0))

    def tracer_values(s, which, g, start, prey_tile):
        values = []
        for c in range(4):
            t = start + c
            living = jnp.where(t < species, 1.0, 0.0)
            slot = jnp.minimum(t, species - 1)
            rate = rate_ref[slot] * living
            mortality = MORTALITY * living
            prey = prey_ref[slot]
            for i in range(size_x):
                centre = cur[s, g, c, i]
                to_west = cur[s, g, c, i - 1] if i > 0 else hx[s, WEST, g, c]
                to_east = cur[s, g, c, i + 1] if i < last_x else hx[s, EAST, g, c]
                to_north = north_of(centre, s, g, c, i)
                to_south = south_of(centre, s, g, c, i)
                spread = to_east + to_west + to_north + to_south - 4.0 * centre
                advect = (
                    flux[which, 0, i] * (to_east - to_west) * 0.5
                    + flux[which, 1, i] * (to_north - to_south) * 0.5
                )
                reaction = rate * centre * prey_tile(prey, c, i) - mortality * centre
                values.append(wetc[i] * (centre + DT * (NU * spread - advect + reaction)))
        return values

    def ocean_part():
        def first(g, carry):
            load(g).wait()
            put(0, g, [raw[g, c, i] * wet[c, i] for c, i in tiles])
            start_copies(0, g, True)
            return carry

        lax.fori_loop(0, groups, first, 0)
        flux_load.wait()
        prey_load.wait()
        rate_load.wait()

        guest_copy().wait_recv()
        values = [cur[0, groups, c, i] for c, i in tiles]
        put_rows(0, groups, values)
        start_copies(0, groups, False)
        for (c, i), value in zip(tiles, values):
            hosts[0, c, i] = jnp.tanh(value)

        def step(s, carry):
            def field(f, inner):
                wait_arrivals(s, f, True)

                @pl.when(jnp.logical_and(s == NSUB, f == 2))
                def _():
                    light_copy().wait_recv()
                    heat[...] = light[...] * HEATING

                of_u = jnp.where(f == 0, -DRAG, jnp.where(f == 1, -CORIOLIS, 0.0))
                of_v = jnp.where(f == 0, CORIOLIS, jnp.where(f == 1, -DRAG, 0.0))
                of_heat = jnp.where(f == 2, 1.0, 0.0)
                ageing = jnp.where(f == 4, 1.0, 0.0)
                values = []
                for c, i in tiles:
                    a, b = c // 2, c % 2
                    centre = cur[s, f, c, i]
                    if a == 0:
                        to_east = cur[s, f, 2 + b, i]
                        to_west = cur[s, f, 2 + b, i - 1] if i > 0 else hx[s, WEST, f, b]
                    else:
                        to_west = cur[s, f, b, i]
                        to_east = cur[s, f, b, i + 1] if i < last_x else hx[s, EAST, f, b]
                    other = cur[s, f, 2 * a + 1 - b, i]
                    if b == 0:
                        to_north = other
                        to_south = south_of(other, s, f, c + 1, i)
                    else:
                        to_south = other
                        to_north = north_of(other, s, f, c - 1, i)
                    u, v = cur[s, 0, c, i], cur[s, 1, c, i]
                    spread = to_east + to_west + to_north + to_south - 4.0 * centre
                    advect = u * (to_east - to_west) * 0.5 + v * (to_north - to_south) * 0.5
                    forcing = of_u * u + of_v * v + of_heat * heat[i] + ageing
                    values.append(wet[c, i] * (centre + DT * (NU * spread - advect + forcing)))

                put(s + 1, f, values)

                @pl.when(s < NSUB)
                def _():
                    start_copies(s + 1, f, True)

                for (c, i), value in zip(tiles, values):
                    out_ref[0, 4 * f + c, i] = value

                @pl.when(jnp.logical_and(f < 2, s < NSUB))
                def _():
                    for i in range(size_x):
                        total = sum(value for (_, row), value in zip(tiles, values) if row == i)
                        run[f, i] = run[f, i] + total * (0.25 / NSUB)

                @pl.when(jnp.logical_and(s == NSUB - 1, f == 1))
                def _():
                    flux_copy().start()
                    flux[1] = run[...]

                return inner
            lax.fori_loop(0, groups, field, 0)

            wait_arrivals(s, groups, False)
            prey_copy(s).wait_recv()

            def prey_tile(prey, c, i):
                tile = preys[s, c, i]
                for h in range(4):
                    tile = jnp.where(prey == 4 * guest + h, hosts[s, h, i], tile)
                return tile

            values = tracer_values(s, s // NSUB, groups, 4 * guest, prey_tile)
            put(s + 1, groups, values)

            @pl.when(s < NSUB)
            def _():
                start_copies(s + 1, groups, False)
                for (c, i), value in zip(tiles, values):
                    hosts[s + 1, c, i] = jnp.tanh(value)
                host_copy(s + 1).start()

            return carry

        lax.fori_loop(0, STEPS, step, 0)
        result_copy().start()
        wait_sends(0, groups, True)
        wait_sends(groups, groups + 1, False)
        flux_copy().wait_send()
        for s in range(1, STEPS):
            host_copy(s).wait_send()
        result_copy().wait_send()

    def tracer_part():
        def first(g, carry):
            load(g).wait()
            values = [raw[g, c, i] * wetc[i] for c, i in tiles]
            put(0, g, values)

            @pl.when(g < own)
            def _():
                start_copies(0, g, False)

            @pl.when(g == guest)
            def _():
                pl.semaphore_wait(ready_sem, 1)
                guest_copy().start()

            for (c, i), value in zip(tiles, values):
                tanhs[0, 4 * g + c, i] = jnp.tanh(value)
            return carry

        lax.fori_loop(0, groups, first, 0)
        flux_load.wait()
        prey_load.wait()
        rate_load.wait()

        def send_preys(s):
            for c in range(4):
                prey = prey_ref[min(4 * guest + c, species - 1)]
                for i in range(size_x):
                    preys[s, c, i] = tanhs[lax.rem(s, 2), prey, i]
            prey_copy(s).start()

        send_preys(0)

        def step(s, carry):
            now, later = lax.rem(s, 2), lax.rem(s + 1, 2)

            @pl.when(s > 0)
            def _():
                host_copy(s).wait_recv()
                for c, i in tiles:
                    tanhs[now, 4 * guest + c, i] = hosts[s, c, i]

            @pl.when(s == NSUB)
            def _():
                flux_copy().wait_recv()

            def group(g, inner):
                wait_arrivals(s, g, False)
                values = tracer_values(
                    s, s // NSUB, g, 4 * g, lambda prey, c, i: tanhs[now, prey, i]
                )
                put(s + 1, g, values)

                @pl.when(s < NSUB)
                def _():
                    start_copies(s + 1, g, False)

                for (c, i), value in zip(tiles, values):
                    out_ref[0, 4 * g + c, i] = value
                    tanhs[later, 4 * g + c, i] = jnp.tanh(value)

                @pl.when(jnp.logical_and(s == NSUB - 1, g == 0))
                def _():
                    above = (
                        lax.broadcasted_iota(jnp.int32, (depth, depth), 0)
                        < lax.broadcasted_iota(jnp.int32, (depth, depth), 1)
                    ).astype(jnp.float32)
                    for i in range(size_x):
                        green = cur[s + 1, 0, 0, i]
                        soft = jnp.maximum(green, 0.0) + jnp.log(1.0 + jnp.exp(-jnp.abs(green)))
                        attenuation = wetc[i] * (0.03 + 0.05 * soft)
                        overhead = jnp.dot(
                            attenuation, above, precision=lax.Precision.HIGHEST,
                            preferred_element_type=jnp.float32,
                        )
                        heat[i] = SURFACE * jnp.exp(-overhead) * (1.0 - jnp.exp(-attenuation))
                    light_copy().start()

                return inner
            lax.fori_loop(0, own, group, 0)

            @pl.when(s < NSUB)
            def _():
                send_preys(s + 1)

            return carry

        lax.fori_loop(0, STEPS, step, 0)
        wait_sends(0, own, False)
        guest_copy().wait_send()
        light_copy().wait_send()
        for s in range(STEPS):
            prey_copy(s).wait_send()
        result_copy().wait_recv()

    greeted = is_ocean.astype(jnp.int32)
    for side in range(4):
        greeted = greeted + has[side].astype(jnp.int32)
    pl.semaphore_wait(barrier, greeted)

    @pl.when(is_ocean)
    def _():
        pl.semaphore_signal(ready_sem, inc=1, device_id=partner, device_id_type=MESH)

    pl.when(is_ocean)(ocean_part)
    pl.when(jnp.logical_not(is_ocean))(tracer_part)


def body(state, levels, old_flux, eco_prey, eco_rate):
    channels, size_x, size_y, depth = state.shape[1:]
    groups = channels // 4
    slots = groups + 1
    f32 = jnp.float32
    tile = (size_x, size_y, depth)
    return pl.pallas_call(
        kernel,
        out_shape=pltpu.VMEM(state.shape, f32),
        in_specs=[pl.BlockSpec(memory_space=pltpu.HBM)] * 5,
        out_specs=pl.BlockSpec(memory_space=pltpu.VMEM),
        scratch_shapes=[
            pltpu.VMEM(levels.shape, levels.dtype),
            pltpu.SMEM(eco_prey.shape, eco_prey.dtype),
            pltpu.SMEM(eco_rate.shape, eco_rate.dtype),
            pltpu.VMEM((groups, 4) + tile, f32),
            pltpu.VMEM((STEPS + 1, slots, 4) + tile, f32),
            pltpu.VMEM((2, channels) + tile, f32),
            pltpu.VMEM((STEPS, 4) + tile, f32),
            pltpu.VMEM((STEPS, 4) + tile, f32),
            pltpu.VMEM((STEPS, 2, slots, 4, size_y, depth), f32),
            pltpu.VMEM((STEPS + 1, 2, slots, 4 * size_x, depth), f32),
            pltpu.VMEM((STEPS, 2, slots, 4 * size_x, depth), f32),
            pltpu.VMEM((4,) + tile, f32),
            pltpu.VMEM(tile, f32),
            pltpu.VMEM((2, 2) + tile, f32),
            pltpu.VMEM((2,) + tile, f32),
            pltpu.VMEM(tile, f32),
            pltpu.VMEM(tile, f32),
            pltpu.SemaphoreType.DMA((groups,)),
            pltpu.SemaphoreType.DMA((4,)),
            pltpu.SemaphoreType.DMA((STEPS, slots, 4)),
            pltpu.SemaphoreType.DMA((STEPS, slots, 4)),
            pltpu.SemaphoreType.DMA((2 + STEPS,)),
            pltpu.SemaphoreType.DMA((2 + STEPS,)),
            pltpu.SemaphoreType.REGULAR,
        ],
        compiler_params=pltpu.CompilerParams(
            collective_id=0, has_side_effects=True, vmem_limit_bytes=60 * 1024 * 1024
        ),
    )(state, levels, old_flux, eco_prey, eco_rate)


def solution(mesh):
    placed = (
        P("half", None, "gx", "gy", None),
        P(None, "gx", "gy"),
        P(None, "gx", "gy", None),
        P(),
        P(),
    )
    return jax.shard_map(
        body,
        mesh=mesh,
        in_specs=placed,
        out_specs=P("half", None, "gx", "gy", None),
        check_vma=False,
    )
```

```python
import jax
import jax.numpy as jnp
from jax import lax
from jax.experimental import pallas as pl
from jax.experimental.pallas import tpu as pltpu
from jax.sharding import PartitionSpec as P

NSUB = 4
STEPS = NSUB + 1
DT = 0.1
NU = 1.0
CORIOLIS = 0.5
DRAG = 0.1
MORTALITY = 0.1
HEATING = 2.0
SURFACE = 8.0
MESH = pl.DeviceIdType.MESH
WEST, EAST, SOUTH, NORTH = 0, 1, 2, 3
BATCHES = 2


def kernel(
    state_hbm, levels_hbm, flux_hbm, prey_hbm, rate_hbm, out_ref,
    levels_ref, prey_ref, rate_ref, raw, cur, tanhs, hx, ys, yr, wet, flux, run, light, heat,
    load_sem, small_sem, send_sem, recv_sem, pair_send, pair_recv, ready_sem,
):
    groups = cur.shape[1]
    size_x, size_y, depth = cur.shape[3:]
    last_x, last_y = size_x - 1, size_y - 1
    species = prey_ref.shape[0]
    half = lax.axis_index("half")
    gx, gy = lax.axis_index("gx"), lax.axis_index("gy")
    nx, ny = lax.axis_size("gx"), lax.axis_size("gy")
    is_ocean = half == 0
    has = (gx > 0, gx < nx - 1, gy > 0, gy < ny - 1)
    peer = ((half, gx - 1, gy), (half, gx + 1, gy), (half, gx, gy - 1), (half, gx, gy + 1))
    partner = (1 - half, gx, gy)
    bounds = [groups * n // BATCHES for n in range(BATCHES + 1)]
    batches = [(n, bounds[n], bounds[n + 1]) for n in range(BATCHES)]

    def load(g):
        return pltpu.make_async_copy(state_hbm.at[0, pl.ds(4 * g, 4)], raw.at[g], load_sem.at[g])

    levels_load = pltpu.make_async_copy(levels_hbm, levels_ref, small_sem.at[0])
    flux_load = pltpu.make_async_copy(flux_hbm, flux.at[0], small_sem.at[1])
    prey_load = pltpu.make_async_copy(prey_hbm, prey_ref, small_sem.at[2])
    rate_load = pltpu.make_async_copy(rate_hbm, rate_ref, small_sem.at[3])
    levels_load.start()
    for g in range(groups):
        load(g).start()
    flux_load.start()
    prey_load.start()
    rate_load.start()

    barrier = pltpu.get_barrier_semaphore()
    for side in range(4):
        @pl.when(has[side])
        def _():
            pl.semaphore_signal(barrier, inc=1, device_id=peer[side], device_id_type=MESH)

    @pl.when(jnp.logical_not(is_ocean))
    def _():
        pl.semaphore_signal(barrier, inc=1, device_id=partner, device_id_type=MESH)

    for side in (WEST, EAST):
        @pl.when(jnp.logical_not(has[side]))
        def _():
            for s in range(STEPS):
                hx[s, side] = jnp.zeros(hx.shape[2:], jnp.float32)
    for side in (SOUTH, NORTH):
        @pl.when(jnp.logical_not(has[side]))
        def _():
            for s in range(STEPS):
                yr[s, side - 2] = jnp.zeros(yr.shape[2:], jnp.float32)

    rows = lax.broadcasted_iota(jnp.int32, (size_y, depth), 0)
    level_k = lax.broadcasted_iota(jnp.int32, (size_y, depth), 1).astype(jnp.float32)
    diagonal = lax.broadcasted_iota(jnp.int32, (size_y, size_y), 0) == lax.broadcasted_iota(
        jnp.int32, (size_y, size_y), 1
    )
    levels_load.wait()
    for i in range(size_x):
        active = []
        for c in range(4):
            line = levels_ref[c, pl.ds(i, 1), :].astype(jnp.float32)
            spread = jnp.where(diagonal, jnp.broadcast_to(line, (size_y, size_y)), 0.0)
            active.append(jnp.sum(spread, axis=1, keepdims=True))
        most = jnp.maximum(jnp.maximum(active[0], active[1]), jnp.maximum(active[2], active[3]))
        for c in range(4):
            mine = jnp.where(is_ocean, active[c], most)
            wet[c, i] = jnp.where(level_k < mine, 1.0, 0.0)

    run[...] = jnp.zeros(run.shape, jnp.float32)
    heat[...] = jnp.zeros(heat.shape, jnp.float32)

    def copy_of(s, batch, side, ocean):
        n, low, high = batch
        span = pl.ds(low, high - low)
        if side < 2:
            row = 0 if side == WEST else last_x
            if ocean:
                channels = pl.ds(0, 2) if side == WEST else pl.ds(2, 2)
                src = cur.at[s, span, channels, row]
                dst = hx.at[s, 1 - side, span, pl.ds(0, 2)]
            else:
                src = cur.at[s, span, :, row]
                dst = hx.at[s, 1 - side, span]
        else:
            src = ys.at[s, side - 2, span]
            dst = yr.at[s, 3 - side, span]
        lands = 1 - side if side < 2 else 5 - side
        return pltpu.make_async_remote_copy(
            src, dst, send_sem.at[side], recv_sem.at[s, n, lands],
            device_id=peer[side], device_id_type=MESH,
        )

    def start_copies(s, batch, ocean):
        for side in range(4):
            @pl.when(has[side])
            def _():
                copy_of(s, batch, side, ocean).start()

    def wait_arrivals(s, batch, ocean):
        n, low, high = batch
        span = pl.ds(low, high - low)
        for side in range(4):
            @pl.when(has[side])
            def _():
                if side < 2:
                    lands = hx.at[s, side, span, pl.ds(0, 2)] if ocean else hx.at[s, side, span]
                else:
                    lands = yr.at[s, side - 2, span]
                pltpu.make_async_remote_copy(
                    lands, lands, send_sem.at[side], recv_sem.at[s, n, side],
                    device_id=peer[side], device_id_type=MESH,
                ).wait_recv()

    def wait_sends(ocean):
        for side in range(4):
            @pl.when(has[side])
            def _():
                if side < 2:
                    sent = hx.at[:, side, :, pl.ds(0, 2)] if ocean else hx.at[:, side]
                else:
                    sent = yr.at[:, side - 2]
                pltpu.make_async_remote_copy(
                    sent, sent, send_sem.at[side], recv_sem.at[0, 0, side],
                    device_id=peer[side], device_id_type=MESH,
                ).wait_send()

    tiles = [(c, i) for c in range(4) for i in range(size_x)]

    def put(s, g, values):
        for (c, i), value in zip(tiles, values):
            cur[s, g, c, i] = value
            ys[s, 0, g, pl.ds(c * size_x + i, 1), :] = value[0:1]
            ys[s, 1, g, pl.ds(c * size_x + i, 1), :] = value[last_y:]

    def north_of(value, s, g, c, i):
        arrived = yr[s, 1, g, pl.ds(c * size_x + i, 1), :]
        return jnp.where(rows == last_y, arrived, pltpu.roll(value, size_y - 1, 0))

    def south_of(value, s, g, c, i):
        arrived = yr[s, 0, g, pl.ds(c * size_x + i, 1), :]
        return jnp.where(rows == 0, arrived, pltpu.roll(value, 1, 0))

    def ocean_part():
        def first(g, carry):
            load(g).wait()
            put(0, g, [raw[g, c, i] * wet[c, i] for c, i in tiles])
            return carry

        for batch in batches:
            lax.fori_loop(batch[1], batch[2], first, 0)
            start_copies(0, batch, True)
        flux_load.wait()
        prey_load.wait()
        rate_load.wait()

        def pair_copy():
            return pltpu.make_async_remote_copy(
                run, flux.at[1], pair_send, pair_recv, device_id=partner, device_id_type=MESH
            )

        def step(s, carry):
            def field(f, inner):
                @pl.when(jnp.logical_and(s == NSUB, f == 2))
                def _():
                    pltpu.make_async_remote_copy(
                        light, light, pair_send, pair_recv,
                        device_id=partner, device_id_type=MESH,
                    ).wait_recv()
                    heat[...] = light[...] * HEATING

                of_u = jnp.where(f == 0, -DRAG, jnp.where(f == 1, -CORIOLIS, 0.0))
                of_v = jnp.where(f == 0, CORIOLIS, jnp.where(f == 1, -DRAG, 0.0))
                of_heat = jnp.where(f == 2, 1.0, 0.0)
                ageing = jnp.where(f == 4, 1.0, 0.0)
                values = []
                for c, i in tiles:
                    a, b = c // 2, c % 2
                    centre = cur[s, f, c, i]
                    if a == 0:
                        to_east = cur[s, f, 2 + b, i]
                        to_west = cur[s, f, 2 + b, i - 1] if i > 0 else hx[s, WEST, f, b]
                    else:
                        to_west = cur[s, f, b, i]
                        to_east = cur[s, f, b, i + 1] if i < last_x else hx[s, EAST, f, b]
                    other = cur[s, f, 2 * a + 1 - b, i]
                    if b == 0:
                        to_north = other
                        to_south = south_of(other, s, f, c + 1, i)
                    else:
                        to_south = other
                        to_north = north_of(other, s, f, c - 1, i)
                    u, v = cur[s, 0, c, i], cur[s, 1, c, i]
                    spread = to_east + to_west + to_north + to_south - 4.0 * centre
                    advect = u * (to_east - to_west) * 0.5 + v * (to_north - to_south) * 0.5
                    forcing = of_u * u + of_v * v + of_heat * heat[i] + ageing
                    values.append(wet[c, i] * (centre + DT * (NU * spread - advect + forcing)))

                put(s + 1, f, values)

                for (c, i), value in zip(tiles, values):
                    out_ref[0, 4 * f + c, i] = value

                @pl.when(jnp.logical_and(f < 2, s < NSUB))
                def _():
                    for i in range(size_x):
                        total = sum(value for (_, row), value in zip(tiles, values) if row == i)
                        run[f, i] = run[f, i] + total * (0.25 / NSUB)

                @pl.when(jnp.logical_and(s == NSUB - 1, f == 1))
                def _():
                    pair_copy().start()
                return inner

            for batch in batches:
                wait_arrivals(s, batch, True)
                lax.fori_loop(batch[1], batch[2], field, 0)

                @pl.when(s < NSUB)
                def _():
                    start_copies(s + 1, batch, True)
            return carry

        lax.fori_loop(0, STEPS, step, 0)
        wait_sends(True)
        pair_copy().wait_send()

    def tracer_part():
        def first(g, carry):
            load(g).wait()
            values = [raw[g, c, i] * wet[c, i] for c, i in tiles]
            put(0, g, values)
            for (c, i), value in zip(tiles, values):
                tanhs[0, 4 * g + c, i] = jnp.tanh(value)
            return carry

        for batch in batches:
            lax.fori_loop(batch[1], batch[2], first, 0)
            start_copies(0, batch, False)
        flux_load.wait()
        prey_load.wait()
        rate_load.wait()

        def pair_copy():
            return pltpu.make_async_remote_copy(
                heat, light, pair_send, pair_recv, device_id=partner, device_id_type=MESH
            )

        def step(s, carry):
            now, later = lax.rem(s, 2), lax.rem(s + 1, 2)
            which = s // NSUB

            @pl.when(s == NSUB)
            def _():
                pltpu.make_async_remote_copy(
                    flux.at[1], flux.at[1], pair_send, pair_recv,
                    device_id=partner, device_id_type=MESH,
                ).wait_recv()

            def group(g, inner):
                values = []
                for c in range(4):
                    t = 4 * g + c
                    living = jnp.where(t < species, 1.0, 0.0)
                    slot = jnp.minimum(t, species - 1)
                    rate = rate_ref[slot] * living
                    mortality = MORTALITY * living
                    prey = prey_ref[slot]
                    for i in range(size_x):
                        centre = cur[s, g, c, i]
                        to_west = cur[s, g, c, i - 1] if i > 0 else hx[s, WEST, g, c]
                        to_east = cur[s, g, c, i + 1] if i < last_x else hx[s, EAST, g, c]
                        to_north = north_of(centre, s, g, c, i)
                        to_south = south_of(centre, s, g, c, i)
                        spread = to_east + to_west + to_north + to_south - 4.0 * centre
                        advect = (
                            flux[which, 0, i] * (to_east - to_west) * 0.5
                            + flux[which, 1, i] * (to_north - to_south) * 0.5
                        )
                        reaction = rate * centre * tanhs[now, prey, i] - mortality * centre
                        values.append(
                            wet[c, i] * (centre + DT * (NU * spread - advect + reaction))
                        )
                put(s + 1, g, values)

                for (c, i), value in zip(tiles, values):
                    out_ref[0, 4 * g + c, i] = value
                    tanhs[later, 4 * g + c, i] = jnp.tanh(value)

                @pl.when(jnp.logical_and(s == NSUB - 1, g == 0))
                def _():
                    above = (
                        lax.broadcasted_iota(jnp.int32, (depth, depth), 0)
                        < lax.broadcasted_iota(jnp.int32, (depth, depth), 1)
                    ).astype(jnp.float32)
                    for i in range(size_x):
                        green = cur[s + 1, 0, 0, i]
                        soft = jnp.maximum(green, 0.0) + jnp.log(1.0 + jnp.exp(-jnp.abs(green)))
                        attenuation = wet[0, i] * (0.03 + 0.05 * soft)
                        overhead = jnp.dot(
                            attenuation, above, precision=lax.Precision.HIGHEST,
                            preferred_element_type=jnp.float32,
                        )
                        heat[i] = SURFACE * jnp.exp(-overhead) * (1.0 - jnp.exp(-attenuation))
                    pl.semaphore_wait(ready_sem, 1)
                    pair_copy().start()
                return inner

            for batch in batches:
                wait_arrivals(s, batch, False)
                lax.fori_loop(batch[1], batch[2], group, 0)

                @pl.when(s < NSUB)
                def _():
                    start_copies(s + 1, batch, False)
            return carry

        lax.fori_loop(0, STEPS, step, 0)
        wait_sends(False)
        pair_copy().wait_send()

    greeted = is_ocean.astype(jnp.int32)
    for side in range(4):
        greeted = greeted + has[side].astype(jnp.int32)
    pl.semaphore_wait(barrier, greeted)

    @pl.when(is_ocean)
    def _():
        pl.semaphore_signal(ready_sem, inc=1, device_id=partner, device_id_type=MESH)

    pl.when(is_ocean)(ocean_part)
    pl.when(jnp.logical_not(is_ocean))(tracer_part)


def body(state, levels, old_flux, eco_prey, eco_rate):
    channels, size_x, size_y, depth = state.shape[1:]
    groups = channels // 4
    f32 = jnp.float32
    tile = (size_x, size_y, depth)
    return pl.pallas_call(
        kernel,
        out_shape=pltpu.VMEM(state.shape, f32),
        in_specs=[pl.BlockSpec(memory_space=pltpu.HBM)] * 5,
        out_specs=pl.BlockSpec(memory_space=pltpu.VMEM),
        scratch_shapes=[
            pltpu.VMEM(levels.shape, levels.dtype),
            pltpu.SMEM(eco_prey.shape, eco_prey.dtype),
            pltpu.SMEM(eco_rate.shape, eco_rate.dtype),
            pltpu.VMEM((groups, 4) + tile, f32),
            pltpu.VMEM((STEPS + 1, groups, 4) + tile, f32),
            pltpu.VMEM((2, channels) + tile, f32),
            pltpu.VMEM((STEPS, 2, groups, 4, size_y, depth), f32),
            pltpu.VMEM((STEPS + 1, 2, groups, 4 * size_x, depth), f32),
            pltpu.VMEM((STEPS, 2, groups, 4 * size_x, depth), f32),
            pltpu.VMEM((4,) + tile, f32),
            pltpu.VMEM((2, 2) + tile, f32),
            pltpu.VMEM((2,) + tile, f32),
            pltpu.VMEM(tile, f32),
            pltpu.VMEM(tile, f32),
            pltpu.SemaphoreType.DMA((groups,)),
            pltpu.SemaphoreType.DMA((4,)),
            pltpu.SemaphoreType.DMA((4,)),
            pltpu.SemaphoreType.DMA((STEPS, BATCHES, 4)),
            pltpu.SemaphoreType.DMA,
            pltpu.SemaphoreType.DMA,
            pltpu.SemaphoreType.REGULAR,
        ],
        compiler_params=pltpu.CompilerParams(
            collective_id=0, has_side_effects=True, vmem_limit_bytes=60 * 1024 * 1024
        ),
    )(state, levels, old_flux, eco_prey, eco_rate)


def solution(mesh):
    placed = (
        P("half", None, "gx", "gy", None),
        P(None, "gx", "gy"),
        P(None, "gx", "gy", None),
        P(),
        P(),
    )
    return jax.shard_map(
        body,
        mesh=mesh,
        in_specs=placed,
        out_specs=P("half", None, "gx", "gy", None),
        check_vma=False,
    )
```

```python
import jax
import jax.numpy as jnp
from jax import lax
from jax.experimental import pallas as pl
from jax.experimental.pallas import tpu as pltpu
from jax.sharding import PartitionSpec as P

NSUB = 4
STEPS = NSUB + 1
DT = 0.1
NU = 1.0
CORIOLIS = 0.5
DRAG = 0.1
MORTALITY = 0.1
HEATING = 2.0
SURFACE = 8.0
MESH = pl.DeviceIdType.MESH
WEST, EAST, SOUTH, NORTH = 0, 1, 2, 3


def kernel(
    state_hbm, levels_hbm, flux_hbm, prey_hbm, rate_hbm, out_ref,
    levels_ref, prey_ref, rate_ref, raw, cur, tanhs, hx, ys, yr, wet, flux, run, light, heat,
    load_sem, small_sem, send_sem, recv_sem, pair_send, pair_recv, ready_sem,
):
    groups = cur.shape[1]
    size_x, size_y, depth = cur.shape[3:]
    last_x, last_y = size_x - 1, size_y - 1
    species = prey_ref.shape[0]
    half = lax.axis_index("half")
    gx, gy = lax.axis_index("gx"), lax.axis_index("gy")
    nx, ny = lax.axis_size("gx"), lax.axis_size("gy")
    is_ocean = half == 0
    has = (gx > 0, gx < nx - 1, gy > 0, gy < ny - 1)
    peer = ((half, gx - 1, gy), (half, gx + 1, gy), (half, gx, gy - 1), (half, gx, gy + 1))
    partner = (1 - half, gx, gy)
    even = lax.rem(gy, 2) == 0

    def load(g):
        return pltpu.make_async_copy(state_hbm.at[0, pl.ds(4 * g, 4)], raw.at[g], load_sem.at[g])

    levels_load = pltpu.make_async_copy(levels_hbm, levels_ref, small_sem.at[0])
    flux_load = pltpu.make_async_copy(flux_hbm, flux.at[0], small_sem.at[1])
    prey_load = pltpu.make_async_copy(prey_hbm, prey_ref, small_sem.at[2])
    rate_load = pltpu.make_async_copy(rate_hbm, rate_ref, small_sem.at[3])
    levels_load.start()
    for g in range(groups):
        load(g).start()
    flux_load.start()
    prey_load.start()
    rate_load.start()

    barrier = pltpu.get_barrier_semaphore()
    for side in range(4):
        @pl.when(has[side])
        def _():
            pl.semaphore_signal(barrier, inc=1, device_id=peer[side], device_id_type=MESH)

    @pl.when(jnp.logical_not(is_ocean))
    def _():
        pl.semaphore_signal(barrier, inc=1, device_id=partner, device_id_type=MESH)

    for side in (WEST, EAST):
        @pl.when(jnp.logical_not(has[side]))
        def _():
            for s in range(STEPS):
                hx[s, side] = jnp.zeros(hx.shape[2:], jnp.float32)
    for side in (SOUTH, NORTH):
        @pl.when(jnp.logical_not(has[side]))
        def _():
            for s in range(STEPS):
                yr[s, side - 2] = jnp.zeros(yr.shape[2:], jnp.float32)

    rows = lax.broadcasted_iota(jnp.int32, (size_y, depth), 0)
    level_k = lax.broadcasted_iota(jnp.int32, (size_y, depth), 1).astype(jnp.float32)
    diagonal = lax.broadcasted_iota(jnp.int32, (size_y, size_y), 0) == lax.broadcasted_iota(
        jnp.int32, (size_y, size_y), 1
    )
    levels_load.wait()
    for i in range(size_x):
        active = []
        for c in range(4):
            line = levels_ref[c, pl.ds(i, 1), :].astype(jnp.float32)
            spread = jnp.where(diagonal, jnp.broadcast_to(line, (size_y, size_y)), 0.0)
            active.append(jnp.sum(spread, axis=1, keepdims=True))
        most = jnp.maximum(jnp.maximum(active[0], active[1]), jnp.maximum(active[2], active[3]))
        for c in range(4):
            mine = jnp.where(is_ocean, active[c], most)
            wet[c, i] = jnp.where(level_k < mine, 1.0, 0.0)

    run[...] = jnp.zeros(run.shape, jnp.float32)
    heat[...] = jnp.zeros(heat.shape, jnp.float32)

    def copy_of(s, g, side, ocean):
        if side < 2:
            row = 0 if side == WEST else last_x
            if ocean:
                channels = pl.ds(0, 2) if side == WEST else pl.ds(2, 2)
                src = cur.at[s, g, channels, row]
                dst = hx.at[s, 1 - side, g, pl.ds(0, 2)]
            else:
                src = cur.at[s, g, :, row]
                dst = hx.at[s, 1 - side, g]
        else:
            src = ys.at[s, side - 2, g]
            dst = yr.at[s, 3 - side, g]
        lands = 1 - side if side < 2 else 5 - side
        return pltpu.make_async_remote_copy(
            src, dst, send_sem.at[side], recv_sem.at[s, g, lands],
            device_id=peer[side], device_id_type=MESH,
        )

    def start_copies(s, g, ocean):
        for side, turn in (
            (SOUTH, None), (NORTH, None), (WEST, even), (EAST, None), (WEST, jnp.logical_not(even)),
        ):
            @pl.when(has[side] if turn is None else jnp.logical_and(has[side], turn))
            def _():
                copy_of(s, g, side, ocean).start()

    def wait_arrivals(s, g, ocean):
        for side in range(4):
            @pl.when(has[side])
            def _():
                if side < 2:
                    lands = hx.at[s, side, g, pl.ds(0, 2)] if ocean else hx.at[s, side, g]
                else:
                    lands = yr.at[s, side - 2, g]
                pltpu.make_async_remote_copy(
                    lands, lands, send_sem.at[side], recv_sem.at[s, g, side],
                    device_id=peer[side], device_id_type=MESH,
                ).wait_recv()

    def wait_sends(ocean):
        for side in range(4):
            @pl.when(has[side])
            def _():
                if side < 2:
                    sent = hx.at[:, side, :, pl.ds(0, 2)] if ocean else hx.at[:, side]
                else:
                    sent = yr.at[:, side - 2]
                pltpu.make_async_remote_copy(
                    sent, sent, send_sem.at[side], recv_sem.at[0, 0, side],
                    device_id=peer[side], device_id_type=MESH,
                ).wait_send()

    tiles = [(c, i) for c in range(4) for i in range(size_x)]

    def put(s, g, values):
        for (c, i), value in zip(tiles, values):
            cur[s, g, c, i] = value
            ys[s, 0, g, pl.ds(c * size_x + i, 1), :] = value[0:1]
            ys[s, 1, g, pl.ds(c * size_x + i, 1), :] = value[last_y:]

    def north_of(value, s, g, c, i):
        arrived = yr[s, 1, g, pl.ds(c * size_x + i, 1), :]
        return jnp.where(rows == last_y, arrived, pltpu.roll(value, size_y - 1, 0))

    def south_of(value, s, g, c, i):
        arrived = yr[s, 0, g, pl.ds(c * size_x + i, 1), :]
        return jnp.where(rows == 0, arrived, pltpu.roll(value, 1, 0))

    def ocean_part():
        def first(g, carry):
            load(g).wait()
            put(0, g, [raw[g, c, i] * wet[c, i] for c, i in tiles])
            start_copies(0, g, True)
            return carry

        lax.fori_loop(0, groups, first, 0)
        flux_load.wait()
        prey_load.wait()
        rate_load.wait()

        def pair_copy():
            return pltpu.make_async_remote_copy(
                run, flux.at[1], pair_send, pair_recv, device_id=partner, device_id_type=MESH
            )

        def step(s, carry):
            def field(f, inner):
                wait_arrivals(s, f, True)
                @pl.when(jnp.logical_and(s == NSUB, f == 2))
                def _():
                    pltpu.make_async_remote_copy(
                        light, light, pair_send, pair_recv,
                        device_id=partner, device_id_type=MESH,
                    ).wait_recv()
                    heat[...] = light[...] * HEATING

                of_u = jnp.where(f == 0, -DRAG, jnp.where(f == 1, -CORIOLIS, 0.0))
                of_v = jnp.where(f == 0, CORIOLIS, jnp.where(f == 1, -DRAG, 0.0))
                of_heat = jnp.where(f == 2, 1.0, 0.0)
                ageing = jnp.where(f == 4, 1.0, 0.0)
                values = []
                for c, i in tiles:
                    a, b = c // 2, c % 2
                    centre = cur[s, f, c, i]
                    if a == 0:
                        to_east = cur[s, f, 2 + b, i]
                        to_west = cur[s, f, 2 + b, i - 1] if i > 0 else hx[s, WEST, f, b]
                    else:
                        to_west = cur[s, f, b, i]
                        to_east = cur[s, f, b, i + 1] if i < last_x else hx[s, EAST, f, b]
                    other = cur[s, f, 2 * a + 1 - b, i]
                    if b == 0:
                        to_north = other
                        to_south = south_of(other, s, f, c + 1, i)
                    else:
                        to_south = other
                        to_north = north_of(other, s, f, c - 1, i)
                    u, v = cur[s, 0, c, i], cur[s, 1, c, i]
                    spread = to_east + to_west + to_north + to_south - 4.0 * centre
                    advect = u * (to_east - to_west) * 0.5 + v * (to_north - to_south) * 0.5
                    forcing = of_u * u + of_v * v + of_heat * heat[i] + ageing
                    values.append(wet[c, i] * (centre + DT * (NU * spread - advect + forcing)))

                put(s + 1, f, values)

                @pl.when(s < NSUB)
                def _():
                    start_copies(s + 1, f, True)

                for (c, i), value in zip(tiles, values):
                    out_ref[0, 4 * f + c, i] = value

                @pl.when(jnp.logical_and(f < 2, s < NSUB))
                def _():
                    for i in range(size_x):
                        total = sum(value for (_, row), value in zip(tiles, values) if row == i)
                        run[f, i] = run[f, i] + total * (0.25 / NSUB)

                @pl.when(jnp.logical_and(s == NSUB - 1, f == 1))
                def _():
                    pair_copy().start()
                return inner
            return lax.fori_loop(0, groups, field, carry)

        lax.fori_loop(0, STEPS, step, 0)
        wait_sends(True)
        pair_copy().wait_send()

    def tracer_part():
        def first(g, carry):
            load(g).wait()
            values = [raw[g, c, i] * wet[c, i] for c, i in tiles]
            put(0, g, values)
            start_copies(0, g, False)
            for (c, i), value in zip(tiles, values):
                tanhs[0, 4 * g + c, i] = jnp.tanh(value)
            return carry

        lax.fori_loop(0, groups, first, 0)
        flux_load.wait()
        prey_load.wait()
        rate_load.wait()

        def pair_copy():
            return pltpu.make_async_remote_copy(
                heat, light, pair_send, pair_recv, device_id=partner, device_id_type=MESH
            )

        def step(s, carry):
            now, later = lax.rem(s, 2), lax.rem(s + 1, 2)
            which = s // NSUB

            @pl.when(s == NSUB)
            def _():
                pltpu.make_async_remote_copy(
                    flux.at[1], flux.at[1], pair_send, pair_recv,
                    device_id=partner, device_id_type=MESH,
                ).wait_recv()

            def group(g, inner):
                wait_arrivals(s, g, False)
                values = []
                for c in range(4):
                    t = 4 * g + c
                    living = jnp.where(t < species, 1.0, 0.0)
                    slot = jnp.minimum(t, species - 1)
                    rate = rate_ref[slot] * living
                    mortality = MORTALITY * living
                    prey = prey_ref[slot]
                    for i in range(size_x):
                        centre = cur[s, g, c, i]
                        to_west = cur[s, g, c, i - 1] if i > 0 else hx[s, WEST, g, c]
                        to_east = cur[s, g, c, i + 1] if i < last_x else hx[s, EAST, g, c]
                        to_north = north_of(centre, s, g, c, i)
                        to_south = south_of(centre, s, g, c, i)
                        spread = to_east + to_west + to_north + to_south - 4.0 * centre
                        advect = (
                            flux[which, 0, i] * (to_east - to_west) * 0.5
                            + flux[which, 1, i] * (to_north - to_south) * 0.5
                        )
                        reaction = rate * centre * tanhs[now, prey, i] - mortality * centre
                        values.append(
                            wet[c, i] * (centre + DT * (NU * spread - advect + reaction))
                        )
                put(s + 1, g, values)

                @pl.when(s < NSUB)
                def _():
                    start_copies(s + 1, g, False)

                for (c, i), value in zip(tiles, values):
                    out_ref[0, 4 * g + c, i] = value
                    tanhs[later, 4 * g + c, i] = jnp.tanh(value)

                @pl.when(jnp.logical_and(s == NSUB - 1, g == 0))
                def _():
                    above = (
                        lax.broadcasted_iota(jnp.int32, (depth, depth), 0)
                        < lax.broadcasted_iota(jnp.int32, (depth, depth), 1)
                    ).astype(jnp.float32)
                    for i in range(size_x):
                        green = cur[s + 1, 0, 0, i]
                        soft = jnp.maximum(green, 0.0) + jnp.log(1.0 + jnp.exp(-jnp.abs(green)))
                        attenuation = wet[0, i] * (0.03 + 0.05 * soft)
                        overhead = jnp.dot(
                            attenuation, above, precision=lax.Precision.HIGHEST,
                            preferred_element_type=jnp.float32,
                        )
                        heat[i] = SURFACE * jnp.exp(-overhead) * (1.0 - jnp.exp(-attenuation))
                    pl.semaphore_wait(ready_sem, 1)
                    pair_copy().start()
                return inner
            return lax.fori_loop(0, groups, group, carry)

        lax.fori_loop(0, STEPS, step, 0)
        wait_sends(False)
        pair_copy().wait_send()

    greeted = is_ocean.astype(jnp.int32)
    for side in range(4):
        greeted = greeted + has[side].astype(jnp.int32)
    pl.semaphore_wait(barrier, greeted)

    @pl.when(is_ocean)
    def _():
        pl.semaphore_signal(ready_sem, inc=1, device_id=partner, device_id_type=MESH)

    pl.when(is_ocean)(ocean_part)
    pl.when(jnp.logical_not(is_ocean))(tracer_part)


def body(state, levels, old_flux, eco_prey, eco_rate):
    channels, size_x, size_y, depth = state.shape[1:]
    groups = channels // 4
    f32 = jnp.float32
    tile = (size_x, size_y, depth)
    return pl.pallas_call(
        kernel,
        out_shape=pltpu.VMEM(state.shape, f32),
        in_specs=[pl.BlockSpec(memory_space=pltpu.HBM)] * 5,
        out_specs=pl.BlockSpec(memory_space=pltpu.VMEM),
        scratch_shapes=[
            pltpu.VMEM(levels.shape, levels.dtype),
            pltpu.SMEM(eco_prey.shape, eco_prey.dtype),
            pltpu.SMEM(eco_rate.shape, eco_rate.dtype),
            pltpu.VMEM((groups, 4) + tile, f32),
            pltpu.VMEM((STEPS + 1, groups, 4) + tile, f32),
            pltpu.VMEM((2, channels) + tile, f32),
            pltpu.VMEM((STEPS, 2, groups, 4, size_y, depth), f32),
            pltpu.VMEM((STEPS + 1, 2, groups, 4 * size_x, depth), f32),
            pltpu.VMEM((STEPS, 2, groups, 4 * size_x, depth), f32),
            pltpu.VMEM((4,) + tile, f32),
            pltpu.VMEM((2, 2) + tile, f32),
            pltpu.VMEM((2,) + tile, f32),
            pltpu.VMEM(tile, f32),
            pltpu.VMEM(tile, f32),
            pltpu.SemaphoreType.DMA((groups,)),
            pltpu.SemaphoreType.DMA((4,)),
            pltpu.SemaphoreType.DMA((4,)),
            pltpu.SemaphoreType.DMA((STEPS, groups, 4)),
            pltpu.SemaphoreType.DMA,
            pltpu.SemaphoreType.DMA,
            pltpu.SemaphoreType.REGULAR,
        ],
        compiler_params=pltpu.CompilerParams(
            collective_id=0, has_side_effects=True, vmem_limit_bytes=60 * 1024 * 1024
        ),
    )(state, levels, old_flux, eco_prey, eco_rate)


def solution(mesh):
    placed = (
        P("half", None, "gx", "gy", None),
        P(None, "gx", "gy"),
        P(None, "gx", "gy", None),
        P(),
        P(),
    )
    return jax.shard_map(
        body,
        mesh=mesh,
        in_specs=placed,
        out_specs=P("half", None, "gx", "gy", None),
        check_vma=False,
    )
```

```python
import jax
import jax.numpy as jnp
from jax import lax
from jax.experimental import pallas as pl
from jax.experimental.pallas import tpu as pltpu
from jax.sharding import PartitionSpec as P

NSUB = 4
STEPS = NSUB + 1
DT = 0.1
NU = 1.0
CORIOLIS = 0.5
DRAG = 0.1
MORTALITY = 0.1
HEATING = 2.0
SURFACE = 8.0
MESH = pl.DeviceIdType.MESH
WEST, EAST, SOUTH, NORTH = 0, 1, 2, 3


def kernel(
    state_hbm, levels_hbm, flux_hbm, prey_hbm, rate_hbm, out_ref,
    levels_ref, prey_ref, rate_ref, raw, cur, tanhs, hx, ys, yr, wet, flux, run, light, heat,
    load_sem, small_sem, send_sem, recv_sem, pair_send, pair_recv, ready_sem,
):
    groups = cur.shape[1]
    size_x, size_y, depth = cur.shape[3:]
    last_x, last_y = size_x - 1, size_y - 1
    species = prey_ref.shape[0]
    half = lax.axis_index("half")
    gx, gy = lax.axis_index("gx"), lax.axis_index("gy")
    nx, ny = lax.axis_size("gx"), lax.axis_size("gy")
    is_ocean = half == 0
    has = (gx > 0, gx < nx - 1, gy > 0, gy < ny - 1)
    peer = ((half, gx - 1, gy), (half, gx + 1, gy), (half, gx, gy - 1), (half, gx, gy + 1))
    partner = (1 - half, gx, gy)
    even = lax.rem(gy, 2) == 0

    def load(g):
        return pltpu.make_async_copy(state_hbm.at[0, pl.ds(4 * g, 4)], raw.at[g], load_sem.at[g])

    levels_load = pltpu.make_async_copy(levels_hbm, levels_ref, small_sem.at[0])
    flux_load = pltpu.make_async_copy(flux_hbm, flux.at[0], small_sem.at[1])
    prey_load = pltpu.make_async_copy(prey_hbm, prey_ref, small_sem.at[2])
    rate_load = pltpu.make_async_copy(rate_hbm, rate_ref, small_sem.at[3])
    levels_load.start()
    for g in range(groups):
        load(g).start()
    flux_load.start()
    prey_load.start()
    rate_load.start()

    barrier = pltpu.get_barrier_semaphore()
    for side in range(4):
        @pl.when(has[side])
        def _():
            pl.semaphore_signal(barrier, inc=1, device_id=peer[side], device_id_type=MESH)

    @pl.when(jnp.logical_not(is_ocean))
    def _():
        pl.semaphore_signal(barrier, inc=1, device_id=partner, device_id_type=MESH)

    for side in (WEST, EAST):
        @pl.when(jnp.logical_not(has[side]))
        def _():
            for s in range(STEPS):
                hx[s, side] = jnp.zeros(hx.shape[2:], jnp.float32)
    for side in (SOUTH, NORTH):
        @pl.when(jnp.logical_not(has[side]))
        def _():
            for s in range(STEPS):
                yr[s, side - 2] = jnp.zeros(yr.shape[2:], jnp.float32)

    rows = lax.broadcasted_iota(jnp.int32, (size_y, depth), 0)
    level_k = lax.broadcasted_iota(jnp.int32, (size_y, depth), 1).astype(jnp.float32)
    diagonal = lax.broadcasted_iota(jnp.int32, (size_y, size_y), 0) == lax.broadcasted_iota(
        jnp.int32, (size_y, size_y), 1
    )
    levels_load.wait()
    for i in range(size_x):
        active = []
        for c in range(4):
            line = levels_ref[c, pl.ds(i, 1), :].astype(jnp.float32)
            spread = jnp.where(diagonal, jnp.broadcast_to(line, (size_y, size_y)), 0.0)
            active.append(jnp.sum(spread, axis=1, keepdims=True))
        most = jnp.maximum(jnp.maximum(active[0], active[1]), jnp.maximum(active[2], active[3]))
        for c in range(4):
            mine = jnp.where(is_ocean, active[c], most)
            wet[c, i] = jnp.where(level_k < mine, 1.0, 0.0)

    run[...] = jnp.zeros(run.shape, jnp.float32)
    heat[...] = jnp.zeros(heat.shape, jnp.float32)

    def copy_of(s, g, side, ocean, part=0):
        if side < 2:
            row = 0 if side == WEST else last_x
            if ocean:
                channels = pl.ds(0, 2) if side == WEST else pl.ds(2, 2)
                dst = hx.at[s, 1 - side, g, pl.ds(0, 2)]
            else:
                channels = pl.ds(2 * part, 2)
                dst = hx.at[s, 1 - side, g, channels]
            src = cur.at[s, g, channels, row]
            lands = 2 * part + 1 - side
        else:
            src = ys.at[s, side - 2, g]
            dst = yr.at[s, 3 - side, g]
            lands = 4 + 3 - side
        return pltpu.make_async_remote_copy(
            src, dst, send_sem.at[side], recv_sem.at[s, g, lands],
            device_id=peer[side], device_id_type=MESH,
        )

    def start_y(s, g):
        for side in (SOUTH, NORTH):
            @pl.when(has[side])
            def _():
                copy_of(s, g, side, False).start()

    def start_x(s, g, ocean, part=0):
        for side, turn in ((WEST, even), (EAST, None), (WEST, jnp.logical_not(even))):
            @pl.when(has[side] if turn is None else jnp.logical_and(has[side], turn))
            def _():
                copy_of(s, g, side, ocean, part).start()

    def arrival(lands, s, g, side, n):
        @pl.when(has[side])
        def _():
            pltpu.make_async_remote_copy(
                lands, lands, send_sem.at[side], recv_sem.at[s, g, n],
                device_id=peer[side], device_id_type=MESH,
            ).wait_recv()

    def wait_y(s, g):
        for side in (SOUTH, NORTH):
            arrival(yr.at[s, side - 2, g], s, g, side, 2 + side)

    def wait_x(s, g, part=0):
        for side in (WEST, EAST):
            arrival(hx.at[s, side, g, pl.ds(2 * part, 2)], s, g, side, 2 * part + side)

    def wait_sends(ocean):
        for side in range(4):
            @pl.when(has[side])
            def _():
                if side < 2:
                    sent = hx.at[:, side, :, pl.ds(0, 2)] if ocean else hx.at[:, side]
                else:
                    sent = yr.at[:, side - 2]
                pltpu.make_async_remote_copy(
                    sent, sent, send_sem.at[side], recv_sem.at[0, 0, side],
                    device_id=peer[side], device_id_type=MESH,
                ).wait_send()

    tiles = [(c, i) for c in range(4) for i in range(size_x)]

    parts = [[(c, i) for c, i in tiles if c // 2 == part] for part in range(2)]

    def put(s, g, values, where=tiles):
        for (c, i), value in zip(where, values):
            cur[s, g, c, i] = value
            ys[s, 0, g, pl.ds(c * size_x + i, 1), :] = value[0:1]
            ys[s, 1, g, pl.ds(c * size_x + i, 1), :] = value[last_y:]

    def north_of(value, s, g, c, i):
        arrived = yr[s, 1, g, pl.ds(c * size_x + i, 1), :]
        return jnp.where(rows == last_y, arrived, pltpu.roll(value, size_y - 1, 0))

    def south_of(value, s, g, c, i):
        arrived = yr[s, 0, g, pl.ds(c * size_x + i, 1), :]
        return jnp.where(rows == 0, arrived, pltpu.roll(value, 1, 0))

    def ocean_part():
        def first(g, carry):
            load(g).wait()
            put(0, g, [raw[g, c, i] * wet[c, i] for c, i in tiles])
            start_y(0, g)
            start_x(0, g, True)
            return carry

        lax.fori_loop(0, groups, first, 0)
        flux_load.wait()
        prey_load.wait()
        rate_load.wait()

        def pair_copy():
            return pltpu.make_async_remote_copy(
                run, flux.at[1], pair_send, pair_recv, device_id=partner, device_id_type=MESH
            )

        def step(s, carry):
            def field(f, inner):
                wait_y(s, f)
                wait_x(s, f)
                @pl.when(jnp.logical_and(s == NSUB, f == 2))
                def _():
                    pltpu.make_async_remote_copy(
                        light, light, pair_send, pair_recv,
                        device_id=partner, device_id_type=MESH,
                    ).wait_recv()
                    heat[...] = light[...] * HEATING

                of_u = jnp.where(f == 0, -DRAG, jnp.where(f == 1, -CORIOLIS, 0.0))
                of_v = jnp.where(f == 0, CORIOLIS, jnp.where(f == 1, -DRAG, 0.0))
                of_heat = jnp.where(f == 2, 1.0, 0.0)
                ageing = jnp.where(f == 4, 1.0, 0.0)
                values = []
                for c, i in tiles:
                    a, b = c // 2, c % 2
                    centre = cur[s, f, c, i]
                    if a == 0:
                        to_east = cur[s, f, 2 + b, i]
                        to_west = cur[s, f, 2 + b, i - 1] if i > 0 else hx[s, WEST, f, b]
                    else:
                        to_west = cur[s, f, b, i]
                        to_east = cur[s, f, b, i + 1] if i < last_x else hx[s, EAST, f, b]
                    other = cur[s, f, 2 * a + 1 - b, i]
                    if b == 0:
                        to_north = other
                        to_south = south_of(other, s, f, c + 1, i)
                    else:
                        to_south = other
                        to_north = north_of(other, s, f, c - 1, i)
                    u, v = cur[s, 0, c, i], cur[s, 1, c, i]
                    spread = to_east + to_west + to_north + to_south - 4.0 * centre
                    advect = u * (to_east - to_west) * 0.5 + v * (to_north - to_south) * 0.5
                    forcing = of_u * u + of_v * v + of_heat * heat[i] + ageing
                    values.append(wet[c, i] * (centre + DT * (NU * spread - advect + forcing)))

                put(s + 1, f, values)

                @pl.when(s < NSUB)
                def _():
                    start_y(s + 1, f)
                    start_x(s + 1, f, True)

                for (c, i), value in zip(tiles, values):
                    out_ref[0, 4 * f + c, i] = value

                @pl.when(jnp.logical_and(f < 2, s < NSUB))
                def _():
                    for i in range(size_x):
                        total = sum(value for (_, row), value in zip(tiles, values) if row == i)
                        run[f, i] = run[f, i] + total * (0.25 / NSUB)

                @pl.when(jnp.logical_and(s == NSUB - 1, f == 1))
                def _():
                    pair_copy().start()
                return inner
            return lax.fori_loop(0, groups, field, carry)

        lax.fori_loop(0, STEPS, step, 0)
        wait_sends(True)
        pair_copy().wait_send()

    def tracer_part():
        def first(g, carry):
            load(g).wait()
            for part, where in enumerate(parts):
                values = [raw[g, c, i] * wet[c, i] for c, i in where]
                put(0, g, values, where)
                start_x(0, g, False, part)
                for (c, i), value in zip(where, values):
                    tanhs[0, 4 * g + c, i] = jnp.tanh(value)
            start_y(0, g)
            return carry

        lax.fori_loop(0, groups, first, 0)
        flux_load.wait()
        prey_load.wait()
        rate_load.wait()

        def pair_copy():
            return pltpu.make_async_remote_copy(
                heat, light, pair_send, pair_recv, device_id=partner, device_id_type=MESH
            )

        def step(s, carry):
            now, later = lax.rem(s, 2), lax.rem(s + 1, 2)
            which = s // NSUB

            @pl.when(s == NSUB)
            def _():
                pltpu.make_async_remote_copy(
                    flux.at[1], flux.at[1], pair_send, pair_recv,
                    device_id=partner, device_id_type=MESH,
                ).wait_recv()

            def group(g, inner):
                wait_y(s, g)
                for part, where in enumerate(parts):
                    wait_x(s, g, part)
                    values = []
                    for c, i in where:
                        t = 4 * g + c
                        living = jnp.where(t < species, 1.0, 0.0)
                        slot = jnp.minimum(t, species - 1)
                        rate = rate_ref[slot] * living
                        mortality = MORTALITY * living
                        prey = prey_ref[slot]
                        centre = cur[s, g, c, i]
                        to_west = cur[s, g, c, i - 1] if i > 0 else hx[s, WEST, g, c]
                        to_east = cur[s, g, c, i + 1] if i < last_x else hx[s, EAST, g, c]
                        to_north = north_of(centre, s, g, c, i)
                        to_south = south_of(centre, s, g, c, i)
                        spread = to_east + to_west + to_north + to_south - 4.0 * centre
                        advect = (
                            flux[which, 0, i] * (to_east - to_west) * 0.5
                            + flux[which, 1, i] * (to_north - to_south) * 0.5
                        )
                        reaction = rate * centre * tanhs[now, prey, i] - mortality * centre
                        values.append(
                            wet[c, i] * (centre + DT * (NU * spread - advect + reaction))
                        )
                    put(s + 1, g, values, where)

                    @pl.when(s < NSUB)
                    def _():
                        start_x(s + 1, g, False, part)

                    for (c, i), value in zip(where, values):
                        out_ref[0, 4 * g + c, i] = value
                        tanhs[later, 4 * g + c, i] = jnp.tanh(value)

                @pl.when(s < NSUB)
                def _():
                    start_y(s + 1, g)

                @pl.when(jnp.logical_and(s == NSUB - 1, g == 0))
                def _():
                    above = (
                        lax.broadcasted_iota(jnp.int32, (depth, depth), 0)
                        < lax.broadcasted_iota(jnp.int32, (depth, depth), 1)
                    ).astype(jnp.float32)
                    for i in range(size_x):
                        green = cur[s + 1, 0, 0, i]
                        soft = jnp.maximum(green, 0.0) + jnp.log(1.0 + jnp.exp(-jnp.abs(green)))
                        attenuation = wet[0, i] * (0.03 + 0.05 * soft)
                        overhead = jnp.dot(
                            attenuation, above, precision=lax.Precision.HIGHEST,
                            preferred_element_type=jnp.float32,
                        )
                        heat[i] = SURFACE * jnp.exp(-overhead) * (1.0 - jnp.exp(-attenuation))
                    pl.semaphore_wait(ready_sem, 1)
                    pair_copy().start()
                return inner
            return lax.fori_loop(0, groups, group, carry)

        lax.fori_loop(0, STEPS, step, 0)
        wait_sends(False)
        pair_copy().wait_send()

    greeted = is_ocean.astype(jnp.int32)
    for side in range(4):
        greeted = greeted + has[side].astype(jnp.int32)
    pl.semaphore_wait(barrier, greeted)

    @pl.when(is_ocean)
    def _():
        pl.semaphore_signal(ready_sem, inc=1, device_id=partner, device_id_type=MESH)

    pl.when(is_ocean)(ocean_part)
    pl.when(jnp.logical_not(is_ocean))(tracer_part)


def body(state, levels, old_flux, eco_prey, eco_rate):
    channels, size_x, size_y, depth = state.shape[1:]
    groups = channels // 4
    f32 = jnp.float32
    tile = (size_x, size_y, depth)
    return pl.pallas_call(
        kernel,
        out_shape=pltpu.VMEM(state.shape, f32),
        in_specs=[pl.BlockSpec(memory_space=pltpu.HBM)] * 5,
        out_specs=pl.BlockSpec(memory_space=pltpu.VMEM),
        scratch_shapes=[
            pltpu.VMEM(levels.shape, levels.dtype),
            pltpu.SMEM(eco_prey.shape, eco_prey.dtype),
            pltpu.SMEM(eco_rate.shape, eco_rate.dtype),
            pltpu.VMEM((groups, 4) + tile, f32),
            pltpu.VMEM((STEPS + 1, groups, 4) + tile, f32),
            pltpu.VMEM((2, channels) + tile, f32),
            pltpu.VMEM((STEPS, 2, groups, 4, size_y, depth), f32),
            pltpu.VMEM((STEPS + 1, 2, groups, 4 * size_x, depth), f32),
            pltpu.VMEM((STEPS, 2, groups, 4 * size_x, depth), f32),
            pltpu.VMEM((4,) + tile, f32),
            pltpu.VMEM((2, 2) + tile, f32),
            pltpu.VMEM((2,) + tile, f32),
            pltpu.VMEM(tile, f32),
            pltpu.VMEM(tile, f32),
            pltpu.SemaphoreType.DMA((groups,)),
            pltpu.SemaphoreType.DMA((4,)),
            pltpu.SemaphoreType.DMA((4,)),
            pltpu.SemaphoreType.DMA((STEPS, groups, 6)),
            pltpu.SemaphoreType.DMA,
            pltpu.SemaphoreType.DMA,
            pltpu.SemaphoreType.REGULAR,
        ],
        compiler_params=pltpu.CompilerParams(
            collective_id=0, has_side_effects=True, vmem_limit_bytes=60 * 1024 * 1024
        ),
    )(state, levels, old_flux, eco_prey, eco_rate)


def solution(mesh):
    placed = (
        P("half", None, "gx", "gy", None),
        P(None, "gx", "gy"),
        P(None, "gx", "gy", None),
        P(),
        P(),
    )
    return jax.shard_map(
        body,
        mesh=mesh,
        in_specs=placed,
        out_specs=P("half", None, "gx", "gy", None),
        check_vma=False,
    )
```

```python
import jax
import jax.numpy as jnp
from jax import lax
from jax.experimental import pallas as pl
from jax.experimental.pallas import tpu as pltpu
from jax.sharding import PartitionSpec as P

NSUB = 4
STEPS = NSUB + 1
DT = 0.1
NU = 1.0
CORIOLIS = 0.5
DRAG = 0.1
MORTALITY = 0.1
HEATING = 2.0
SURFACE = 8.0
MESH = pl.DeviceIdType.MESH
WEST, EAST, SOUTH, NORTH = 0, 1, 2, 3


def kernel(
    state_hbm, levels_hbm, flux_hbm, prey_hbm, rate_hbm, out_ref,
    levels_ref, levels_by, halo_wet, prey_ref, rate_ref, raw, cur, tanhs, hx, ys, yr, wet, flux, run, light, heat,
    load_sem, small_sem, send_sem, recv_sem, pair_send, pair_recv, ready_sem, by_send, by_recv,
):
    groups = cur.shape[1]
    size_x, size_y, depth = cur.shape[3:]
    last_x, last_y = size_x - 1, size_y - 1
    species = prey_ref.shape[0]
    half = lax.axis_index("half")
    gx, gy = lax.axis_index("gx"), lax.axis_index("gy")
    nx, ny = lax.axis_size("gx"), lax.axis_size("gy")
    is_ocean = half == 0
    has = (gx > 0, gx < nx - 1, gy > 0, gy < ny - 1)
    peer = ((half, gx - 1, gy), (half, gx + 1, gy), (half, gx, gy - 1), (half, gx, gy + 1))
    partner = (1 - half, gx, gy)
    even = lax.rem(gy, 2) == 0

    def load(g):
        return pltpu.make_async_copy(state_hbm.at[0, pl.ds(4 * g, 4)], raw.at[g], load_sem.at[g])

    levels_load = pltpu.make_async_copy(levels_hbm, levels_ref, small_sem.at[0])
    flux_load = pltpu.make_async_copy(flux_hbm, flux.at[0], small_sem.at[1])
    prey_load = pltpu.make_async_copy(prey_hbm, prey_ref, small_sem.at[2])
    rate_load = pltpu.make_async_copy(rate_hbm, rate_ref, small_sem.at[3])
    levels_load.start()
    for g in range(groups):
        load(g).start()
    flux_load.start()
    prey_load.start()
    rate_load.start()

    barrier = pltpu.get_barrier_semaphore()
    for side in range(4):
        @pl.when(has[side])
        def _():
            pl.semaphore_signal(barrier, inc=1, device_id=peer[side], device_id_type=MESH)

    @pl.when(jnp.logical_not(is_ocean))
    def _():
        pl.semaphore_signal(barrier, inc=1, device_id=partner, device_id_type=MESH)

    for side in (WEST, EAST):
        @pl.when(jnp.logical_not(has[side]))
        def _():
            for s in range(STEPS):
                hx[s, side] = jnp.zeros(hx.shape[2:], jnp.float32)
    for side in (SOUTH, NORTH):
        @pl.when(jnp.logical_not(has[side]))
        def _():
            for s in range(STEPS):
                yr[s, side - 2] = jnp.zeros(yr.shape[2:], jnp.float32)

    rows = lax.broadcasted_iota(jnp.int32, (size_y, depth), 0)
    level_k = lax.broadcasted_iota(jnp.int32, (size_y, depth), 1).astype(jnp.float32)
    diagonal = lax.broadcasted_iota(jnp.int32, (size_y, size_y), 0) == lax.broadcasted_iota(
        jnp.int32, (size_y, size_y), 1
    )
    run[...] = jnp.zeros(run.shape, jnp.float32)
    heat[...] = jnp.zeros(heat.shape, jnp.float32)

    def masks_of(line_of):
        active = []
        for c in range(4):
            line = line_of(c).astype(jnp.float32)
            spread = jnp.where(diagonal, jnp.broadcast_to(line, (size_y, size_y)), 0.0)
            active.append(jnp.sum(spread, axis=1, keepdims=True))
        most = jnp.maximum(jnp.maximum(active[0], active[1]), jnp.maximum(active[2], active[3]))
        mine = [jnp.where(is_ocean, own, most) for own in active]
        return [jnp.where(level_k < own, 1.0, 0.0) for own in mine]

    def levels_copy(side):
        return pltpu.make_async_remote_copy(
            levels_hbm, levels_by.at[1 - side], by_send.at[side], by_recv.at[1 - side],
            device_id=peer[side], device_id_type=MESH,
        )

    def own_masks():
        levels_load.wait()
        for i in range(size_x):
            for c, mask in enumerate(masks_of(lambda c: levels_ref[c, pl.ds(i, 1), :])):
                wet[c, i] = mask

    def halo_masks():
        for side in (WEST, EAST):
            halo_wet[1, side] = jnp.ones(halo_wet.shape[2:], jnp.float32)

            @pl.when(has[side])
            def _():
                pltpu.make_async_remote_copy(
                    levels_by.at[side], levels_by.at[side], by_send.at[side], by_recv.at[side],
                    device_id=peer[side], device_id_type=MESH,
                ).wait_recv()
                row = last_x if side == WEST else 0
                masks = masks_of(lambda c: levels_by[side, c, pl.ds(row, 1), :])
                for c in range(4):
                    halo_wet[0, side, c] = masks[(c + 2) % 4 if side == WEST else c]

            @pl.when(jnp.logical_not(has[side]))
            def _():
                halo_wet[0, side] = jnp.zeros(halo_wet.shape[2:], jnp.float32)

    def copy_of(s, g, side, ocean, first=False):
        if side < 2:
            row = 0 if side == WEST else last_x
            if ocean:
                channels = pl.ds(0, 2) if side == WEST else pl.ds(2, 2)
                src = cur.at[s, g, channels, row]
                if first:
                    src = state_hbm.at[0, pl.ds(4 * g + (0 if side == WEST else 2), 2), row]
                dst = hx.at[s, 1 - side, g, pl.ds(0, 2)]
            else:
                src = cur.at[s, g, :, row]
                if first:
                    src = state_hbm.at[0, pl.ds(4 * g, 4), row]
                dst = hx.at[s, 1 - side, g]
        else:
            src = ys.at[s, side - 2, g]
            dst = yr.at[s, 3 - side, g]
        lands = 1 - side if side < 2 else 5 - side
        return pltpu.make_async_remote_copy(
            src, dst, send_sem.at[side], recv_sem.at[s, g, lands],
            device_id=peer[side], device_id_type=MESH,
        )

    def start_y(s, g):
        for side in (SOUTH, NORTH):
            @pl.when(has[side])
            def _():
                copy_of(s, g, side, False).start()

    def start_x(s, g, ocean, first=False):
        for side, turn in ((WEST, even), (EAST, None), (WEST, jnp.logical_not(even))):
            @pl.when(has[side] if turn is None else jnp.logical_and(has[side], turn))
            def _():
                copy_of(s, g, side, ocean, first).start()

    def start_copies(s, g, ocean):
        start_y(s, g)
        start_x(s, g, ocean)

    def start_first(ocean):
        for side in (WEST, EAST):
            @pl.when(has[side])
            def _():
                levels_copy(side).start()

        def group(g, carry):
            start_x(0, g, ocean, True)
            return carry

        lax.fori_loop(0, groups, group, 0)

    def wait_arrivals(s, g, ocean):
        for side in range(4):
            @pl.when(has[side])
            def _():
                if side < 2:
                    lands = hx.at[s, side, g, pl.ds(0, 2)] if ocean else hx.at[s, side, g]
                else:
                    lands = yr.at[s, side - 2, g]
                pltpu.make_async_remote_copy(
                    lands, lands, send_sem.at[side], recv_sem.at[s, g, side],
                    device_id=peer[side], device_id_type=MESH,
                ).wait_recv()

    def wait_sends(ocean):
        for side in range(4):
            @pl.when(has[side])
            def _():
                if side < 2:
                    levels_copy(side).wait_send()
                    sent = hx.at[:, side, :, pl.ds(0, 2)] if ocean else hx.at[:, side]
                else:
                    sent = yr.at[:, side - 2]
                pltpu.make_async_remote_copy(
                    sent, sent, send_sem.at[side], recv_sem.at[0, 0, side],
                    device_id=peer[side], device_id_type=MESH,
                ).wait_send()

    tiles = [(c, i) for c in range(4) for i in range(size_x)]

    def put(s, g, values):
        for (c, i), value in zip(tiles, values):
            cur[s, g, c, i] = value
            ys[s, 0, g, pl.ds(c * size_x + i, 1), :] = value[0:1]
            ys[s, 1, g, pl.ds(c * size_x + i, 1), :] = value[last_y:]

    def north_of(value, s, g, c, i):
        arrived = yr[s, 1, g, pl.ds(c * size_x + i, 1), :]
        return jnp.where(rows == last_y, arrived, pltpu.roll(value, size_y - 1, 0))

    def south_of(value, s, g, c, i):
        arrived = yr[s, 0, g, pl.ds(c * size_x + i, 1), :]
        return jnp.where(rows == 0, arrived, pltpu.roll(value, 1, 0))

    def beyond(s, side, g, c):
        return hx[s, side, g, c] * halo_wet[jnp.minimum(s, 1), side, c]

    def ocean_part():
        start_first(True)
        own_masks()

        def first(g, carry):
            load(g).wait()
            put(0, g, [raw[g, c, i] * wet[c, i] for c, i in tiles])
            start_y(0, g)
            return carry

        lax.fori_loop(0, groups, first, 0)
        flux_load.wait()
        prey_load.wait()
        rate_load.wait()
        halo_masks()

        def pair_copy():
            return pltpu.make_async_remote_copy(
                run, flux.at[1], pair_send, pair_recv, device_id=partner, device_id_type=MESH
            )

        def step(s, carry):
            def field(f, inner):
                wait_arrivals(s, f, True)
                @pl.when(jnp.logical_and(s == NSUB, f == 2))
                def _():
                    pltpu.make_async_remote_copy(
                        light, light, pair_send, pair_recv,
                        device_id=partner, device_id_type=MESH,
                    ).wait_recv()
                    heat[...] = light[...] * HEATING

                of_u = jnp.where(f == 0, -DRAG, jnp.where(f == 1, -CORIOLIS, 0.0))
                of_v = jnp.where(f == 0, CORIOLIS, jnp.where(f == 1, -DRAG, 0.0))
                of_heat = jnp.where(f == 2, 1.0, 0.0)
                ageing = jnp.where(f == 4, 1.0, 0.0)
                values = []
                for c, i in tiles:
                    a, b = c // 2, c % 2
                    centre = cur[s, f, c, i]
                    if a == 0:
                        to_east = cur[s, f, 2 + b, i]
                        to_west = cur[s, f, 2 + b, i - 1] if i > 0 else beyond(s, WEST, f, b)
                    else:
                        to_west = cur[s, f, b, i]
                        to_east = cur[s, f, b, i + 1] if i < last_x else beyond(s, EAST, f, b)
                    other = cur[s, f, 2 * a + 1 - b, i]
                    if b == 0:
                        to_north = other
                        to_south = south_of(other, s, f, c + 1, i)
                    else:
                        to_south = other
                        to_north = north_of(other, s, f, c - 1, i)
                    u, v = cur[s, 0, c, i], cur[s, 1, c, i]
                    spread = to_east + to_west + to_north + to_south - 4.0 * centre
                    advect = u * (to_east - to_west) * 0.5 + v * (to_north - to_south) * 0.5
                    forcing = of_u * u + of_v * v + of_heat * heat[i] + ageing
                    values.append(wet[c, i] * (centre + DT * (NU * spread - advect + forcing)))

                put(s + 1, f, values)

                @pl.when(s < NSUB)
                def _():
                    start_copies(s + 1, f, True)

                for (c, i), value in zip(tiles, values):
                    out_ref[0, 4 * f + c, i] = value

                @pl.when(jnp.logical_and(f < 2, s < NSUB))
                def _():
                    for i in range(size_x):
                        total = sum(value for (_, row), value in zip(tiles, values) if row == i)
                        run[f, i] = run[f, i] + total * (0.25 / NSUB)

                @pl.when(jnp.logical_and(s == NSUB - 1, f == 1))
                def _():
                    pair_copy().start()
                return inner
            return lax.fori_loop(0, groups, field, carry)

        lax.fori_loop(0, STEPS, step, 0)
        wait_sends(True)
        pair_copy().wait_send()

    def tracer_part():
        start_first(False)
        own_masks()

        def first(g, carry):
            load(g).wait()
            values = [raw[g, c, i] * wet[c, i] for c, i in tiles]
            put(0, g, values)
            start_y(0, g)
            for (c, i), value in zip(tiles, values):
                tanhs[0, 4 * g + c, i] = jnp.tanh(value)
            return carry

        lax.fori_loop(0, groups, first, 0)
        flux_load.wait()
        prey_load.wait()
        rate_load.wait()
        halo_masks()

        def pair_copy():
            return pltpu.make_async_remote_copy(
                heat, light, pair_send, pair_recv, device_id=partner, device_id_type=MESH
            )

        def step(s, carry):
            now, later = lax.rem(s, 2), lax.rem(s + 1, 2)
            which = s // NSUB

            @pl.when(s == NSUB)
            def _():
                pltpu.make_async_remote_copy(
                    flux.at[1], flux.at[1], pair_send, pair_recv,
                    device_id=partner, device_id_type=MESH,
                ).wait_recv()

            def group(g, inner):
                wait_arrivals(s, g, False)
                values = []
                for c in range(4):
                    t = 4 * g + c
                    living = jnp.where(t < species, 1.0, 0.0)
                    slot = jnp.minimum(t, species - 1)
                    rate = rate_ref[slot] * living
                    mortality = MORTALITY * living
                    prey = prey_ref[slot]
                    for i in range(size_x):
                        centre = cur[s, g, c, i]
                        to_west = cur[s, g, c, i - 1] if i > 0 else beyond(s, WEST, g, c)
                        to_east = cur[s, g, c, i + 1] if i < last_x else beyond(s, EAST, g, c)
                        to_north = north_of(centre, s, g, c, i)
                        to_south = south_of(centre, s, g, c, i)
                        spread = to_east + to_west + to_north + to_south - 4.0 * centre
                        advect = (
                            flux[which, 0, i] * (to_east - to_west) * 0.5
                            + flux[which, 1, i] * (to_north - to_south) * 0.5
                        )
                        reaction = rate * centre * tanhs[now, prey, i] - mortality * centre
                        values.append(
                            wet[c, i] * (centre + DT * (NU * spread - advect + reaction))
                        )
                put(s + 1, g, values)

                @pl.when(s < NSUB)
                def _():
                    start_copies(s + 1, g, False)

                for (c, i), value in zip(tiles, values):
                    out_ref[0, 4 * g + c, i] = value
                    tanhs[later, 4 * g + c, i] = jnp.tanh(value)

                @pl.when(jnp.logical_and(s == NSUB - 1, g == 0))
                def _():
                    above = (
                        lax.broadcasted_iota(jnp.int32, (depth, depth), 0)
                        < lax.broadcasted_iota(jnp.int32, (depth, depth), 1)
                    ).astype(jnp.float32)
                    for i in range(size_x):
                        green = cur[s + 1, 0, 0, i]
                        soft = jnp.maximum(green, 0.0) + jnp.log(1.0 + jnp.exp(-jnp.abs(green)))
                        attenuation = wet[0, i] * (0.03 + 0.05 * soft)
                        overhead = jnp.dot(
                            attenuation, above, precision=lax.Precision.HIGHEST,
                            preferred_element_type=jnp.float32,
                        )
                        heat[i] = SURFACE * jnp.exp(-overhead) * (1.0 - jnp.exp(-attenuation))
                    pl.semaphore_wait(ready_sem, 1)
                    pair_copy().start()
                return inner
            return lax.fori_loop(0, groups, group, carry)

        lax.fori_loop(0, STEPS, step, 0)
        wait_sends(False)
        pair_copy().wait_send()

    greeted = is_ocean.astype(jnp.int32)
    for side in range(4):
        greeted = greeted + has[side].astype(jnp.int32)
    pl.semaphore_wait(barrier, greeted)

    @pl.when(is_ocean)
    def _():
        pl.semaphore_signal(ready_sem, inc=1, device_id=partner, device_id_type=MESH)

    pl.when(is_ocean)(ocean_part)
    pl.when(jnp.logical_not(is_ocean))(tracer_part)


def body(state, levels, old_flux, eco_prey, eco_rate):
    channels, size_x, size_y, depth = state.shape[1:]
    groups = channels // 4
    f32 = jnp.float32
    tile = (size_x, size_y, depth)
    return pl.pallas_call(
        kernel,
        out_shape=pltpu.VMEM(state.shape, f32),
        in_specs=[pl.BlockSpec(memory_space=pltpu.HBM)] * 5,
        out_specs=pl.BlockSpec(memory_space=pltpu.VMEM),
        scratch_shapes=[
            pltpu.VMEM(levels.shape, levels.dtype),
            pltpu.VMEM((2,) + levels.shape, levels.dtype),
            pltpu.VMEM((2, 2, 4, size_y, depth), f32),
            pltpu.SMEM(eco_prey.shape, eco_prey.dtype),
            pltpu.SMEM(eco_rate.shape, eco_rate.dtype),
            pltpu.VMEM((groups, 4) + tile, f32),
            pltpu.VMEM((STEPS + 1, groups, 4) + tile, f32),
            pltpu.VMEM((2, channels) + tile, f32),
            pltpu.VMEM((STEPS, 2, groups, 4, size_y, depth), f32),
            pltpu.VMEM((STEPS + 1, 2, groups, 4 * size_x, depth), f32),
            pltpu.VMEM((STEPS, 2, groups, 4 * size_x, depth), f32),
            pltpu.VMEM((4,) + tile, f32),
            pltpu.VMEM((2, 2) + tile, f32),
            pltpu.VMEM((2,) + tile, f32),
            pltpu.VMEM(tile, f32),
            pltpu.VMEM(tile, f32),
            pltpu.SemaphoreType.DMA((groups,)),
            pltpu.SemaphoreType.DMA((4,)),
            pltpu.SemaphoreType.DMA((4,)),
            pltpu.SemaphoreType.DMA((STEPS, groups, 4)),
            pltpu.SemaphoreType.DMA,
            pltpu.SemaphoreType.DMA,
            pltpu.SemaphoreType.REGULAR,
            pltpu.SemaphoreType.DMA((2,)),
            pltpu.SemaphoreType.DMA((2,)),
        ],
        compiler_params=pltpu.CompilerParams(
            collective_id=0, has_side_effects=True, vmem_limit_bytes=60 * 1024 * 1024
        ),
    )(state, levels, old_flux, eco_prey, eco_rate)


def solution(mesh):
    placed = (
        P("half", None, "gx", "gy", None),
        P(None, "gx", "gy"),
        P(None, "gx", "gy", None),
        P(),
        P(),
    )
    return jax.shard_map(
        body,
        mesh=mesh,
        in_specs=placed,
        out_specs=P("half", None, "gx", "gy", None),
        check_vma=False,
    )
```

```python
import jax
import jax.numpy as jnp
from jax import lax
from jax.experimental import pallas as pl
from jax.experimental.pallas import tpu as pltpu
from jax.sharding import PartitionSpec as P

NSUB = 4
STEPS = NSUB + 1
DT = 0.1
NU = 1.0
CORIOLIS = 0.5
DRAG = 0.1
MORTALITY = 0.1
HEATING = 2.0
SURFACE = 8.0
AHEAD = 2
MESH = pl.DeviceIdType.MESH
WEST, EAST, SOUTH, NORTH = 0, 1, 2, 3


def kernel(
    state_hbm, levels_hbm, flux_hbm, prey_hbm, rate_hbm, out_ref,
    levels_ref, levels_by, halo_wet, prey_ref, rate_ref, raw, cur, tanhs, hx, ys, yr, wet, flux, run, light, heat,
    load_sem, small_sem, send_sem, recv_sem, pair_send, pair_recv, ready_sem, by_send, by_recv,
):
    groups = cur.shape[1]
    size_x, size_y, depth = cur.shape[3:]
    last_x, last_y = size_x - 1, size_y - 1
    species = prey_ref.shape[0]
    half = lax.axis_index("half")
    gx, gy = lax.axis_index("gx"), lax.axis_index("gy")
    nx, ny = lax.axis_size("gx"), lax.axis_size("gy")
    is_ocean = half == 0
    has = (gx > 0, gx < nx - 1, gy > 0, gy < ny - 1)
    peer = ((half, gx - 1, gy), (half, gx + 1, gy), (half, gx, gy - 1), (half, gx, gy + 1))
    partner = (1 - half, gx, gy)
    even = lax.rem(gy, 2) == 0

    def load(g):
        return pltpu.make_async_copy(state_hbm.at[0, pl.ds(4 * g, 4)], raw.at[g], load_sem.at[g])

    levels_load = pltpu.make_async_copy(levels_hbm, levels_ref, small_sem.at[0])
    flux_load = pltpu.make_async_copy(flux_hbm, flux.at[0], small_sem.at[1])
    prey_load = pltpu.make_async_copy(prey_hbm, prey_ref, small_sem.at[2])
    rate_load = pltpu.make_async_copy(rate_hbm, rate_ref, small_sem.at[3])
    levels_load.start()
    for g in range(groups):
        load(g).start()
    flux_load.start()
    prey_load.start()
    rate_load.start()

    barrier = pltpu.get_barrier_semaphore()
    for side in range(4):
        @pl.when(has[side])
        def _():
            pl.semaphore_signal(barrier, inc=1, device_id=peer[side], device_id_type=MESH)

    @pl.when(jnp.logical_not(is_ocean))
    def _():
        pl.semaphore_signal(barrier, inc=1, device_id=partner, device_id_type=MESH)

    for side in (WEST, EAST):
        @pl.when(jnp.logical_not(has[side]))
        def _():
            for s in range(STEPS):
                hx[s, side] = jnp.zeros(hx.shape[2:], jnp.float32)
    for side in (SOUTH, NORTH):
        @pl.when(jnp.logical_not(has[side]))
        def _():
            for s in range(STEPS):
                yr[s, side - 2] = jnp.zeros(yr.shape[2:], jnp.float32)

    rows = lax.broadcasted_iota(jnp.int32, (size_y, depth), 0)
    level_k = lax.broadcasted_iota(jnp.int32, (size_y, depth), 1).astype(jnp.float32)
    diagonal = lax.broadcasted_iota(jnp.int32, (size_y, size_y), 0) == lax.broadcasted_iota(
        jnp.int32, (size_y, size_y), 1
    )
    run[...] = jnp.zeros(run.shape, jnp.float32)
    heat[...] = jnp.zeros(heat.shape, jnp.float32)

    def masks_of(line_of):
        active = []
        for c in range(4):
            line = line_of(c).astype(jnp.float32)
            spread = jnp.where(diagonal, jnp.broadcast_to(line, (size_y, size_y)), 0.0)
            active.append(jnp.sum(spread, axis=1, keepdims=True))
        most = jnp.maximum(jnp.maximum(active[0], active[1]), jnp.maximum(active[2], active[3]))
        mine = [jnp.where(is_ocean, own, most) for own in active]
        return [jnp.where(level_k < own, 1.0, 0.0) for own in mine]

    def levels_copy(side):
        return pltpu.make_async_remote_copy(
            levels_hbm, levels_by.at[1 - side], by_send.at[side], by_recv.at[1 - side],
            device_id=peer[side], device_id_type=MESH,
        )

    def own_masks():
        levels_load.wait()
        for i in range(size_x):
            for c, mask in enumerate(masks_of(lambda c: levels_ref[c, pl.ds(i, 1), :])):
                wet[c, i] = mask

    def halo_masks():
        for side in (WEST, EAST):
            halo_wet[1, side] = jnp.ones(halo_wet.shape[2:], jnp.float32)

            @pl.when(has[side])
            def _():
                pltpu.make_async_remote_copy(
                    levels_by.at[side], levels_by.at[side], by_send.at[side], by_recv.at[side],
                    device_id=peer[side], device_id_type=MESH,
                ).wait_recv()
                row = last_x if side == WEST else 0
                masks = masks_of(lambda c: levels_by[side, c, pl.ds(row, 1), :])
                for c in range(4):
                    halo_wet[0, side, c] = masks[(c + 2) % 4 if side == WEST else c]

            @pl.when(jnp.logical_not(has[side]))
            def _():
                halo_wet[0, side] = jnp.zeros(halo_wet.shape[2:], jnp.float32)

    def copy_of(s, g, side, ocean, first=False):
        if side < 2:
            row = 0 if side == WEST else last_x
            if ocean:
                channels = pl.ds(0, 2) if side == WEST else pl.ds(2, 2)
                src = cur.at[s, g, channels, row]
                if first:
                    src = state_hbm.at[0, pl.ds(4 * g + (0 if side == WEST else 2), 2), row]
                dst = hx.at[s, 1 - side, g, pl.ds(0, 2)]
            else:
                src = cur.at[s, g, :, row]
                if first:
                    src = state_hbm.at[0, pl.ds(4 * g, 4), row]
                dst = hx.at[s, 1 - side, g]
        else:
            src = ys.at[s, side - 2, g]
            dst = yr.at[s, 3 - side, g]
        lands = 1 - side if side < 2 else 5 - side
        return pltpu.make_async_remote_copy(
            src, dst, send_sem.at[side], recv_sem.at[s, g, lands],
            device_id=peer[side], device_id_type=MESH,
        )

    def start_y(s, g):
        for side in (SOUTH, NORTH):
            @pl.when(has[side])
            def _():
                copy_of(s, g, side, False).start()

    def start_x(s, g, ocean, first=False):
        for side, turn in ((WEST, even), (EAST, None), (WEST, jnp.logical_not(even))):
            @pl.when(has[side] if turn is None else jnp.logical_and(has[side], turn))
            def _():
                copy_of(s, g, side, ocean, first).start()

    def start_copies(s, g, ocean):
        start_y(s, g)
        start_x(s, g, ocean)

    def start_first(ocean):
        for side in (WEST, EAST):
            @pl.when(has[side])
            def _():
                levels_copy(side).start()

        def group(g, carry):
            start_x(0, g, ocean, True)
            return carry

        lax.fori_loop(0, AHEAD, group, 0)

    def wait_arrivals(s, g, ocean):
        for side in range(4):
            @pl.when(has[side])
            def _():
                if side < 2:
                    lands = hx.at[s, side, g, pl.ds(0, 2)] if ocean else hx.at[s, side, g]
                else:
                    lands = yr.at[s, side - 2, g]
                pltpu.make_async_remote_copy(
                    lands, lands, send_sem.at[side], recv_sem.at[s, g, side],
                    device_id=peer[side], device_id_type=MESH,
                ).wait_recv()

    def wait_sends(ocean):
        for side in range(4):
            @pl.when(has[side])
            def _():
                if side < 2:
                    levels_copy(side).wait_send()
                    sent = hx.at[:, side, :, pl.ds(0, 2)] if ocean else hx.at[:, side]
                else:
                    sent = yr.at[:, side - 2]
                pltpu.make_async_remote_copy(
                    sent, sent, send_sem.at[side], recv_sem.at[0, 0, side],
                    device_id=peer[side], device_id_type=MESH,
                ).wait_send()

    tiles = [(c, i) for c in range(4) for i in range(size_x)]

    def put(s, g, values):
        for (c, i), value in zip(tiles, values):
            cur[s, g, c, i] = value
            ys[s, 0, g, pl.ds(c * size_x + i, 1), :] = value[0:1]
            ys[s, 1, g, pl.ds(c * size_x + i, 1), :] = value[last_y:]

    def north_of(value, s, g, c, i):
        arrived = yr[s, 1, g, pl.ds(c * size_x + i, 1), :]
        return jnp.where(rows == last_y, arrived, pltpu.roll(value, size_y - 1, 0))

    def south_of(value, s, g, c, i):
        arrived = yr[s, 0, g, pl.ds(c * size_x + i, 1), :]
        return jnp.where(rows == 0, arrived, pltpu.roll(value, 1, 0))

    def beyond(s, side, g, c):
        return hx[s, side, g, c] * halo_wet[jnp.minimum(s, 1), side, c]

    def ocean_part():
        start_first(True)
        own_masks()

        def first(g, carry):
            load(g).wait()
            put(0, g, [raw[g, c, i] * wet[c, i] for c, i in tiles])
            start_y(0, g)

            @pl.when(g >= AHEAD)
            def _():
                start_x(0, g, True, True)

            return carry

        lax.fori_loop(0, groups, first, 0)
        flux_load.wait()
        prey_load.wait()
        rate_load.wait()
        halo_masks()

        def pair_copy():
            return pltpu.make_async_remote_copy(
                run, flux.at[1], pair_send, pair_recv, device_id=partner, device_id_type=MESH
            )

        def step(s, carry):
            def field(f, inner):
                wait_arrivals(s, f, True)
                @pl.when(jnp.logical_and(s == NSUB, f == 2))
                def _():
                    pltpu.make_async_remote_copy(
                        light, light, pair_send, pair_recv,
                        device_id=partner, device_id_type=MESH,
                    ).wait_recv()
                    heat[...] = light[...] * HEATING

                of_u = jnp.where(f == 0, -DRAG, jnp.where(f == 1, -CORIOLIS, 0.0))
                of_v = jnp.where(f == 0, CORIOLIS, jnp.where(f == 1, -DRAG, 0.0))
                of_heat = jnp.where(f == 2, 1.0, 0.0)
                ageing = jnp.where(f == 4, 1.0, 0.0)
                values = []
                for c, i in tiles:
                    a, b = c // 2, c % 2
                    centre = cur[s, f, c, i]
                    if a == 0:
                        to_east = cur[s, f, 2 + b, i]
                        to_west = cur[s, f, 2 + b, i - 1] if i > 0 else beyond(s, WEST, f, b)
                    else:
                        to_west = cur[s, f, b, i]
                        to_east = cur[s, f, b, i + 1] if i < last_x else beyond(s, EAST, f, b)
                    other = cur[s, f, 2 * a + 1 - b, i]
                    if b == 0:
                        to_north = other
                        to_south = south_of(other, s, f, c + 1, i)
                    else:
                        to_south = other
                        to_north = north_of(other, s, f, c - 1, i)
                    u, v = cur[s, 0, c, i], cur[s, 1, c, i]
                    spread = to_east + to_west + to_north + to_south - 4.0 * centre
                    advect = u * (to_east - to_west) * 0.5 + v * (to_north - to_south) * 0.5
                    forcing = of_u * u + of_v * v + of_heat * heat[i] + ageing
                    values.append(wet[c, i] * (centre + DT * (NU * spread - advect + forcing)))

                put(s + 1, f, values)

                @pl.when(s < NSUB)
                def _():
                    start_copies(s + 1, f, True)

                for (c, i), value in zip(tiles, values):
                    out_ref[0, 4 * f + c, i] = value

                @pl.when(jnp.logical_and(f < 2, s < NSUB))
                def _():
                    for i in range(size_x):
                        total = sum(value for (_, row), value in zip(tiles, values) if row == i)
                        run[f, i] = run[f, i] + total * (0.25 / NSUB)

                @pl.when(jnp.logical_and(s == NSUB - 1, f == 1))
                def _():
                    pair_copy().start()
                return inner
            return lax.fori_loop(0, groups, field, carry)

        lax.fori_loop(0, STEPS, step, 0)
        wait_sends(True)
        pair_copy().wait_send()

    def tracer_part():
        start_first(False)
        own_masks()

        def first(g, carry):
            load(g).wait()
            values = [raw[g, c, i] * wet[c, i] for c, i in tiles]
            put(0, g, values)
            start_y(0, g)

            @pl.when(g >= AHEAD)
            def _():
                start_x(0, g, False, True)

            for (c, i), value in zip(tiles, values):
                tanhs[0, 4 * g + c, i] = jnp.tanh(value)
            return carry

        lax.fori_loop(0, groups, first, 0)
        flux_load.wait()
        prey_load.wait()
        rate_load.wait()
        halo_masks()

        def pair_copy():
            return pltpu.make_async_remote_copy(
                heat, light, pair_send, pair_recv, device_id=partner, device_id_type=MESH
            )

        def step(s, carry):
            now, later = lax.rem(s, 2), lax.rem(s + 1, 2)
            which = s // NSUB

            @pl.when(s == NSUB)
            def _():
                pltpu.make_async_remote_copy(
                    flux.at[1], flux.at[1], pair_send, pair_recv,
                    device_id=partner, device_id_type=MESH,
                ).wait_recv()

            def group(g, inner):
                wait_arrivals(s, g, False)
                values = []
                for c in range(4):
                    t = 4 * g + c
                    living = jnp.where(t < species, 1.0, 0.0)
                    slot = jnp.minimum(t, species - 1)
                    rate = rate_ref[slot] * living
                    mortality = MORTALITY * living
                    prey = prey_ref[slot]
                    for i in range(size_x):
                        centre = cur[s, g, c, i]
                        to_west = cur[s, g, c, i - 1] if i > 0 else beyond(s, WEST, g, c)
                        to_east = cur[s, g, c, i + 1] if i < last_x else beyond(s, EAST, g, c)
                        to_north = north_of(centre, s, g, c, i)
                        to_south = south_of(centre, s, g, c, i)
                        spread = to_east + to_west + to_north + to_south - 4.0 * centre
                        advect = (
                            flux[which, 0, i] * (to_east - to_west) * 0.5
                            + flux[which, 1, i] * (to_north - to_south) * 0.5
                        )
                        reaction = rate * centre * tanhs[now, prey, i] - mortality * centre
                        values.append(
                            wet[c, i] * (centre + DT * (NU * spread - advect + reaction))
                        )
                put(s + 1, g, values)

                @pl.when(s < NSUB)
                def _():
                    start_copies(s + 1, g, False)

                for (c, i), value in zip(tiles, values):
                    out_ref[0, 4 * g + c, i] = value
                    tanhs[later, 4 * g + c, i] = jnp.tanh(value)

                @pl.when(jnp.logical_and(s == NSUB - 1, g == 0))
                def _():
                    above = (
                        lax.broadcasted_iota(jnp.int32, (depth, depth), 0)
                        < lax.broadcasted_iota(jnp.int32, (depth, depth), 1)
                    ).astype(jnp.float32)
                    for i in range(size_x):
                        green = cur[s + 1, 0, 0, i]
                        soft = jnp.maximum(green, 0.0) + jnp.log(1.0 + jnp.exp(-jnp.abs(green)))
                        attenuation = wet[0, i] * (0.03 + 0.05 * soft)
                        overhead = jnp.dot(
                            attenuation, above, precision=lax.Precision.HIGHEST,
                            preferred_element_type=jnp.float32,
                        )
                        heat[i] = SURFACE * jnp.exp(-overhead) * (1.0 - jnp.exp(-attenuation))
                    pl.semaphore_wait(ready_sem, 1)
                    pair_copy().start()
                return inner
            return lax.fori_loop(0, groups, group, carry)

        lax.fori_loop(0, STEPS, step, 0)
        wait_sends(False)
        pair_copy().wait_send()

    greeted = is_ocean.astype(jnp.int32)
    for side in range(4):
        greeted = greeted + has[side].astype(jnp.int32)
    pl.semaphore_wait(barrier, greeted)

    @pl.when(is_ocean)
    def _():
        pl.semaphore_signal(ready_sem, inc=1, device_id=partner, device_id_type=MESH)

    pl.when(is_ocean)(ocean_part)
    pl.when(jnp.logical_not(is_ocean))(tracer_part)


def body(state, levels, old_flux, eco_prey, eco_rate):
    channels, size_x, size_y, depth = state.shape[1:]
    groups = channels // 4
    f32 = jnp.float32
    tile = (size_x, size_y, depth)
    return pl.pallas_call(
        kernel,
        out_shape=pltpu.VMEM(state.shape, f32),
        in_specs=[pl.BlockSpec(memory_space=pltpu.HBM)] * 5,
        out_specs=pl.BlockSpec(memory_space=pltpu.VMEM),
        scratch_shapes=[
            pltpu.VMEM(levels.shape, levels.dtype),
            pltpu.VMEM((2,) + levels.shape, levels.dtype),
            pltpu.VMEM((2, 2, 4, size_y, depth), f32),
            pltpu.SMEM(eco_prey.shape, eco_prey.dtype),
            pltpu.SMEM(eco_rate.shape, eco_rate.dtype),
            pltpu.VMEM((groups, 4) + tile, f32),
            pltpu.VMEM((STEPS + 1, groups, 4) + tile, f32),
            pltpu.VMEM((2, channels) + tile, f32),
            pltpu.VMEM((STEPS, 2, groups, 4, size_y, depth), f32),
            pltpu.VMEM((STEPS + 1, 2, groups, 4 * size_x, depth), f32),
            pltpu.VMEM((STEPS, 2, groups, 4 * size_x, depth), f32),
            pltpu.VMEM((4,) + tile, f32),
            pltpu.VMEM((2, 2) + tile, f32),
            pltpu.VMEM((2,) + tile, f32),
            pltpu.VMEM(tile, f32),
            pltpu.VMEM(tile, f32),
            pltpu.SemaphoreType.DMA((groups,)),
            pltpu.SemaphoreType.DMA((4,)),
            pltpu.SemaphoreType.DMA((4,)),
            pltpu.SemaphoreType.DMA((STEPS, groups, 4)),
            pltpu.SemaphoreType.DMA,
            pltpu.SemaphoreType.DMA,
            pltpu.SemaphoreType.REGULAR,
            pltpu.SemaphoreType.DMA((2,)),
            pltpu.SemaphoreType.DMA((2,)),
        ],
        compiler_params=pltpu.CompilerParams(
            collective_id=0, has_side_effects=True, vmem_limit_bytes=60 * 1024 * 1024
        ),
    )(state, levels, old_flux, eco_prey, eco_rate)


def solution(mesh):
    placed = (
        P("half", None, "gx", "gy", None),
        P(None, "gx", "gy"),
        P(None, "gx", "gy", None),
        P(),
        P(),
    )
    return jax.shard_map(
        body,
        mesh=mesh,
        in_specs=placed,
        out_specs=P("half", None, "gx", "gy", None),
        check_vma=False,
    )
```

```python
import jax
import jax.numpy as jnp
from jax import lax
from jax.experimental import pallas as pl
from jax.experimental.pallas import tpu as pltpu
from jax.sharding import PartitionSpec as P

NSUB = 4
STEPS = NSUB + 1
DT = 0.1
NU = 1.0
CORIOLIS = 0.5
DRAG = 0.1
MORTALITY = 0.1
HEATING = 2.0
SURFACE = 8.0
MESH = pl.DeviceIdType.MESH
WEST, EAST, SOUTH, NORTH = 0, 1, 2, 3


def kernel(
    state_hbm, levels_hbm, flux_hbm, prey_hbm, rate_hbm, out_ref,
    levels_ref, prey_ref, rate_ref, raw, cur, tanhs, hx, ys, yr, wet, flux, run, light, heat,
    load_sem, small_sem, send_sem, recv_sem, pair_send, pair_recv, ready_sem,
):
    groups = cur.shape[1]
    size_x, size_y, depth = cur.shape[3:]
    last_x, last_y = size_x - 1, size_y - 1
    species = prey_ref.shape[0]
    half = lax.axis_index("half")
    gx, gy = lax.axis_index("gx"), lax.axis_index("gy")
    nx, ny = lax.axis_size("gx"), lax.axis_size("gy")
    is_ocean = half == 0
    has = (gx > 0, gx < nx - 1, gy > 0, gy < ny - 1)
    peer = ((half, gx - 1, gy), (half, gx + 1, gy), (half, gx, gy - 1), (half, gx, gy + 1))
    partner = (1 - half, gx, gy)
    even = lax.rem(gy, 2) == 0
    batches = ((0, groups // 2), (groups // 2, groups - groups // 2))

    def load(g):
        return pltpu.make_async_copy(state_hbm.at[0, pl.ds(4 * g, 4)], raw.at[g], load_sem.at[g])

    levels_load = pltpu.make_async_copy(levels_hbm, levels_ref, small_sem.at[0])
    flux_load = pltpu.make_async_copy(flux_hbm, flux.at[0], small_sem.at[1])
    prey_load = pltpu.make_async_copy(prey_hbm, prey_ref, small_sem.at[2])
    rate_load = pltpu.make_async_copy(rate_hbm, rate_ref, small_sem.at[3])
    levels_load.start()
    for g in range(groups):
        load(g).start()
    flux_load.start()
    prey_load.start()
    rate_load.start()

    barrier = pltpu.get_barrier_semaphore()
    for side in range(4):
        @pl.when(has[side])
        def _():
            pl.semaphore_signal(barrier, inc=1, device_id=peer[side], device_id_type=MESH)

    @pl.when(jnp.logical_not(is_ocean))
    def _():
        pl.semaphore_signal(barrier, inc=1, device_id=partner, device_id_type=MESH)

    for side in (WEST, EAST):
        @pl.when(jnp.logical_not(has[side]))
        def _():
            for s in range(STEPS):
                hx[s, side] = jnp.zeros(hx.shape[2:], jnp.float32)
    for side in (SOUTH, NORTH):
        @pl.when(jnp.logical_not(has[side]))
        def _():
            for s in range(STEPS):
                yr[s, side - 2] = jnp.zeros(yr.shape[2:], jnp.float32)

    rows = lax.broadcasted_iota(jnp.int32, (size_y, depth), 0)
    level_k = lax.broadcasted_iota(jnp.int32, (size_y, depth), 1).astype(jnp.float32)
    diagonal = lax.broadcasted_iota(jnp.int32, (size_y, size_y), 0) == lax.broadcasted_iota(
        jnp.int32, (size_y, size_y), 1
    )
    levels_load.wait()
    for i in range(size_x):
        active = []
        for c in range(4):
            line = levels_ref[c, pl.ds(i, 1), :].astype(jnp.float32)
            spread = jnp.where(diagonal, jnp.broadcast_to(line, (size_y, size_y)), 0.0)
            active.append(jnp.sum(spread, axis=1, keepdims=True))
        most = jnp.maximum(jnp.maximum(active[0], active[1]), jnp.maximum(active[2], active[3]))
        for c in range(4):
            mine = jnp.where(is_ocean, active[c], most)
            wet[c, i] = jnp.where(level_k < mine, 1.0, 0.0)

    run[...] = jnp.zeros(run.shape, jnp.float32)
    heat[...] = jnp.zeros(heat.shape, jnp.float32)

    def copy_of(s, g, side, ocean):
        row = 0 if side == WEST else last_x
        if ocean:
            channels = pl.ds(0, 2) if side == WEST else pl.ds(2, 2)
            src = cur.at[s, g, channels, row]
            dst = hx.at[s, 1 - side, g, pl.ds(0, 2)]
        else:
            src = cur.at[s, g, :, row]
            dst = hx.at[s, 1 - side, g]
        return pltpu.make_async_remote_copy(
            src, dst, send_sem.at[side], recv_sem.at[s, g, 1 - side],
            device_id=peer[side], device_id_type=MESH,
        )

    def y_copy(s, n, side):
        span = pl.ds(*batches[n])
        return pltpu.make_async_remote_copy(
            ys.at[s, side - 2, span], yr.at[s, 3 - side, span],
            send_sem.at[side], recv_sem.at[s, n, 5 - side],
            device_id=peer[side], device_id_type=MESH,
        )

    def start_copies(s, g, ocean):
        for n, (low, count) in enumerate(batches):
            for side in (SOUTH, NORTH):
                @pl.when(jnp.logical_and(g == low + count - 1, has[side]))
                def _():
                    y_copy(s, n, side).start()
        for side, turn in ((WEST, even), (EAST, None), (WEST, jnp.logical_not(even))):
            @pl.when(has[side] if turn is None else jnp.logical_and(has[side], turn))
            def _():
                copy_of(s, g, side, ocean).start()

    def arrival(condition, lands, side, sem):
        @pl.when(condition)
        def _():
            pltpu.make_async_remote_copy(
                lands, lands, send_sem.at[side], sem,
                device_id=peer[side], device_id_type=MESH,
            ).wait_recv()

    def wait_arrivals(s, g, ocean):
        for n, (low, count) in enumerate(batches):
            for side in (SOUTH, NORTH):
                arrival(
                    jnp.logical_and(g == low, has[side]),
                    yr.at[s, side - 2, pl.ds(low, count)], side, recv_sem.at[s, n, side],
                )
        for side in (WEST, EAST):
            lands = hx.at[s, side, g, pl.ds(0, 2)] if ocean else hx.at[s, side, g]
            arrival(has[side], lands, side, recv_sem.at[s, g, side])

    def wait_sends(ocean):
        for side in range(4):
            @pl.when(has[side])
            def _():
                if side < 2:
                    sent = hx.at[:, side, :, pl.ds(0, 2)] if ocean else hx.at[:, side]
                else:
                    sent = yr.at[:, side - 2]
                pltpu.make_async_remote_copy(
                    sent, sent, send_sem.at[side], recv_sem.at[0, 0, side],
                    device_id=peer[side], device_id_type=MESH,
                ).wait_send()

    tiles = [(c, i) for c in range(4) for i in range(size_x)]

    def put(s, g, values):
        for (c, i), value in zip(tiles, values):
            cur[s, g, c, i] = value
            ys[s, 0, g, pl.ds(c * size_x + i, 1), :] = value[0:1]
            ys[s, 1, g, pl.ds(c * size_x + i, 1), :] = value[last_y:]

    def north_of(value, s, g, c, i):
        arrived = yr[s, 1, g, pl.ds(c * size_x + i, 1), :]
        return jnp.where(rows == last_y, arrived, pltpu.roll(value, size_y - 1, 0))

    def south_of(value, s, g, c, i):
        arrived = yr[s, 0, g, pl.ds(c * size_x + i, 1), :]
        return jnp.where(rows == 0, arrived, pltpu.roll(value, 1, 0))

    def ocean_part():
        def first(g, carry):
            load(g).wait()
            put(0, g, [raw[g, c, i] * wet[c, i] for c, i in tiles])
            start_copies(0, g, True)
            return carry

        lax.fori_loop(0, groups, first, 0)
        flux_load.wait()
        prey_load.wait()
        rate_load.wait()

        def pair_copy():
            return pltpu.make_async_remote_copy(
                run, flux.at[1], pair_send, pair_recv, device_id=partner, device_id_type=MESH
            )

        def step(s, carry):
            def field(f, inner):
                wait_arrivals(s, f, True)
                @pl.when(jnp.logical_and(s == NSUB, f == 2))
                def _():
                    pltpu.make_async_remote_copy(
                        light, light, pair_send, pair_recv,
                        device_id=partner, device_id_type=MESH,
                    ).wait_recv()
                    heat[...] = light[...] * HEATING

                of_u = jnp.where(f == 0, -DRAG, jnp.where(f == 1, -CORIOLIS, 0.0))
                of_v = jnp.where(f == 0, CORIOLIS, jnp.where(f == 1, -DRAG, 0.0))
                of_heat = jnp.where(f == 2, 1.0, 0.0)
                ageing = jnp.where(f == 4, 1.0, 0.0)
                values = []
                for c, i in tiles:
                    a, b = c // 2, c % 2
                    centre = cur[s, f, c, i]
                    if a == 0:
                        to_east = cur[s, f, 2 + b, i]
                        to_west = cur[s, f, 2 + b, i - 1] if i > 0 else hx[s, WEST, f, b]
                    else:
                        to_west = cur[s, f, b, i]
                        to_east = cur[s, f, b, i + 1] if i < last_x else hx[s, EAST, f, b]
                    other = cur[s, f, 2 * a + 1 - b, i]
                    if b == 0:
                        to_north = other
                        to_south = south_of(other, s, f, c + 1, i)
                    else:
                        to_south = other
                        to_north = north_of(other, s, f, c - 1, i)
                    u, v = cur[s, 0, c, i], cur[s, 1, c, i]
                    spread = to_east + to_west + to_north + to_south - 4.0 * centre
                    advect = u * (to_east - to_west) * 0.5 + v * (to_north - to_south) * 0.5
                    forcing = of_u * u + of_v * v + of_heat * heat[i] + ageing
                    values.append(wet[c, i] * (centre + DT * (NU * spread - advect + forcing)))

                put(s + 1, f, values)

                @pl.when(s < NSUB)
                def _():
                    start_copies(s + 1, f, True)

                for (c, i), value in zip(tiles, values):
                    out_ref[0, 4 * f + c, i] = value

                @pl.when(jnp.logical_and(f < 2, s < NSUB))
                def _():
                    for i in range(size_x):
                        total = sum(value for (_, row), value in zip(tiles, values) if row == i)
                        run[f, i] = run[f, i] + total * (0.25 / NSUB)

                @pl.when(jnp.logical_and(s == NSUB - 1, f == 1))
                def _():
                    pair_copy().start()
                return inner
            return lax.fori_loop(0, groups, field, carry)

        lax.fori_loop(0, STEPS, step, 0)
        wait_sends(True)
        pair_copy().wait_send()

    def tracer_part():
        def first(g, carry):
            load(g).wait()
            values = [raw[g, c, i] * wet[c, i] for c, i in tiles]
            put(0, g, values)
            start_copies(0, g, False)
            for (c, i), value in zip(tiles, values):
                tanhs[0, 4 * g + c, i] = jnp.tanh(value)
            return carry

        lax.fori_loop(0, groups, first, 0)
        flux_load.wait()
        prey_load.wait()
        rate_load.wait()

        def pair_copy():
            return pltpu.make_async_remote_copy(
                heat, light, pair_send, pair_recv, device_id=partner, device_id_type=MESH
            )

        def step(s, carry):
            now, later = lax.rem(s, 2), lax.rem(s + 1, 2)
            which = s // NSUB

            @pl.when(s == NSUB)
            def _():
                pltpu.make_async_remote_copy(
                    flux.at[1], flux.at[1], pair_send, pair_recv,
                    device_id=partner, device_id_type=MESH,
                ).wait_recv()

            def group(g, inner):
                wait_arrivals(s, g, False)
                values = []
                for c in range(4):
                    t = 4 * g + c
                    living = jnp.where(t < species, 1.0, 0.0)
                    slot = jnp.minimum(t, species - 1)
                    rate = rate_ref[slot] * living
                    mortality = MORTALITY * living
                    prey = prey_ref[slot]
                    for i in range(size_x):
                        centre = cur[s, g, c, i]
                        to_west = cur[s, g, c, i - 1] if i > 0 else hx[s, WEST, g, c]
                        to_east = cur[s, g, c, i + 1] if i < last_x else hx[s, EAST, g, c]
                        to_north = north_of(centre, s, g, c, i)
                        to_south = south_of(centre, s, g, c, i)
                        spread = to_east + to_west + to_north + to_south - 4.0 * centre
                        advect = (
                            flux[which, 0, i] * (to_east - to_west) * 0.5
                            + flux[which, 1, i] * (to_north - to_south) * 0.5
                        )
                        reaction = rate * centre * tanhs[now, prey, i] - mortality * centre
                        values.append(
                            wet[c, i] * (centre + DT * (NU * spread - advect + reaction))
                        )
                put(s + 1, g, values)

                @pl.when(s < NSUB)
                def _():
                    start_copies(s + 1, g, False)

                for (c, i), value in zip(tiles, values):
                    out_ref[0, 4 * g + c, i] = value
                    tanhs[later, 4 * g + c, i] = jnp.tanh(value)

                @pl.when(jnp.logical_and(s == NSUB - 1, g == 0))
                def _():
                    above = (
                        lax.broadcasted_iota(jnp.int32, (depth, depth), 0)
                        < lax.broadcasted_iota(jnp.int32, (depth, depth), 1)
                    ).astype(jnp.float32)
                    for i in range(size_x):
                        green = cur[s + 1, 0, 0, i]
                        soft = jnp.maximum(green, 0.0) + jnp.log(1.0 + jnp.exp(-jnp.abs(green)))
                        attenuation = wet[0, i] * (0.03 + 0.05 * soft)
                        overhead = jnp.dot(
                            attenuation, above, precision=lax.Precision.HIGHEST,
                            preferred_element_type=jnp.float32,
                        )
                        heat[i] = SURFACE * jnp.exp(-overhead) * (1.0 - jnp.exp(-attenuation))
                    pl.semaphore_wait(ready_sem, 1)
                    pair_copy().start()
                return inner
            return lax.fori_loop(0, groups, group, carry)

        lax.fori_loop(0, STEPS, step, 0)
        wait_sends(False)
        pair_copy().wait_send()

    greeted = is_ocean.astype(jnp.int32)
    for side in range(4):
        greeted = greeted + has[side].astype(jnp.int32)
    pl.semaphore_wait(barrier, greeted)

    @pl.when(is_ocean)
    def _():
        pl.semaphore_signal(ready_sem, inc=1, device_id=partner, device_id_type=MESH)

    pl.when(is_ocean)(ocean_part)
    pl.when(jnp.logical_not(is_ocean))(tracer_part)


def body(state, levels, old_flux, eco_prey, eco_rate):
    channels, size_x, size_y, depth = state.shape[1:]
    groups = channels // 4
    f32 = jnp.float32
    tile = (size_x, size_y, depth)
    return pl.pallas_call(
        kernel,
        out_shape=pltpu.VMEM(state.shape, f32),
        in_specs=[pl.BlockSpec(memory_space=pltpu.HBM)] * 5,
        out_specs=pl.BlockSpec(memory_space=pltpu.VMEM),
        scratch_shapes=[
            pltpu.VMEM(levels.shape, levels.dtype),
            pltpu.SMEM(eco_prey.shape, eco_prey.dtype),
            pltpu.SMEM(eco_rate.shape, eco_rate.dtype),
            pltpu.VMEM((groups, 4) + tile, f32),
            pltpu.VMEM((STEPS + 1, groups, 4) + tile, f32),
            pltpu.VMEM((2, channels) + tile, f32),
            pltpu.VMEM((STEPS, 2, groups, 4, size_y, depth), f32),
            pltpu.VMEM((STEPS + 1, 2, groups, 4 * size_x, depth), f32),
            pltpu.VMEM((STEPS, 2, groups, 4 * size_x, depth), f32),
            pltpu.VMEM((4,) + tile, f32),
            pltpu.VMEM((2, 2) + tile, f32),
            pltpu.VMEM((2,) + tile, f32),
            pltpu.VMEM(tile, f32),
            pltpu.VMEM(tile, f32),
            pltpu.SemaphoreType.DMA((groups,)),
            pltpu.SemaphoreType.DMA((4,)),
            pltpu.SemaphoreType.DMA((4,)),
            pltpu.SemaphoreType.DMA((STEPS, groups, 4)),
            pltpu.SemaphoreType.DMA,
            pltpu.SemaphoreType.DMA,
            pltpu.SemaphoreType.REGULAR,
        ],
        compiler_params=pltpu.CompilerParams(
            collective_id=0, has_side_effects=True, vmem_limit_bytes=60 * 1024 * 1024
        ),
    )(state, levels, old_flux, eco_prey, eco_rate)


def solution(mesh):
    placed = (
        P("half", None, "gx", "gy", None),
        P(None, "gx", "gy"),
        P(None, "gx", "gy", None),
        P(),
        P(),
    )
    return jax.shard_map(
        body,
        mesh=mesh,
        in_specs=placed,
        out_specs=P("half", None, "gx", "gy", None),
        check_vma=False,
    )
```

```python
import jax
import jax.numpy as jnp
from jax import lax
from jax.experimental import pallas as pl
from jax.experimental.pallas import tpu as pltpu
from jax.sharding import PartitionSpec as P

NSUB = 4
STEPS = NSUB + 1
DT = 0.1
NU = 1.0
CORIOLIS = 0.5
DRAG = 0.1
MORTALITY = 0.1
HEATING = 2.0
SURFACE = 8.0
MESH = pl.DeviceIdType.MESH
WEST, EAST, SOUTH, NORTH = 0, 1, 2, 3


def kernel(
    state_hbm, levels_hbm, flux_hbm, prey_hbm, rate_hbm, out_ref,
    levels_ref, prey_ref, rate_ref, raw, cur, tanhs, hx, ys, yr, wet, flux, run, light, heat,
    load_sem, small_sem, send_sem, recv_sem, pair_send, pair_recv, ready_sem,
):
    groups = cur.shape[1]
    size_x, size_y, depth = cur.shape[3:]
    last_x, last_y = size_x - 1, size_y - 1
    species = prey_ref.shape[0]
    half = lax.axis_index("half")
    gx, gy = lax.axis_index("gx"), lax.axis_index("gy")
    nx, ny = lax.axis_size("gx"), lax.axis_size("gy")
    is_ocean = half == 0
    has = (gx > 0, gx < nx - 1, gy > 0, gy < ny - 1)
    peer = ((half, gx - 1, gy), (half, gx + 1, gy), (half, gx, gy - 1), (half, gx, gy + 1))
    partner = (1 - half, gx, gy)
    even = lax.rem(gy, 2) == 0

    def load(g):
        return pltpu.make_async_copy(state_hbm.at[0, pl.ds(4 * g, 4)], raw.at[g], load_sem.at[g])

    levels_load = pltpu.make_async_copy(levels_hbm, levels_ref, small_sem.at[0])
    flux_load = pltpu.make_async_copy(flux_hbm, flux.at[0], small_sem.at[1])
    prey_load = pltpu.make_async_copy(prey_hbm, prey_ref, small_sem.at[2])
    rate_load = pltpu.make_async_copy(rate_hbm, rate_ref, small_sem.at[3])
    levels_load.start()
    for g in range(groups):
        load(g).start()
    flux_load.start()
    prey_load.start()
    rate_load.start()

    barrier = pltpu.get_barrier_semaphore()
    for side in range(4):
        @pl.when(has[side])
        def _():
            pl.semaphore_signal(barrier, inc=1, device_id=peer[side], device_id_type=MESH)

    @pl.when(jnp.logical_not(is_ocean))
    def _():
        pl.semaphore_signal(barrier, inc=1, device_id=partner, device_id_type=MESH)

    for side in (WEST, EAST):
        @pl.when(jnp.logical_not(has[side]))
        def _():
            for s in range(STEPS):
                hx[s, side] = jnp.zeros(hx.shape[2:], jnp.float32)
    for side in (SOUTH, NORTH):
        @pl.when(jnp.logical_not(has[side]))
        def _():
            for s in range(STEPS):
                yr[s, side - 2] = jnp.zeros(yr.shape[2:], jnp.float32)

    rows = lax.broadcasted_iota(jnp.int32, (size_y, depth), 0)
    level_k = lax.broadcasted_iota(jnp.int32, (size_y, depth), 1).astype(jnp.float32)
    diagonal = lax.broadcasted_iota(jnp.int32, (size_y, size_y), 0) == lax.broadcasted_iota(
        jnp.int32, (size_y, size_y), 1
    )
    levels_load.wait()
    for i in range(size_x):
        active = []
        for c in range(4):
            line = levels_ref[c, pl.ds(i, 1), :].astype(jnp.float32)
            spread = jnp.where(diagonal, jnp.broadcast_to(line, (size_y, size_y)), 0.0)
            active.append(jnp.sum(spread, axis=1, keepdims=True))
        most = jnp.maximum(jnp.maximum(active[0], active[1]), jnp.maximum(active[2], active[3]))
        for c in range(4):
            mine = jnp.where(is_ocean, active[c], most)
            wet[c, i] = jnp.where(level_k < mine, 1.0, 0.0)

    run[...] = jnp.zeros(run.shape, jnp.float32)
    heat[...] = jnp.zeros(heat.shape, jnp.float32)

    def copy_of(s, g, side, ocean):
        if side < 2:
            row = 0 if side == WEST else last_x
            if ocean:
                channels = pl.ds(0, 2) if side == WEST else pl.ds(2, 2)
                src = cur.at[s, g, channels, row]
                dst = hx.at[s, 1 - side, g, pl.ds(0, 2)]
            else:
                src = cur.at[s, g, :, row]
                dst = hx.at[s, 1 - side, g]
        else:
            src = ys.at[s, side - 2, g]
            dst = yr.at[s, 3 - side, g]
        lands = 1 - side if side < 2 else 5 - side
        return pltpu.make_async_remote_copy(
            src, dst, send_sem.at[side], recv_sem.at[s, g, lands],
            device_id=peer[side], device_id_type=MESH,
        )

    def start_copies(s, g, ocean):
        for side, turn in (
            (SOUTH, None), (NORTH, None), (WEST, even), (EAST, None), (WEST, jnp.logical_not(even)),
        ):
            @pl.when(has[side] if turn is None else jnp.logical_and(has[side], turn))
            def _():
                copy_of(s, g, side, ocean).start()

    def wait_arrivals(s, g, ocean):
        for side in range(4):
            @pl.when(has[side])
            def _():
                if side < 2:
                    lands = hx.at[s, side, g, pl.ds(0, 2)] if ocean else hx.at[s, side, g]
                else:
                    lands = yr.at[s, side - 2, g]
                pltpu.make_async_remote_copy(
                    lands, lands, send_sem.at[side], recv_sem.at[s, g, side],
                    device_id=peer[side], device_id_type=MESH,
                ).wait_recv()

    def wait_sends(ocean):
        for side in range(4):
            @pl.when(has[side])
            def _():
                if side < 2:
                    sent = hx.at[:, side, :, pl.ds(0, 2)] if ocean else hx.at[:, side]
                else:
                    sent = yr.at[:, side - 2]
                pltpu.make_async_remote_copy(
                    sent, sent, send_sem.at[side], recv_sem.at[0, 0, side],
                    device_id=peer[side], device_id_type=MESH,
                ).wait_send()

    tiles = [(c, i) for c in range(4) for i in range(size_x)]

    def put(s, g, values):
        for (c, i), value in zip(tiles, values):
            cur[s, g, c, i] = value
            ys[s, 0, g, pl.ds(c * size_x + i, 1), :] = value[0:1]
            ys[s, 1, g, pl.ds(c * size_x + i, 1), :] = value[last_y:]

    def north_of(value, s, g, c, i):
        arrived = yr[s, 1, g, pl.ds(c * size_x + i, 1), :]
        return jnp.where(rows == last_y, arrived, pltpu.roll(value, size_y - 1, 0))

    def south_of(value, s, g, c, i):
        arrived = yr[s, 0, g, pl.ds(c * size_x + i, 1), :]
        return jnp.where(rows == 0, arrived, pltpu.roll(value, 1, 0))

    def ocean_part():
        def first(g, carry):
            load(g).wait()
            put(0, g, [raw[g, c, i] * wet[c, i] for c, i in tiles])
            start_copies(0, g, True)
            return carry

        lax.fori_loop(0, groups, first, 0)
        flux_load.wait()
        prey_load.wait()
        rate_load.wait()

        def pair_copy():
            return pltpu.make_async_remote_copy(
                run, flux.at[1], pair_send, pair_recv, device_id=partner, device_id_type=MESH
            )

        def step(s, carry):
            def field(f, inner):
                wait_arrivals(s, f, True)
                @pl.when(jnp.logical_and(s == NSUB, f == 2))
                def _():
                    pltpu.make_async_remote_copy(
                        light, light, pair_send, pair_recv,
                        device_id=partner, device_id_type=MESH,
                    ).wait_recv()
                    heat[...] = light[...] * HEATING

                of_u = jnp.where(f == 0, -DRAG, jnp.where(f == 1, -CORIOLIS, 0.0))
                of_v = jnp.where(f == 0, CORIOLIS, jnp.where(f == 1, -DRAG, 0.0))
                of_heat = jnp.where(f == 2, 1.0, 0.0)
                ageing = jnp.where(f == 4, 1.0, 0.0)
                values = []
                for c, i in tiles:
                    a, b = c // 2, c % 2
                    centre = cur[s, f, c, i]
                    if a == 0:
                        to_east = cur[s, f, 2 + b, i]
                        to_west = cur[s, f, 2 + b, i - 1] if i > 0 else hx[s, WEST, f, b]
                    else:
                        to_west = cur[s, f, b, i]
                        to_east = cur[s, f, b, i + 1] if i < last_x else hx[s, EAST, f, b]
                    other = cur[s, f, 2 * a + 1 - b, i]
                    if b == 0:
                        to_north = other
                        to_south = south_of(other, s, f, c + 1, i)
                    else:
                        to_south = other
                        to_north = north_of(other, s, f, c - 1, i)
                    u, v = cur[s, 0, c, i], cur[s, 1, c, i]
                    spread = to_east + to_west + to_north + to_south - 4.0 * centre
                    advect = u * (to_east - to_west) * 0.5 + v * (to_north - to_south) * 0.5
                    forcing = of_u * u + of_v * v + of_heat * heat[i] + ageing
                    values.append(wet[c, i] * (centre + DT * (NU * spread - advect + forcing)))

                put(s + 1, f, values)

                @pl.when(s < NSUB)
                def _():
                    start_copies(s + 1, f, True)

                for (c, i), value in zip(tiles, values):
                    out_ref[0, 4 * f + c, i] = value

                @pl.when(jnp.logical_and(f < 2, s < NSUB))
                def _():
                    for i in range(size_x):
                        total = sum(value for (_, row), value in zip(tiles, values) if row == i)
                        run[f, i] = run[f, i] + total * (0.25 / NSUB)

                @pl.when(jnp.logical_and(s == NSUB - 1, f == 1))
                def _():
                    pair_copy().start()
                return inner
            return lax.fori_loop(0, groups, field, carry)

        lax.fori_loop(0, STEPS, step, 0)
        wait_sends(True)
        pair_copy().wait_send()

    def tracer_part():
        def first(g, carry):
            load(g).wait()
            values = [raw[g, c, i] * wet[c, i] for c, i in tiles]
            put(0, g, values)
            start_copies(0, g, False)
            for (c, i), value in zip(tiles, values):
                tanhs[0, 4 * g + c, i] = jnp.tanh(value)
            return carry

        lax.fori_loop(0, groups, first, 0)
        flux_load.wait()
        prey_load.wait()
        rate_load.wait()

        def pair_copy():
            return pltpu.make_async_remote_copy(
                heat, light, pair_send, pair_recv, device_id=partner, device_id_type=MESH
            )

        def step(s, carry):
            now, later = lax.rem(s, 2), lax.rem(s + 1, 2)
            which = s // NSUB

            @pl.when(s == NSUB)
            def _():
                pltpu.make_async_remote_copy(
                    flux.at[1], flux.at[1], pair_send, pair_recv,
                    device_id=partner, device_id_type=MESH,
                ).wait_recv()

            def group(g, inner):
                wait_arrivals(s, g, False)
                values = []
                for c in range(4):
                    t = 4 * g + c
                    living = jnp.where(t < species, 1.0, 0.0)
                    slot = jnp.minimum(t, species - 1)
                    rate = rate_ref[slot] * living
                    mortality = MORTALITY * living
                    prey = prey_ref[slot]
                    for i in range(size_x):
                        centre = cur[s, g, c, i]
                        to_west = cur[s, g, c, i - 1] if i > 0 else hx[s, WEST, g, c]
                        to_east = cur[s, g, c, i + 1] if i < last_x else hx[s, EAST, g, c]
                        to_north = north_of(centre, s, g, c, i)
                        to_south = south_of(centre, s, g, c, i)
                        spread = to_east + to_west + to_north + to_south - 4.0 * centre
                        advect = (
                            flux[which, 0, i] * (to_east - to_west) * 0.5
                            + flux[which, 1, i] * (to_north - to_south) * 0.5
                        )
                        reaction = rate * centre * tanhs[now, prey, i] - mortality * centre
                        values.append(
                            wet[c, i] * (centre + DT * (NU * spread - advect + reaction))
                        )
                put(s + 1, g, values)

                @pl.when(s < NSUB)
                def _():
                    start_copies(s + 1, g, False)

                for (c, i), value in zip(tiles, values):
                    out_ref[0, 4 * g + c, i] = value
                    tanhs[later, 4 * g + c, i] = jnp.tanh(value)

                @pl.when(jnp.logical_and(s == NSUB - 1, g == groups // 2))
                def _():
                    above = (
                        lax.broadcasted_iota(jnp.int32, (depth, depth), 0)
                        < lax.broadcasted_iota(jnp.int32, (depth, depth), 1)
                    ).astype(jnp.float32)
                    for i in range(size_x):
                        green = cur[s + 1, 0, 0, i]
                        soft = jnp.maximum(green, 0.0) + jnp.log(1.0 + jnp.exp(-jnp.abs(green)))
                        attenuation = wet[0, i] * (0.03 + 0.05 * soft)
                        overhead = jnp.dot(
                            attenuation, above, precision=lax.Precision.HIGHEST,
                            preferred_element_type=jnp.float32,
                        )
                        heat[i] = SURFACE * jnp.exp(-overhead) * (1.0 - jnp.exp(-attenuation))
                    pl.semaphore_wait(ready_sem, 1)
                    pair_copy().start()
                return inner
            return lax.fori_loop(0, groups, group, carry)

        lax.fori_loop(0, STEPS, step, 0)
        wait_sends(False)
        pair_copy().wait_send()

    greeted = is_ocean.astype(jnp.int32)
    for side in range(4):
        greeted = greeted + has[side].astype(jnp.int32)
    pl.semaphore_wait(barrier, greeted)

    @pl.when(is_ocean)
    def _():
        pl.semaphore_signal(ready_sem, inc=1, device_id=partner, device_id_type=MESH)

    pl.when(is_ocean)(ocean_part)
    pl.when(jnp.logical_not(is_ocean))(tracer_part)


def body(state, levels, old_flux, eco_prey, eco_rate):
    channels, size_x, size_y, depth = state.shape[1:]
    groups = channels // 4
    f32 = jnp.float32
    tile = (size_x, size_y, depth)
    return pl.pallas_call(
        kernel,
        out_shape=pltpu.VMEM(state.shape, f32),
        in_specs=[pl.BlockSpec(memory_space=pltpu.HBM)] * 5,
        out_specs=pl.BlockSpec(memory_space=pltpu.VMEM),
        scratch_shapes=[
            pltpu.VMEM(levels.shape, levels.dtype),
            pltpu.SMEM(eco_prey.shape, eco_prey.dtype),
            pltpu.SMEM(eco_rate.shape, eco_rate.dtype),
            pltpu.VMEM((groups, 4) + tile, f32),
            pltpu.VMEM((STEPS + 1, groups, 4) + tile, f32),
            pltpu.VMEM((2, channels) + tile, f32),
            pltpu.VMEM((STEPS, 2, groups, 4, size_y, depth), f32),
            pltpu.VMEM((STEPS + 1, 2, groups, 4 * size_x, depth), f32),
            pltpu.VMEM((STEPS, 2, groups, 4 * size_x, depth), f32),
            pltpu.VMEM((4,) + tile, f32),
            pltpu.VMEM((2, 2) + tile, f32),
            pltpu.VMEM((2,) + tile, f32),
            pltpu.VMEM(tile, f32),
            pltpu.VMEM(tile, f32),
            pltpu.SemaphoreType.DMA((groups,)),
            pltpu.SemaphoreType.DMA((4,)),
            pltpu.SemaphoreType.DMA((4,)),
            pltpu.SemaphoreType.DMA((STEPS, groups, 4)),
            pltpu.SemaphoreType.DMA,
            pltpu.SemaphoreType.DMA,
            pltpu.SemaphoreType.REGULAR,
        ],
        compiler_params=pltpu.CompilerParams(
            collective_id=0, has_side_effects=True, vmem_limit_bytes=60 * 1024 * 1024
        ),
    )(state, levels, old_flux, eco_prey, eco_rate)


def solution(mesh):
    placed = (
        P("half", None, "gx", "gy", None),
        P(None, "gx", "gy"),
        P(None, "gx", "gy", None),
        P(),
        P(),
    )
    return jax.shard_map(
        body,
        mesh=mesh,
        in_specs=placed,
        out_specs=P("half", None, "gx", "gy", None),
        check_vma=False,
    )
```
